128 devices in a mesh: dp: 8 (over y_hi, x), width: 4 (over y_lo, core), heads: 4 (over z).
Axes of the slice: x: 4, y: 4 (y_hi: 2, y_lo: 2; y = y_hi * 2 + y_lo), z: 4, core: 2. Of those that a mesh axis runs over, the one named last changes fastest.
Arguments:
- tokens: bfloat16 [16384, 1280], P(('dp', 'heads'), 'width'), may hold values from -22 to 22
- ln_gain: float32 [2, 1280], P(None, 'width'), may hold values from 0.5 to 1.5
- ln_bias: float32 [2, 1280], P(None, 'width'), may hold values from -4 to 4
- w_attn: bfloat16 [3, 1280, 1280], P(None, 'width', 'heads'), may hold values from -0.15625 to 0.15625
- b_qv: float32 [2, 1280], P(None, 'heads'), may hold values from -4 to 4
- w_proj: bfloat16 [1280, 1280], P('heads', 'width'), may hold values from -1.25 to 1.25
- b_proj: float32 [1280], P('width'), may hold values from -4 to 4
- w_fc: bfloat16 [1280, 5120], P('width', 'heads'), may hold values from -1 to 1
- b_fc: float32 [5120], P('heads'), may hold values from -4 to 4
- w_out: bfloat16 [5120, 1280], P('heads', 'width'), may hold values from -0.078125 to 0.078125
- b_out: float32 [1280], P('width'), may hold values from -4 to 4
- d_out: bfloat16 [16384, 1280], P(('dp', 'heads'), 'width'), may hold values from -22 to 22
Outputs:
- block_out: bfloat16 [16384, 1280], P(('dp', 'heads'), 'width')
- d_tokens: bfloat16 [16384, 1280], P(('dp', 'heads'), 'width')
- d_ln_gain: float32 [2, 1280], P(None, 'width')
- d_ln_bias: float32 [2, 1280], P(None, 'width')
- d_w_attn: float32 [3, 1280, 1280], P(None, 'width', 'heads')
- d_b_qv: float32 [2, 1280], P(None, 'heads')
- d_w_proj: float32 [1280, 1280], P('heads', 'width')
- d_b_proj: float32 [1280], P('width')
- d_w_fc: float32 [1280, 5120], P('width', 'heads')
- d_b_fc: float32 [5120], P('heads')
- d_w_out: float32 [5120, 1280], P('heads', 'width')
- d_b_out: float32 [1280], P('width')
The draws below stay inside these ranges and needn't reach their ends.
All inputs are finite; a program needn't handle non-finite values.
Results may differ from the reference program's by a relative error of at most 0.023.
Values may be sent and summed in bfloat16 or wider, within the bound.
A program may use at most 192 MiB of HBM per device.

```python
import jax
import jax.numpy as jnp
from jax import lax

D = 1280
NH = 20
HS = 64
FF = 5120
LEN = 2048
TOKENS = 16384


def column_ramp(values, steepness):
    places = jnp.arange(D, dtype=jnp.float32) / (D - 1)
    return values * steepness ** places


def ramped_field(key):
    base = jax.random.normal(key, (TOKENS, D), jnp.float32)
    return column_ramp(jnp.clip(base, -5.0, 5.0) * 0.6, 3.0)


def draw_tokens(key, part):
    key = jax.random.fold_in(key, 11)
    return ramped_field(key).astype(jnp.bfloat16)


def draw_d_out(key, part):
    key = jax.random.fold_in(key, 12)
    return ramped_field(key).astype(jnp.bfloat16)


def draw_w_fc(key, part):
    key = jax.random.fold_in(key, 13)
    noise_key, common_key = jax.random.split(key)
    noise = jnp.clip(jax.random.normal(noise_key, (D, FF), jnp.float32), -5.0, 5.0)
    common = 0.5 * jnp.clip(jax.random.normal(common_key, (1, FF), jnp.float32), -5.0, 5.0)
    return ((noise + common) * D ** (-0.5)).astype(jnp.bfloat16)


def shard_levels(rng, shape, cuts, low, top_value):
    loudness, own = 1.0, jax.random.fold_in(rng, 6)
    for dim, parts in cuts:
        heights = jnp.exp(jax.random.uniform(jax.random.fold_in(own, dim), (parts,), jnp.float32, low / len(cuts), top_value / len(cuts)))
        loudness = loudness * jnp.repeat(heights, shape[dim] // parts).reshape([-1 if axis == dim else 1 for axis in range(len(shape))])
    return loudness


def normal_values(stream_key, dims, scale, most, cuts=(), kind=jnp.bfloat16):
    values = scale * jax.random.normal(stream_key, dims, jnp.float32)
    if cuts:
        values = values * shard_levels(stream_key, dims, cuts, -0.22, 0.18)
    return jnp.clip(values, -most, most).astype(kind)


def setup_inputs(seed: int = 0) -> dict:
    keys = jax.random.split(jax.random.key(seed), 13)
    tokens = draw_tokens(jax.random.fold_in(keys[12], 71), 0)
    ln_gain = jnp.clip(1.0 + 0.1 * jax.random.normal(keys[1], (2, D), jnp.float32), 0.5, 1.5)
    ln_bias = normal_values(keys[2], (2, D), 0.3, 4.0, ((1, 4),), jnp.float32)
    w_attn = normal_values(keys[3], (3, D, D), D ** -0.5, 0.15625, ((1, 4), (2, 4)))
    b_qv = normal_values(keys[4], (2, D), 0.5, 4.0, ((1, 4),), jnp.float32)
    w_proj = normal_values(keys[5], (D, D), (max(D // 64, 4)) ** -0.5, 1.25, ((0, 4), (1, 4)))
    b_proj = normal_values(keys[6], (D,), 0.5, 4.0, ((0, 4),), jnp.float32)
    w_fc = draw_w_fc(jax.random.fold_in(keys[12], 71), 0)
    b_fc = normal_values(keys[8], (FF,), 0.5, 4.0, ((0, 4),), jnp.float32)
    w_out = normal_values(keys[9], (FF, D), FF ** -0.5, 0.078125, ((0, 4), (1, 4)))
    b_out = normal_values(keys[10], (D,), 0.5, 4.0, ((0, 4),), jnp.float32)
    d_out = draw_d_out(jax.random.fold_in(keys[12], 71), 0)
    return dict(tokens=tokens, ln_gain=ln_gain, ln_bias=ln_bias, w_attn=w_attn, b_qv=b_qv, w_proj=w_proj, b_proj=b_proj, w_fc=w_fc, b_fc=b_fc, w_out=w_out, b_out=b_out, d_out=d_out)


@jax.custom_vjp
def low(v):
    return lax.optimization_barrier(v.astype(jnp.bfloat16)).astype(jnp.float32)

@jax.custom_vjp
def low_back(v):
    return v

def low_keep(v):
    return (low(v), None)

def low_pass(kept, grad):
    return (grad,)

def back_keep(v):
    return (v, None)

def back_low(kept, grad):
    return (low(grad),)
low.defvjp(low_keep, low_pass)
low_back.defvjp(back_keep, back_low)
EPSILON = 1e-05
GELU_COEF = 0.7978845608028654
MASKED = -1e+30

def high_dot(left_side, right_side):
    return jnp.dot(left_side, right_side, precision=lax.Precision.HIGHEST)

def norm_rows(values, gain_row, shift_row):
    row_mean = lax.optimization_barrier(jnp.mean(values, axis=-1, keepdims=True))
    centred = values - row_mean
    spread = lax.optimization_barrier(jnp.mean(centred * centred, axis=-1, keepdims=True))
    return centred * lax.rsqrt(spread + EPSILON) * gain_row + shift_row

def gelu_tanh(inputs):
    return 0.5 * inputs * (1.0 + jnp.tanh(GELU_COEF * (inputs + 0.044715 * inputs * inputs * inputs)))

def attend_one(triple):
    queries = triple[0].reshape(LEN, NH, HS)
    key_part = triple[1].reshape(LEN, NH, HS)
    value_part = triple[2].reshape(LEN, NH, HS)
    scores = jnp.einsum('qhd,khd->hqk', queries, key_part, precision=lax.Precision.HIGHEST) * HS ** (-0.5)
    places = lax.iota(jnp.int32, LEN)
    visible = places[None, :] <= places[:, None]
    scores = low_back(jnp.where(visible[None], scores, MASKED))
    row_peak = lax.optimization_barrier(jnp.max(scores, axis=-1, keepdims=True))
    weights = jnp.exp(scores - row_peak)
    normalized = low(weights / lax.optimization_barrier(jnp.sum(weights, axis=-1, keepdims=True)))
    result = jnp.einsum('hqk,khd->qhd', normalized, value_part, precision=lax.Precision.HIGHEST)
    return low_back(low(result.reshape(LEN, D)))

def forward(tokens, ln_gain, ln_bias, w_attn, b_qv, w_proj, b_proj, w_fc, b_fc, w_out, b_out):
    normed1 = low(norm_rows(tokens, ln_gain[0], ln_bias[0]))
    query_rows = high_dot(normed1, w_attn[0]) + b_qv[0]
    key_rows = high_dot(normed1, w_attn[1])
    value_rows = high_dot(normed1, w_attn[2]) + b_qv[1]
    triples = low_back(low(jnp.stack([query_rows, key_rows, value_rows])))
    per_sequence = triples.reshape(3, TOKENS // LEN, LEN, D).transpose(1, 0, 2, 3)
    attended = lax.map(jax.checkpoint(attend_one), per_sequence).reshape(TOKENS, D)
    branch = low_back(high_dot(attended, w_proj) + b_proj)
    middle = tokens + branch
    normed2 = low(norm_rows(middle, ln_gain[1], ln_bias[1]))
    pre = low_back(high_dot(normed2, w_fc) + b_fc)
    hidden = low(gelu_tanh(pre))
    second_branch = low_back(high_dot(hidden, w_out) + b_out)
    return middle + second_branch

def reference(tokens, ln_gain, ln_bias, w_attn, b_qv, w_proj, b_proj, w_fc, b_fc, w_out, b_out, d_out):
    inputs = tuple((item.astype(jnp.float32) for item in (tokens, ln_gain, ln_bias, w_attn, b_qv, w_proj, b_proj, w_fc, b_fc, w_out, b_out)))
    result, pullback = jax.vjp(forward, *inputs)
    grads = pullback(d_out.astype(jnp.float32))
    return (result.astype(jnp.bfloat16), grads[0].astype(jnp.bfloat16), grads[1], grads[2], grads[3], grads[4], grads[5], grads[6], grads[7], grads[8], grads[9], grads[10])
```

```python
import functools
import jax
import jax.numpy as jnp
from jax import lax
from jax.experimental import pallas as pl
from jax.experimental.pallas import tpu as pltpu
from jax.sharding import PartitionSpec as P

F32, BF16 = jnp.float32, jnp.bfloat16
D, HS, ROWS, PART, QUARTER = 1280, 64, 128, 320, 512
HEADS = 5
EPSILON = 1e-05
GELU_COEF = 0.7978845608028654
MASKED = -1e30
VMEM = pl.BlockSpec(memory_space=pltpu.VMEM)


def nn(a, b):
    return jnp.dot(a, b, preferred_element_type=F32)


def nt(a, b):
    return lax.dot_general(a, b, (((1,), (1,)), ((), ())), preferred_element_type=F32)


def tn(a, b):
    return lax.dot_general(a, b, (((0,), (0,)), ((), ())), preferred_element_type=F32)


class Place:
    def __init__(self):
        self.dp, self.w, self.h = (lax.axis_index(n) for n in ("dp", "width", "heads"))
        self.wc = self.w + 1 - 2 * lax.rem(self.w, 2)
        self.wy = lax.rem(self.w + 2, 4)
        self.wyc = lax.rem(self.wc + 2, 4)
        self.core = (self.dp, self.wc, self.h)
        self.near = (self.dp, self.wy, self.h)
        self.near_core = (self.dp, self.wyc, self.h)
        self.far = (lax.rem(self.dp + 4, 8), self.wy, self.h)

    def z(self, k):
        return (self.dp, self.w, lax.rem(self.h + k, 4))


def sub_block(quarter, w):
    return w + lax.rem(quarter, 2) * (3 - 2 * w)


def greet(devices):
    barrier = pltpu.get_barrier_semaphore()
    for device in devices:
        pl.semaphore_signal(barrier, inc=1, device_id=device, device_id_type=pl.DeviceIdType.MESH)
    pl.semaphore_wait(barrier, len(devices))


class Links:
    def __init__(self, sent, landed):
        self.sent, self.landed, self.count = sent, landed, 0

    def send(self, source, target, device):
        i = self.count
        self.count += 1
        copy = pltpu.make_async_remote_copy(
            src_ref=source, dst_ref=target, send_sem=self.sent.at[i], recv_sem=self.landed.at[i],
            device_id=device, device_id_type=pl.DeviceIdType.MESH,
        )
        copy.start()
        return copy


def rows_of(start, size=ROWS):
    return pl.ds(pl.multiple_of(start, size), size)


def norm_stats(values):
    mean = jnp.mean(values, axis=1, keepdims=True)
    centred = values - mean
    scale = lax.rsqrt(jnp.mean(centred * centred, axis=1, keepdims=True) + EPSILON)
    return centred * scale, scale


def enter_kernel(
    tok, dout, gain, shift, b_proj, b_out, wa, wp, bqv,
    x_o, d_o, vec_o, x1_o, q_o, kv_o, wa_o, wp_o,
    xa, da, vl, vg, sent, landed,
):
    at = Place()
    w, h = at.w, at.h
    links = Links(sent, landed)
    vl[0:2, :] = gain[...]
    vl[2:4, :] = shift[...]
    vl[4:5, :] = b_proj[...]
    vl[5:6, :] = b_out[...]
    vl[6:8, :] = jnp.zeros((2, PART), F32)
    greet([at.core, at.near, at.near_core, at.far, at.z(1), at.z(2), at.z(3)])
    peers = [(at.near, at.wy), (at.near_core, at.wyc), (at.core, at.wc)]
    arrive_x, arrive_v, arrive_d = [], [], []
    for device, peer in peers:
        mine = tok.at[rows_of(sub_block(h, peer) * ROWS)]
        arrive_x.append(links.send(mine, xa.at[w], device))
    for device, peer in peers:
        arrive_v.append(links.send(vl, vg.at[w], device))
    block = pl.ds(pl.multiple_of(w * PART, 64), PART)
    other = pl.ds(pl.multiple_of(at.wy * PART, 64), PART)
    kv_far = links.send(wa.at[1:3], wa_o.at[1:3, block], at.far)
    kv_core = links.send(wa.at[1:3], wa_o.at[1:3, block], at.core)
    for device, peer in peers:
        mine = dout.at[rows_of(sub_block(h, peer) * ROWS)]
        arrive_d.append(links.send(mine, da.at[w], device))
    q_near = links.send(wa.at[0], wa_o.at[0, block], at.near)
    q_core = links.send(wa.at[0], wa_o.at[0, block], at.core)
    p_far = links.send(wp, wp_o.at[w], at.far)
    p_core = links.send(wp, wp_o.at[w], at.core)
    own = rows_of(sub_block(h, w) * ROWS)
    xa[w] = tok[own, :]
    da[w] = dout[own, :]
    vg[w] = vl[...]
    for i in range(3):
        wa_o[i, block, :] = wa[i]
    wp_o[w] = wp[...]
    for copy in arrive_x + arrive_v:
        copy.wait_recv()
    vec = jnp.concatenate([vg[i] for i in range(4)], axis=1)
    vec_o[...] = vec
    x = jnp.concatenate([xa[i] for i in range(4)], axis=1)
    x_o[...] = x
    unit, _ = norm_stats(x.astype(F32))
    x1_o[rows_of(h * ROWS), :] = (unit * vec[0:1] + vec[2:3]).astype(BF16)
    mine = x1_o.at[rows_of(h * ROWS)]
    gather = {k: links.send(mine, mine, at.z(k)) for k in (1, 3, 2)}
    kv_far.wait_recv()
    forwards = [links.send(wa_o.at[1:3, other], wa_o.at[1:3, other], at.core)]
    kv_core.wait_recv()
    forwards[0].wait_recv()
    shares, passed = [], []

    def key_block(c, who):
        return kv_o.at[rows_of((c * 4 + sub_block(c, who)) * ROWS)]

    chunks = [lax.rem(h + i, 4) for i in (0, 1, 3, 2)]
    for i, c in enumerate(chunks):
        if i:
            gather[4 - (0, 1, 3, 2)[i]].wait_recv()
        rows = x1_o[rows_of(c * ROWS), :]
        keys = nn(rows, wa_o[1]).astype(BF16)
        values = (nn(rows, wa_o[2]) + bqv[1:2]).astype(BF16)
        pieces = []
        for head in range(HEADS):
            part = slice(head * HS, (head + 1) * HS)
            pieces += [keys[:, part], values[:, part]]
        key_block(c, w)[...] = jnp.concatenate(pieces, axis=1)
        shares.append(links.send(key_block(c, w), key_block(c, w), at.near))
        shares.append(links.send(key_block(c, w), key_block(c, w), at.core))
    q_near.wait_recv()
    forwards.append(links.send(wa_o.at[0, other], wa_o.at[0, other], at.core))
    p_far.wait_recv()
    forwards.append(links.send(wp_o.at[at.wy], wp_o.at[at.wy], at.core))
    for i, c in enumerate(chunks):
        shares[2 * i].wait_recv()
        passed.append(links.send(key_block(c, at.wy), key_block(c, at.wy), at.core))
    q_core.wait_recv()
    forwards[1].wait_recv()
    zeros = jnp.zeros((ROWS, HS), BF16)
    for c in range(4):
        rows = x1_o[c * ROWS : (c + 1) * ROWS, :]
        queries = ((nn(rows, wa_o[0]) + bqv[0:1]).astype(BF16).astype(F32) * HS**-0.5).astype(BF16)
        pieces = []
        for head in range(HEADS):
            pieces += [queries[:, head * HS : (head + 1) * HS], zeros]
        q_o[c * ROWS : (c + 1) * ROWS, :] = jnp.concatenate(pieces, axis=1)
    for copy in arrive_d:
        copy.wait_recv()
    d_o[...] = jnp.concatenate([da[i] for i in range(4)], axis=1)
    p_core.wait_recv()
    forwards[2].wait_recv()
    for i in range(4):
        shares[2 * i + 1].wait_recv()
        passed[i].wait_recv()
    for copy in arrive_x + arrive_v + arrive_d + [kv_far, kv_core, q_near, q_core, p_far, p_core]:
        copy.wait_send()
    for copy in list(gather.values()) + forwards + shares + passed:
        copy.wait_send()


def enter(tok, dout, gain, shift, b_proj, b_out, wa, wp, bqv):
    return pl.pallas_call(
        enter_kernel,
        name="enter",
        out_shape=(
            jax.ShapeDtypeStruct((ROWS, D), BF16),
            jax.ShapeDtypeStruct((ROWS, D), BF16),
            jax.ShapeDtypeStruct((8, D), F32),
            jax.ShapeDtypeStruct((QUARTER, D), BF16),
            jax.ShapeDtypeStruct((QUARTER, 640), BF16),
            jax.ShapeDtypeStruct((2048, 640), BF16),
            jax.ShapeDtypeStruct((3, D, PART), BF16),
            jax.ShapeDtypeStruct((4, PART, PART), BF16),
        ),
        in_specs=[VMEM] * 9,
        out_specs=(VMEM,) * 8,
        scratch_shapes=[
            pltpu.VMEM((4, ROWS, PART), BF16),
            pltpu.VMEM((4, ROWS, PART), BF16),
            pltpu.VMEM((8, PART), F32),
            pltpu.VMEM((4, 8, PART), F32),
            pltpu.SemaphoreType.DMA((48,)),
            pltpu.SemaphoreType.DMA((48,)),
        ],
        compiler_params=pltpu.CompilerParams(collective_id=1, has_side_effects=True, vmem_limit_bytes=56 * 2**20),
    )(tok, dout, gain, shift, b_proj, b_out, wa, wp, bqv)
ORDER = (1, 3, 2)


def visible_scores(scores, quarter, shift):
    last = scores[quarter * QUARTER :]
    key = lax.broadcasted_iota(jnp.int32, last.shape, 0)
    query = lax.broadcasted_iota(jnp.int32, last.shape, 1) + shift
    last = jnp.where(key <= query, last, MASKED)
    return last if quarter == 0 else jnp.concatenate([scores[: quarter * QUARTER], last], axis=0)


def attend_kernel(
    q, kv, wp, x, d, vec, wf, wo,
    att_o, lse_o, kvt_o, middle_o, x2_o, d_all, wf_o, wo_o, wp_o,
    att_t, stage, parts, wog, sent, landed,
):
    at = Place()
    w, h = at.w, at.h
    links = Links(sent, landed)
    greet([at.core, at.near, at.far, at.z(1), at.z(2), at.z(3)])
    block = pl.ds(pl.multiple_of(w * PART, 64), PART)
    other = pl.ds(pl.multiple_of(at.wy * PART, 64), PART)
    own = rows_of(h * ROWS)
    f_near = links.send(wf, wf_o.at[block], at.near)
    o_far = links.send(wo, wog.at[w], at.far)
    f_core = links.send(wf, wf_o.at[block], at.core)
    o_core = links.send(wo, wog.at[w], at.core)
    d_all[own, :] = d[...]
    d_moves = [links.send(d, d_all.at[own], at.z(k)) for k in ORDER]
    wf_o[block, :] = wf[...]
    wog[w] = wo[...]
    wp_o[...] = jnp.concatenate([wp[i] for i in range(4)], axis=1)

    @pl.loop(0, HEADS)
    def _(head):
        tile = pl.ds(pl.multiple_of(head * 128, 128), 128)
        kvt_o[tile, :] = kv[:, tile].T

    base = links.count

    def attend_chunk(j):
        keys = (j + 1) * QUARTER
        shift = sub_block(j, w) * ROWS

        @pl.loop(0, HEADS)
        def _(head):
            tile = pl.ds(pl.multiple_of(head * 128, 128), 128)
            scores = nt(kv[0:keys, tile], q[j * ROWS : (j + 1) * ROWS, tile])
            scores = visible_scores(scores, j, shift)
            peak = jnp.max(scores, axis=0, keepdims=True)
            weights = jnp.exp(scores - peak)
            total = jnp.sum(weights, axis=0, keepdims=True)
            probs = (weights * (1.0 / total)).astype(BF16)
            result = nn(kvt_o[tile, 0:keys], probs)
            att_t[pl.ds(pl.multiple_of(head * HS, HS), HS), :] = result[HS:, :]
            lse_o[pl.ds(j * 8 + head, 1), :] = peak + jnp.log(total)

    def move(i, j):
        return pltpu.make_async_remote_copy(
            src_ref=stage.at[j], dst_ref=parts.at[i], send_sem=sent.at[base + i], recv_sem=landed.at[base + i],
            device_id=(at.dp, w, j), device_id_type=pl.DeviceIdType.MESH,
        )

    @pl.loop(0, 4)
    def _(i):
        j = lax.rem(h + i + 1, 4)
        for case in range(4):
            pl.when(j == case)(functools.partial(attend_chunk, case))
        attended = att_t[...].T.astype(BF16)
        att_o[rows_of(j * ROWS), :] = attended
        stage[j] = nn(attended, wp_o[...]).astype(BF16)

        @pl.when(i < 3)
        def _():
            move(i, j).start()

    links.count += 3
    f_near.wait_recv()
    f_pass = links.send(wf_o.at[other], wf_o.at[other], at.core)
    o_far.wait_recv()
    o_pass = links.send(wog.at[at.wy], wog.at[at.wy], at.core)
    middle = x[...].astype(F32) + vec[4:5, :] + stage[h].astype(F32)
    for i in range(3):
        move(i, lax.rem(h + i + 1, 4)).wait()
        middle = middle + parts[i].astype(F32)
    middle_o[...] = middle
    unit, _ = norm_stats(middle)
    x2_o[...] = (unit * vec[1:2] + vec[3:4]).astype(BF16)
    o_core.wait_recv()
    o_pass.wait_recv()

    @pl.loop(0, 10)
    def _(i):
        rows = rows_of(i * ROWS)
        wo_o[rows, :] = jnp.concatenate([wog[part, rows, :] for part in range(4)], axis=1)

    f_core.wait_recv()
    f_pass.wait_recv()
    for copy in d_moves:
        copy.wait()
    for copy in (f_near, o_far, f_core, o_core, f_pass, o_pass):
        copy.wait_send()


def attend(q, kv, wp, x, d, vec, wf, wo):
    return pl.pallas_call(
        attend_kernel,
        name="attend",
        out_shape=(
            jax.ShapeDtypeStruct((QUARTER, PART), BF16),
            jax.ShapeDtypeStruct((32, 128), F32),
            jax.ShapeDtypeStruct((640, 2048), BF16),
            jax.ShapeDtypeStruct((ROWS, D), F32),
            jax.ShapeDtypeStruct((ROWS, D), BF16),
            jax.ShapeDtypeStruct((QUARTER, D), BF16),
            jax.ShapeDtypeStruct((D, D), BF16),
            jax.ShapeDtypeStruct((D, D), BF16),
            jax.ShapeDtypeStruct((PART, D), BF16),
        ),
        in_specs=[VMEM] * 8,
        out_specs=(VMEM,) * 9,
        scratch_shapes=[
            pltpu.VMEM((PART, ROWS), F32),
            pltpu.VMEM((4, ROWS, D), BF16),
            pltpu.VMEM((3, ROWS, D), BF16),
            pltpu.VMEM((4, D, PART), BF16),
            pltpu.SemaphoreType.DMA((16,)),
            pltpu.SemaphoreType.DMA((16,)),
        ],
        compiler_params=pltpu.CompilerParams(collective_id=2, has_side_effects=True, vmem_limit_bytes=56 * 2**20),
    )(q, kv, wp, x, d, vec, wf, wo)


def norm_gradient(grad, unit, scale, gain):
    scaled = grad * gain
    mean = jnp.mean(scaled, axis=1, keepdims=True)
    along = jnp.mean(scaled * unit, axis=1, keepdims=True)
    return scale * (scaled - mean - unit * along)


def feed_kernel(
    x2, middle, d_all, wf, wo, b_fc, vec,
    out_o, gm_o, gb_o, dwf_o, dwo_o, sums_o, dbf_o,
    x2_all, gh, hid, gp, stage, parts, stage_b, parts_b, back, sent, landed,
):
    at = Place()
    w, h = at.w, at.h
    links = Links(sent, landed)
    greet([at.core, at.near, at.near_core, at.z(1), at.z(2), at.z(3)])
    own = rows_of(h * ROWS)
    x2_all[own, :] = x2[...]
    gather = {k: links.send(x2, x2_all.at[own], at.z(k)) for k in ORDER}
    tiles = D // 256

    @pl.loop(0, tiles)
    def _(i):
        tile = pl.ds(pl.multiple_of(i * 256, 256), 256)
        gh[:, tile] = nt(d_all[...], wo[tile, :])

    chunks = [lax.rem(h + i, 4) for i in (0, 1, 3, 2)]
    moves = []
    for i, c in enumerate(chunks):
        k = (0, 1, 3, 2)[i]
        if i:
            gather[4 - k].wait_recv()
        rows = rows_of(c * ROWS)

        @pl.loop(0, tiles)
        def _(t):
            tile = pl.ds(pl.multiple_of(t * 256, 256), 256)
            u = nn(x2_all[rows, :], wf[:, tile]) + b_fc[:, tile]
            square = u * u
            th = jnp.tanh(GELU_COEF * (u + 0.044715 * square * u))
            hid[rows, tile] = (0.5 * u * (1.0 + th)).astype(BF16)
            slope = 0.5 * (1.0 + th) + 0.5 * u * (1.0 - th * th) * (GELU_COEF * (1.0 + 0.134145 * square))
            gp[rows, tile] = (gh[rows, tile] * slope).astype(BF16)

        @pl.loop(0, tiles)
        def _(t):
            tile = pl.ds(pl.multiple_of(t * 256, 256), 256)
            stage[c, :, tile] = nt(gp[rows, :], wf[tile, :]).astype(BF16)

        if i:
            moves.append(links.send(stage.at[c], parts.at[i - 1], at.z(k)))

    @pl.loop(0, tiles)
    def _(t):
        tile = pl.ds(pl.multiple_of(t * 256, 256), 256)
        stage_b[:, tile] = nn(hid[...], wo[:, tile]).astype(BF16)

    moves_b = [
        links.send(stage_b.at[rows_of(chunks[i] * ROWS)], parts_b.at[i - 1], at.z((0, 1, 3, 2)[i])) for i in (1, 2, 3)
    ]
    dbf_o[...] = jnp.sum(gp[...].astype(F32), axis=0, keepdims=True)

    @pl.loop(0, tiles)
    def _(t):
        tile = pl.ds(pl.multiple_of(t * 256, 256), 256)
        dwf_o[tile, :] = tn(x2_all[:, tile], gp[...]).astype(BF16)
        dwo_o[tile, :] = tn(hid[:, tile], d_all[...]).astype(BF16)

    grad_normed = stage[h].astype(F32)
    for i in range(3):
        moves[i].wait_recv()
        grad_normed = grad_normed + parts[i].astype(F32)
    unit, scale = norm_stats(middle[...])
    grad = d_all[own, :].astype(F32)
    grad_middle = grad + norm_gradient(grad_normed, unit, scale, vec[1:2, :])
    gm_o[...] = grad_middle
    branch = grad_middle.astype(BF16)
    gb_o[...] = branch
    sums_o[0:1, :] = jnp.sum(grad_normed * unit, axis=0, keepdims=True)
    sums_o[1:2, :] = jnp.sum(grad_normed, axis=0, keepdims=True)
    sums_o[2:3, :] = jnp.sum(grad, axis=0, keepdims=True)
    sums_o[3:4, :] = jnp.sum(branch.astype(F32), axis=0, keepdims=True)
    sums_o[4:8, :] = jnp.zeros((4, D), F32)
    result = middle[...] + vec[5:6, :] + stage_b[own, :].astype(F32)
    for i in range(3):
        moves_b[i].wait_recv()
        result = result + parts_b[i].astype(F32)
    result = result.astype(BF16)
    for part in range(4):
        back[part] = result[:, part * PART : (part + 1) * PART]
    mine = sub_block(h, w)
    out_o[mine] = back[w]
    returns = [
        links.send(back.at[peer], out_o.at[mine], device)
        for device, peer in ((at.near, at.wy), (at.near_core, at.wyc), (at.core, at.wc))
    ]
    for copy in returns:
        copy.wait_recv()
    for copy in list(gather.values()) + moves + moves_b + returns:
        copy.wait_send()


def feed(x2, middle, d_all, wf, wo, b_fc, vec):
    return pl.pallas_call(
        feed_kernel,
        name="feed",
        out_shape=(
            jax.ShapeDtypeStruct((4, ROWS, PART), BF16),
            jax.ShapeDtypeStruct((ROWS, D), F32),
            jax.ShapeDtypeStruct((ROWS, D), BF16),
            jax.ShapeDtypeStruct((D, D), BF16),
            jax.ShapeDtypeStruct((D, D), BF16),
            jax.ShapeDtypeStruct((8, D), F32),
            jax.ShapeDtypeStruct((1, D), F32),
        ),
        in_specs=[VMEM] * 7,
        out_specs=(VMEM,) * 7,
        scratch_shapes=[
            pltpu.VMEM((QUARTER, D), BF16),
            pltpu.VMEM((QUARTER, D), F32),
            pltpu.VMEM((QUARTER, D), BF16),
            pltpu.VMEM((QUARTER, D), BF16),
            pltpu.VMEM((4, ROWS, D), BF16),
            pltpu.VMEM((3, ROWS, D), BF16),
            pltpu.VMEM((QUARTER, D), BF16),
            pltpu.VMEM((3, ROWS, D), BF16),
            pltpu.VMEM((4, ROWS, PART), BF16),
            pltpu.SemaphoreType.DMA((16,)),
            pltpu.SemaphoreType.DMA((16,)),
        ],
        compiler_params=pltpu.CompilerParams(collective_id=3, has_side_effects=True, vmem_limit_bytes=56 * 2**20),
    )(x2, middle, d_all, wf, wo, b_fc, vec)


def attend_back_kernel(
    gb, att, lse, q, kv, kvt, wp,
    gmx_o, dwp_o,
    g_all, go, dq_t, dkv, give, take, give_y, take_y, sent, landed,
):
    at = Place()
    w, h = at.w, at.h
    links = Links(sent, landed)
    greet([at.core, at.near, at.z(1), at.z(2), at.z(3)])
    own = rows_of(h * ROWS)
    g_all[own, :] = gb[...]
    gather = {k: links.send(gb, g_all.at[own], at.z(k)) for k in ORDER}
    dkv[...] = jnp.zeros(dkv.shape, F32)
    zeros = jnp.zeros((ROWS, HS), BF16)

    def back_chunk(j):
        keys = (j + 1) * QUARTER
        shift = sub_block(j, w) * ROWS
        rows = slice(j * ROWS, (j + 1) * ROWS)

        @pl.loop(0, HEADS)
        def _(head):
            tile = pl.ds(pl.multiple_of(head * 128, 128), 128)
            query, grad = q[rows, tile], go[:, tile]
            scores = visible_scores(nt(kv[0:keys, tile], query), j, shift)
            probs = jnp.exp(scores - lse[pl.ds(j * 8 + head, 1), :])
            grad_probs = nt(kv[0:keys, tile], grad)
            inner = jnp.sum(grad_probs * probs, axis=0, keepdims=True)
            grad_scores = (probs * (grad_probs - inner)).astype(BF16)
            both = jnp.concatenate([grad_scores, probs.astype(BF16)], axis=1)
            dkv[0:keys, tile] += nn(both, jnp.concatenate([query, grad], axis=0))
            result = nn(kvt[tile, 0:keys], grad_scores)
            dq_t[pl.ds(pl.multiple_of(head * HS, HS), HS), :] = result[:HS, :] * HS**-0.5

    for i in range(4):
        k = (0, 1, 3, 2)[i]
        if i:
            gather[4 - k].wait_recv()
        c = lax.rem(h + k, 4)
        rows = rows_of(c * ROWS)
        grad = nt(g_all[rows, :], wp[...]).astype(BF16)
        pieces = []
        for head in range(HEADS):
            pieces += [zeros, grad[:, head * HS : (head + 1) * HS]]
        go[...] = jnp.concatenate(pieces, axis=1)
        for case in range(4):
            pl.when(c == case)(functools.partial(back_chunk, case))
        gmx_o[rows, 0:PART] = dq_t[...].T.astype(BF16)

    def piece(who, j):
        return dkv[rows_of((j * 4 + sub_block(j, who)) * ROWS), :]

    for j in range(4):
        rows = slice(j * ROWS, (j + 1) * ROWS)
        give[1, rows, :] = piece(at.wyc, j).astype(BF16)
    moves = [links.send(give.at[1], take.at[1], at.core)]
    for j in range(4):
        rows = slice(j * ROWS, (j + 1) * ROWS)
        give[0, rows, :] = piece(at.wc, j).astype(BF16)
    moves.append(links.send(give.at[0], take.at[0], at.core))
    moves[0].wait_recv()
    for j in range(4):
        rows = slice(j * ROWS, (j + 1) * ROWS)
        give_y[rows, :] = (piece(at.wy, j) + take[1, rows, :].astype(F32)).astype(BF16)
    moves.append(links.send(give_y, take_y, at.near))
    for i in range(4):
        part = slice(i * PART, (i + 1) * PART)
        dwp_o[i] = tn(att[...], g_all[:, part]).astype(BF16)
    moves[1].wait_recv()
    moves[2].wait_recv()
    for j in range(4):
        rows = slice(j * ROWS, (j + 1) * ROWS)
        total = (piece(w, j) + take[0, rows, :].astype(F32) + take_y[rows, :].astype(F32)).astype(BF16)
        pieces = [total[:, head * 128 : head * 128 + HS] for head in range(HEADS)]
        pieces += [total[:, head * 128 + HS : (head + 1) * 128] for head in range(HEADS)]
        gmx_o[rows, PART:] = jnp.concatenate(pieces, axis=1)
    for copy in list(gather.values()) + moves:
        copy.wait_send()


def attend_back(gb, att, lse, q, kv, kvt, wp):
    return pl.pallas_call(
        attend_back_kernel,
        name="attend_back",
        out_shape=(
            jax.ShapeDtypeStruct((QUARTER, 3 * PART), BF16),
            jax.ShapeDtypeStruct((4, PART, PART), BF16),
        ),
        in_specs=[VMEM] * 7,
        out_specs=(VMEM,) * 2,
        scratch_shapes=[
            pltpu.VMEM((QUARTER, D), BF16),
            pltpu.VMEM((ROWS, 640), BF16),
            pltpu.VMEM((PART, ROWS), F32),
            pltpu.VMEM((2048, 640), F32),
            pltpu.VMEM((2, QUARTER, 640), BF16),
            pltpu.VMEM((2, QUARTER, 640), BF16),
            pltpu.VMEM((QUARTER, 640), BF16),
            pltpu.VMEM((QUARTER, 640), BF16),
            pltpu.SemaphoreType.DMA((8,)),
            pltpu.SemaphoreType.DMA((8,)),
        ],
        compiler_params=pltpu.CompilerParams(collective_id=4, has_side_effects=True, vmem_limit_bytes=56 * 2**20),
    )(gb, att, lse, q, kv, kvt, wp)


def leave_kernel(
    gmx, wa, x1, x, gm, vec,
    dt_o, dwa_o, dbqv_o, sums_o,
    stage, parts, back, sent, landed,
):
    at = Place()
    w, h = at.w, at.h
    links = Links(sent, landed)
    greet([at.core, at.near, at.near_core, at.z(1), at.z(2), at.z(3)])
    moves = []
    for k in (2, 1, 3, 0):
        c = lax.rem(h + k, 4)
        rows = rows_of(c * ROWS)
        partial = nt(gmx[rows, 0:PART], wa[0])
        for i in (1, 2):
            partial = partial + nt(gmx[rows, i * PART : (i + 1) * PART], wa[i])
        stage[c] = partial.astype(BF16)
        if k:
            moves.append(links.send(stage.at[c], parts.at[k - 1], at.z(k)))

    @pl.loop(0, D // 256)
    def _(t):
        tile = pl.ds(pl.multiple_of(t * 256, 256), 256)
        dwa_o[tile, :] = tn(x1[:, tile], gmx[...]).astype(BF16)

    mixed = jnp.sum(gmx[...].astype(F32), axis=0, keepdims=True)
    dbqv_o[0:1, :] = mixed[:, :PART]
    dbqv_o[1:2, :] = mixed[:, 2 * PART :]
    grad_normed = stage[h].astype(F32)
    for copy, k in zip(moves, (2, 1, 3)):
        copy.wait_recv()
        grad_normed = grad_normed + parts[k - 1].astype(F32)
    unit, scale = norm_stats(x[...].astype(F32))
    result = (gm[...] + norm_gradient(grad_normed, unit, scale, vec[0:1, :])).astype(BF16)
    sums_o[0:1, :] = jnp.sum(grad_normed * unit, axis=0, keepdims=True)
    sums_o[1:2, :] = jnp.sum(grad_normed, axis=0, keepdims=True)
    sums_o[2:8, :] = jnp.zeros((6, D), F32)
    for part in range(4):
        back[part] = result[:, part * PART : (part + 1) * PART]
    mine = sub_block(h, w)
    dt_o[mine] = back[w]
    returns = [
        links.send(back.at[peer], dt_o.at[mine], device)
        for device, peer in ((at.near, at.wy), (at.near_core, at.wyc), (at.core, at.wc))
    ]
    for copy in returns:
        copy.wait_recv()
    for copy in moves + returns:
        copy.wait_send()


def leave(gmx, wa, x1, x, gm, vec):
    return pl.pallas_call(
        leave_kernel,
        name="leave",
        out_shape=(
            jax.ShapeDtypeStruct((4, ROWS, PART), BF16),
            jax.ShapeDtypeStruct((D, 3 * PART), BF16),
            jax.ShapeDtypeStruct((2, PART), F32),
            jax.ShapeDtypeStruct((8, D), F32),
        ),
        in_specs=[VMEM] * 6,
        out_specs=(VMEM,) * 4,
        scratch_shapes=[
            pltpu.VMEM((4, ROWS, D), BF16),
            pltpu.VMEM((3, ROWS, D), BF16),
            pltpu.VMEM((4, ROWS, PART), BF16),
            pltpu.SemaphoreType.DMA((8,)),
            pltpu.SemaphoreType.DMA((8,)),
        ],
        compiler_params=pltpu.CompilerParams(collective_id=5, has_side_effects=True, vmem_limit_bytes=56 * 2**20),
    )(gmx, wa, x1, x, gm, vec)


def shards(tokens, ln_gain, ln_bias, w_attn, b_qv, w_proj, b_proj, w_fc, b_fc, w_out, b_out, d_out):
    x, d, vec, x1, q, kv, wa, wp = enter(
        tokens, d_out, ln_gain, ln_bias, b_proj.reshape(1, -1), b_out.reshape(1, -1), w_attn, w_proj, b_qv
    )
    att, lse, kvt, middle, x2, d_all, wf, wo, wp = attend(q, kv, wp, x, d, vec, w_fc, w_out)
    block_out, gm, gb, dwf, dwo, sums_second, dbf = feed(x2, middle, d_all, wf, wo, b_fc.reshape(1, -1), vec)
    gmx, dwp = attend_back(gb, att, lse, q, kv, kvt, wp)
    d_tokens, dwa, dbqv, sums_first = leave(gmx, wa, x1, x, gm, vec)

    def scatter(grad, dim):
        return lax.psum_scatter(grad, "width", scatter_dimension=dim, tiled=True)

    d_w_fc = lax.psum(scatter(dwf, 0), "dp").astype(F32)
    d_w_out = lax.psum(scatter(dwo, 1), "dp").astype(F32)
    d_w_proj = lax.psum(scatter(dwp, 0), "dp").astype(F32)[0]
    d_w_attn = lax.psum(scatter(dwa, 0), "dp").astype(F32).reshape(PART, 3, PART).transpose(1, 0, 2)
    sums = lax.psum(jnp.concatenate([sums_first[0:2], sums_second[0:4]], 0), ("dp", "heads", "width"))
    sums = lax.dynamic_slice_in_dim(sums, lax.axis_index("width") * PART, PART, 1)
    d_ln_gain = jnp.stack((sums[0], sums[2]))
    d_ln_bias = jnp.stack((sums[1], sums[3]))
    d_b_out, d_b_proj = sums[4], sums[5]
    d_b_fc, d_b_qv = lax.psum((dbf, dbqv), ("dp", "width"))
    return (
        block_out.reshape(QUARTER, PART),
        d_tokens.reshape(QUARTER, PART),
        d_ln_gain,
        d_ln_bias,
        d_w_attn,
        d_b_qv,
        d_w_proj,
        d_b_proj,
        d_w_fc,
        d_b_fc[0],
        d_w_out,
        d_b_out,
    )
def solution(mesh):
    in_specs = (
        P(("dp", "heads"), "width"),
        P(None, "width"),
        P(None, "width"),
        P(None, "width", "heads"),
        P(None, "heads"),
        P("heads", "width"),
        P("width"),
        P("width", "heads"),
        P("heads"),
        P("heads", "width"),
        P("width"),
        P(("dp", "heads"), "width"),
    )
    out_specs = (
        P(("dp", "heads"), "width"),
        P(("dp", "heads"), "width"),
        P(None, "width"),
        P(None, "width"),
        P(None, "width", "heads"),
        P(None, "heads"),
        P("heads", "width"),
        P("width"),
        P("width", "heads"),
        P("heads"),
        P("heads", "width"),
        P("width"),
    )
    return jax.shard_map(shards, mesh=mesh, in_specs=in_specs, out_specs=out_specs, check_vma=False)
```

```python
import functools

import jax
import jax.numpy as jnp
from jax import lax
from jax.experimental import pallas as pl
from jax.experimental.pallas import tpu as pltpu
from jax.sharding import PartitionSpec as P

F32, BF16 = jnp.float32, jnp.bfloat16
D, HS, ROWS, PART, QUARTER, HEADS = 1280, 64, 128, 320, 512, 5
PAIR = 2 * PART
STRIP = PART // 4
HALF = ROWS // 2
EPSILON = 1e-05
GELU_COEF = 0.7978845608028654
MASKED = -1e30
VMEM = pl.BlockSpec(memory_space=pltpu.VMEM)
ANY = pl.BlockSpec(memory_space=pl.ANY)
TILES = D // 256


def nn(a, b):
    return jnp.dot(a, b, preferred_element_type=F32)


def nt(a, b):
    return lax.dot_general(a, b, (((1,), (1,)), ((), ())), preferred_element_type=F32)


def tn(a, b):
    return lax.dot_general(a, b, (((0,), (0,)), ((), ())), preferred_element_type=F32)


def rows_of(start, size=ROWS):
    return pl.ds(pl.multiple_of(start, size), size)


def block_of(who):
    return pl.ds(pl.multiple_of(who * PART, 64), PART)


def tile_of(i, size):
    return pl.ds(pl.multiple_of(i * size, size), size)


def sub_block(quarter, w):
    return w + lax.rem(quarter, 2) * (3 - 2 * w)


class Place:
    def __init__(self):
        self.dp, self.w, self.h = (lax.axis_index(n) for n in ("dp", "width", "heads"))
        self.x = lax.rem(self.dp, 4)
        self.wc = self.w + 1 - 2 * lax.rem(self.w, 2)
        self.wy = lax.rem(self.w + 2, 4)
        self.wyc = lax.rem(self.wc + 2, 4)
        across = lax.rem(self.dp + 4, 8)
        self.core = (self.dp, self.wc, self.h)
        self.near = (self.dp, self.wy, self.h)
        self.near_core = (self.dp, self.wyc, self.h)
        self.far = (across, self.wy, self.h)
        self.opposite = (across, self.w, self.h)
        self.width_peers = ((self.near, self.wy), (self.near_core, self.wyc), (self.core, self.wc))

    def along_z(self, k):
        return (self.dp, self.w, lax.rem(self.h + k, 4))

    def along_x(self, k):
        return (self.dp - self.x + lax.rem(self.x + k, 4), self.w, self.h)

    def chunk(self, k):
        return lax.rem(self.h + k, 4)


def greet(devices):
    barrier = pltpu.get_barrier_semaphore()
    for device in devices:
        pl.semaphore_signal(barrier, inc=1, device_id=device, device_id_type=pl.DeviceIdType.MESH)
    pl.semaphore_wait(barrier, len(devices))


class Move:
    def __init__(self, copy):
        self.copy, self.left = copy, False
        self.start, self.wait_recv = copy.start, copy.wait_recv

    def wait_send(self):
        if not self.left:
            self.copy.wait_send()
        self.left = True

    def wait(self):
        self.wait_recv()
        self.wait_send()


class Links:
    def __init__(self, sent, landed):
        self.sent, self.landed, self.copies = sent, landed, []

    def plan(self, source, target, device):
        i = len(self.copies)
        copy = pltpu.make_async_remote_copy(
            src_ref=source,
            dst_ref=target,
            send_sem=self.sent.at[i],
            recv_sem=self.landed.at[i],
            device_id=device,
            device_id_type=pl.DeviceIdType.MESH,
        )
        self.copies.append(Move(copy))
        return self.copies[-1]

    def send(self, source, target, device):
        copy = self.plan(source, target, device)
        copy.start()
        return copy


class GatherZ:
    def __init__(self, links, at, source, rows):
        self.links, self.at, self.rows = links, at, rows
        own = rows.at[rows_of(at.h * ROWS)]
        self.right = links.send(source, own, at.along_z(1))
        self.left = links.send(source, own, at.along_z(3))
        low = rows.at[rows_of(at.chunk(3) * ROWS, HALF)]
        high = rows.at[rows_of(at.chunk(1) * ROWS + HALF, HALF)]
        self.low = links.plan(low, low, at.along_z(1))
        self.high = links.plan(high, high, at.along_z(3))

    def neighbours(self):
        self.left.wait_recv()
        self.high.start()
        self.right.wait_recv()
        self.low.start()

    def rest(self):
        self.low.wait_recv()
        self.high.wait_recv()


class SumZ:
    def __init__(self, links, at, stage, parts, over):
        self.stage, self.parts, self.over, self.at = stage, parts, over, at
        ahead, behind, across = at.chunk(1), at.chunk(3), at.chunk(2)
        right, left = at.along_z(1), at.along_z(3)
        top, bottom = pl.ds(0, HALF), pl.ds(HALF, HALF)
        self.ahead, self.behind = ahead, behind
        self.far_right = links.plan(stage.at[across, top], over.at[0], right)
        self.far_left = links.plan(stage.at[across, bottom], over.at[1], left)
        self.right_bottom = links.plan(stage.at[ahead, bottom], parts.at[0, bottom], right)
        self.right_top = links.plan(stage.at[ahead, top], parts.at[0, top], right)
        self.left_top = links.plan(stage.at[behind, top], parts.at[1, top], left)
        self.left_bottom = links.plan(stage.at[behind, bottom], parts.at[1, bottom], left)

    def sent(self):
        for copy in (self.far_right, self.far_left, self.right_bottom, self.right_top, self.left_top, self.left_bottom):
            copy.wait_send()

    def send_across(self):
        self.far_right.start()
        self.far_left.start()

    def send_ahead(self):
        self.right_bottom.start()
        self.far_right.wait_recv()
        joined = self.stage[self.ahead, 0:HALF, :].astype(F32) + self.over[0].astype(F32)
        self.stage[self.ahead, 0:HALF, :] = joined.astype(BF16)
        self.right_top.start()

    def send_behind(self):
        self.left_top.start()
        self.far_left.wait_recv()
        joined = self.stage[self.behind, HALF:, :].astype(F32) + self.over[1].astype(F32)
        self.stage[self.behind, HALF:, :] = joined.astype(BF16)
        self.left_bottom.start()

    def result(self):
        for copy in (self.right_bottom, self.right_top, self.left_top, self.left_bottom):
            copy.wait_recv()
        return self.stage[self.at.h].astype(F32) + self.parts[0].astype(F32) + self.parts[1].astype(F32)


class GradientSum:
    def __init__(self, links, at, grad, columns, pair, strips, cross, final):
        self.links, self.at, self.grad, self.columns = links, at, grad, columns
        self.pair, self.strips, self.cross, self.final = pair, strips, cross, final
        self.strip = rows_of(at.x * STRIP, STRIP)
        self.total = [pair.at[0, self.strip], pair.at[1, self.strip]]

    def mine(self, who):
        return self.grad.at[block_of(who), self.columns]

    def send_core(self):
        at, links = self.at, self.links
        self.core = [
            links.send(self.mine(at.wc), self.pair.at[0], at.core),
            links.send(self.mine(at.wyc), self.pair.at[1], at.core),
        ]

    def send_x(self):
        at, links = self.at, self.links
        for i, who in ((0, at.w), (1, at.wy)):
            self.core[i].wait()
            self.pair[i] = (self.pair[i].astype(F32) + self.mine(who)[...].astype(F32)).astype(BF16)
        self.along = [
            links.send(
                self.pair.at[:, rows_of(lax.rem(at.x + k, 4) * STRIP, STRIP)], self.strips.at[k - 1], at.along_x(k)
            )
            for k in (2, 1, 3)
        ]

    def send_y(self):
        at, links = self.at, self.links
        for copy in self.along:
            copy.wait()
        for i in range(2):
            joined = self.total[i][...].astype(F32)
            for k in range(3):
                joined = joined + self.strips[k, i].astype(F32)
            self.total[i][...] = joined.astype(BF16)
        self.over = [
            links.send(self.total[1], self.cross.at[0], at.near),
            links.send(self.total[1], self.cross.at[1], at.far),
            links.send(self.total[0], self.cross.at[2], at.opposite),
        ]

    def send_back(self):
        at, links = self.at, self.links
        for copy in self.over:
            copy.wait()
        joined = self.total[0][...].astype(F32)
        for k in range(3):
            joined = joined + self.cross[k].astype(F32)
        self.total[0][...] = joined.astype(BF16)
        strip = self.final.at[self.strip]
        self.back = [links.send(self.total[0], strip, at.along_x(k)) for k in (2, 1, 3)]
        return strip

    def finish(self):
        for copy in self.back:
            copy.wait()


def norm_stats(values):
    mean = jnp.mean(values, axis=1, keepdims=True)
    centred = values - mean
    scale = lax.rsqrt(jnp.mean(centred * centred, axis=1, keepdims=True) + EPSILON)
    return centred * scale, scale


def norm_gradient(grad, unit, scale, gain):
    scaled = grad * gain
    mean = jnp.mean(scaled, axis=1, keepdims=True)
    along = jnp.mean(scaled * unit, axis=1, keepdims=True)
    return scale * (scaled - mean - unit * along)


def interleave(first, second):
    pieces = []
    for head in range(HEADS):
        part = slice(head * HS, (head + 1) * HS)
        pieces += [first[:, part], second[:, part]]
    return jnp.concatenate(pieces, axis=1)


def visible_scores(scores, quarter, shift):
    last = scores[quarter * QUARTER :]
    key = lax.broadcasted_iota(jnp.int32, last.shape, 0)
    query = lax.broadcasted_iota(jnp.int32, last.shape, 1) + shift
    last = jnp.where(key <= query, last, MASKED)
    return last if quarter == 0 else jnp.concatenate([scores[: quarter * QUARTER], last], axis=0)


def column_sum(values):
    return jnp.sum(values, axis=0, keepdims=True)


SCRATCH = dict(
    wkv=((D, PAIR), BF16),
    wq=((D, PART), BF16),
    wpt=((D, PART), BF16),
    wf=((D, D), BF16),
    wt=((D, D), BF16),
    wa_raw=((3, PART, PART), BF16),
    wp_raw=((PART, PART), BF16),
    wo_raw=((D, PART), BF16),
    xa=((4, ROWS, PART), BF16),
    da=((4, ROWS, PART), BF16),
    vl=((8, PART), F32),
    vg=((4, 8, PART), F32),
    vec=((8, D), F32),
    bf=((8, D), F32),
    x=((ROWS, D), BF16),
    x1=((QUARTER, D), BF16),
    q=((QUARTER, PAIR), BF16),
    kv=((2048, PAIR), BF16),
    kvt=((PAIR, 2048), BF16),
    att=((QUARTER, PART), BF16),
    att_t=((PART, ROWS), F32),
    lse=((32, 128), F32),
    middle=((ROWS, D), F32),
    stage=((4, ROWS, D), BF16),
    parts=((2, ROWS, D), BF16),
    over=((2, HALF, D), BF16),
    d_all=((QUARTER, D), BF16),
    x2=((QUARTER, D), BF16),
    hid=((QUARTER, D), BF16),
    gp=((QUARTER, D), BF16),
    stage_g=((4, ROWS, D), BF16),
    parts_g=((3, ROWS, D), BF16),
    parts_b=((2, ROWS, D), BF16),
    over_b=((2, HALF, D), BF16),
    back=((4, ROWS, PART), BF16),
    gm=((ROWS, D), F32),
    grad_f=((D, D), BF16),
    grad_t=((D, D), BF16),
    pair_f=((2, PART, D), BF16),
    pair_t=((2, PART, D), BF16),
    pair_q=((2, PART, PAIR), BF16),
    pair_k=((2, PART, PAIR), BF16),
    strips_f=((3, 2, STRIP, D), BF16),
    strips_t=((3, 2, STRIP, D), BF16),
    strips_q=((3, 2, STRIP, PAIR), BF16),
    strips_k=((3, 2, STRIP, PAIR), BF16),
    cross_f=((3, STRIP, D), BF16),
    cross_t=((3, STRIP, D), BF16),
    cross_q=((3, STRIP, PAIR), BF16),
    cross_k=((3, STRIP, PAIR), BF16),
    g_all=((QUARTER, D), BF16),
    go=((ROWS, PAIR), BF16),
    dkv=((2048, PAIR), F32),
    take=((2, 4, ROWS, PAIR), BF16),
    take_y=((QUARTER, PAIR), BF16),
    dq=((QUARTER, PART), BF16),
    gkv=((QUARTER, PAIR), BF16),
    sums=((16, D), F32),
    sums_z=((3, 8, D), F32),
    sums_w=((4, 8, PART), F32),
    take_w=((3, 8, PART), F32),
    take_v=((3, 8, D), F32),
    sums_d=((8, D), F32),
    sums_x=((3, 8, D), F32),
    sums_o=((8, D), F32),
)
COPIES = 160


def block_kernel(*refs):
    names = ("tok", "dout", "gain", "shift", "b_proj", "b_out", "wa_in", "bqv", "wp_in", "wf_in", "b_fc", "wo_in")
    names += ("bo", "dt", "fin_f", "fin_t", "fin_q", "fin_k", "fin_v")
    names += tuple(SCRATCH) + ("sent", "landed", "local")
    r = dict(zip(names, refs))
    (tok, dout, gain, shift, b_proj, b_out, wa_in, bqv, wp_in, wf_in, b_fc, wo_in) = refs[:12]
    (bo, dt, fin_f, fin_t, fin_q, fin_k, fin_v) = refs[12:19]
    at = Place()
    w, h = at.w, at.h
    links = Links(r["sent"], r["landed"])
    local = r["local"]
    own = rows_of(h * ROWS)
    mine = sub_block(h, w)
    vec = r["vec"]

    loads = [
        pltpu.make_async_copy(wa_in, r["wa_raw"], local.at[0]),
        pltpu.make_async_copy(wp_in, r["wp_raw"], local.at[1]),
        pltpu.make_async_copy(wo_in, r["wo_raw"], local.at[2]),
        pltpu.make_async_copy(wf_in, r["wf"].at[block_of(w)], local.at[3]),
        pltpu.make_async_copy(tok.at[rows_of(mine * ROWS)], r["xa"].at[w], local.at[4]),
        pltpu.make_async_copy(dout.at[rows_of(mine * ROWS)], r["da"].at[w], local.at[5]),
    ]
    for copy in loads:
        copy.start()
    vl = r["vl"]
    vl[0:2, :] = gain[...]
    vl[2:4, :] = shift[...]
    vl[4:5, :] = b_proj[...].reshape(1, PART)
    vl[5:6, :] = b_out[...].reshape(1, PART)
    r["bf"][0:1, :] = b_fc[...].reshape(1, D)
    vl[6:8, :] = jnp.zeros((2, PART), F32)
    greet(
        [at.core, at.near, at.near_core, at.far, at.opposite]
        + [at.along_z(k) for k in (1, 2, 3)]
        + [at.along_x(k) for k in (1, 2, 3)]
    )

    def spread(source, slots):
        return [
            links.send(source.at[rows_of(sub_block(h, peer) * ROWS)], slots.at[w], device)
            for device, peer in at.width_peers
        ]

    arrive = spread(tok, r["xa"])
    arrive += [links.send(vl, r["vg"].at[w], device) for device, _ in at.width_peers]
    r["vg"][w] = vl[...]

    class Weight:
        def __init__(self, full, start=True):
            own_block, next_block = full.at[block_of(w)], full.at[block_of(at.wy)]
            self.far = links.plan(own_block, own_block, at.far)
            self.core = links.plan(own_block, own_block, at.core)
            self.other = links.plan(next_block, next_block, at.core)
            if start:
                self.start()

        def start(self):
            self.far.start()
            self.core.start()

        def forward(self):
            self.far.wait_recv()
            self.other.start()

        def ready(self):
            self.core.wait_recv()
            self.other.wait_recv()

    loads[0].wait()
    r["wkv"][block_of(w), :] = interleave(r["wa_raw"][1], r["wa_raw"][2])
    weight_kv = Weight(r["wkv"])
    r["wq"][block_of(w), :] = r["wa_raw"][0]
    weight_q = Weight(r["wq"])
    loads[1].wait()
    r["wpt"][block_of(w), :] = r["wp_raw"][...].T
    weight_p = Weight(r["wpt"])

    loads[4].wait()
    for copy in arrive:
        copy.wait_recv()
    vec[...] = jnp.concatenate([r["vg"][i] for i in range(4)], axis=1)
    r["x"][...] = jnp.concatenate([r["xa"][i] for i in range(4)], axis=1)
    unit, _ = norm_stats(r["x"][...].astype(F32))
    x1, kv, q = r["x1"], r["kv"], r["q"]
    x1[own, :] = (unit * vec[0:1, :] + vec[2:3, :]).astype(BF16)
    gather = GatherZ(links, at, x1.at[own], x1)
    loads[2].wait()
    r["wt"][block_of(w), :] = r["wo_raw"][...].T
    loads[3].wait()
    weight_kv.forward()
    weight_kv.ready()
    value_bias = interleave(jnp.zeros((1, PART), F32), bqv[1:2, :])

    def key_block(c, who):
        return kv.at[rows_of((c * 4 + sub_block(c, who)) * ROWS)]

    shares, passed = [], []
    order = [at.chunk(k) for k in (0, 1, 3, 2)]
    for i, c in enumerate(order):
        if i == 1:
            gather.neighbours()
        if i == 3:
            gather.rest()
        key_block(c, w)[...] = (nn(x1[rows_of(c * ROWS), :], r["wkv"][...]) + value_bias).astype(BF16)
        shares.append(links.send(key_block(c, w), key_block(c, w), at.near))
        shares.append(links.send(key_block(c, w), key_block(c, w), at.core))
    weight_t = Weight(r["wt"])
    weight_f = Weight(r["wf"])
    weight_q.forward()
    weight_p.forward()
    weight_q.ready()
    queries = (nn(x1[...], r["wq"][...]) + bqv[0:1, :]).astype(BF16).astype(F32) * HS**-0.5
    q[...] = interleave(queries.astype(BF16), jnp.zeros((QUARTER, PART), BF16))
    for i, c in enumerate(order):
        shares[2 * i].wait_recv()
        passed.append(links.send(key_block(c, at.wy), key_block(c, at.wy), at.core))
    arrive_d = spread(dout, r["da"])
    for i in range(4):
        shares[2 * i + 1].wait_recv()
        passed[i].wait_recv()

    kvt, att, lse, d_all = r["kvt"], r["att"], r["lse"], r["d_all"]

    @pl.loop(0, HEADS)
    def _(head):
        kvt[tile_of(head, 128), :] = kv[:, tile_of(head, 128)].T

    weight_p.ready()
    loads[5].wait()
    for copy in arrive_d:
        copy.wait_recv()
    d_all[own, :] = jnp.concatenate([r["da"][i] for i in range(4)], axis=1)
    gather_d = GatherZ(links, at, d_all.at[own], d_all)
    stage = r["stage"]
    sum_p = SumZ(links, at, stage, r["parts"], r["over"])

    def attend_chunk(j):
        keys = (j + 1) * QUARTER
        shift = sub_block(j, w) * ROWS

        @pl.loop(0, HEADS)
        def _(head):
            tile = tile_of(head, 128)
            scores = visible_scores(nt(kv[0:keys, tile], q[j * ROWS : (j + 1) * ROWS, tile]), j, shift)
            peak = jnp.max(scores, axis=0, keepdims=True)
            weights = jnp.exp(scores - peak)
            total = column_sum(weights)
            probs = (weights * (1.0 / total)).astype(BF16)
            r["att_t"][tile_of(head, HS), :] = nn(kvt[tile, 0:keys], probs)[HS:, :]
            lse[pl.ds(j * 8 + head, 1), :] = peak + jnp.log(total)

    @pl.loop(0, 4)
    def _(i):
        j = at.chunk(jnp.where(i == 0, 2, jnp.where(i == 3, 0, 2 * i - 1)))
        for case in range(4):
            pl.when(j == case)(functools.partial(attend_chunk, case))
        attended = r["att_t"][...].T.astype(BF16)
        att[rows_of(j * ROWS), :] = attended
        stage[j] = nt(attended, r["wpt"][...]).astype(BF16)
        pl.when(i == 0)(sum_p.send_across)
        pl.when(i == 0)(gather_d.neighbours)
        pl.when(i == 1)(sum_p.send_ahead)
        pl.when(i == 2)(sum_p.send_behind)

    gather_d.rest()
    weight_t.forward()
    weight_f.forward()
    middle = r["x"][...].astype(F32) + vec[4:5, :] + sum_p.result()
    r["middle"][...] = middle
    unit, _ = norm_stats(middle)
    x2, hid, gp = r["x2"], r["hid"], r["gp"]
    x2[own, :] = (unit * vec[1:2, :] + vec[3:4, :]).astype(BF16)

    gather = GatherZ(links, at, x2.at[own], x2)
    weight_t.ready()
    weight_f.ready()
    wf, wt = r["wf"], r["wt"]
    hidden_grad = r["dkv"]
    stage_g, parts_g = r["stage_g"], r["parts_g"]

    @pl.loop(0, TILES)
    def _(t):
        grad = nn(d_all[...], wt[:, tile_of(t, 256)])
        hidden_grad[rows_of(t // 2 * QUARTER, QUARTER), tile_of(t - t // 2 * 2, 256)] = grad

    moves = []
    for i, c in enumerate(order):
        if i == 1:
            gather.neighbours()
        if i == 3:
            gather.rest()
        rows = rows_of(c * ROWS)

        @pl.loop(0, TILES)
        def _(t):
            tile = tile_of(t, 256)
            u = nn(x2[rows, :], wf[:, tile]) + r["bf"][0:1, tile]
            square = u * u
            th = jnp.tanh(GELU_COEF * (u + 0.044715 * square * u))
            hid[rows, tile] = (0.5 * u * (1.0 + th)).astype(BF16)
            slope = 0.5 * (1.0 + th) + 0.5 * u * (1.0 - th * th) * (GELU_COEF * (1.0 + 0.134145 * square))
            grad = hidden_grad[rows_of(t // 2 * QUARTER + c * ROWS), tile_of(t - t // 2 * 2, 256)]
            gp[rows, tile] = (grad * slope).astype(BF16)

        @pl.loop(0, TILES)
        def _(t):
            stage_g[c, :, tile_of(t, 256)] = nt(gp[rows, :], wf[tile_of(t, 256), :]).astype(BF16)

        if i:
            moves.append(links.send(stage_g.at[c], parts_g.at[i - 1], at.along_z((0, 1, 3, 2)[i])))

    sum_p.sent()
    sum_b = SumZ(links, at, stage, r["parts_b"], r["over_b"])

    @pl.loop(0, TILES)
    def _(t):
        product = nt(hid[...], wt[tile_of(t, 256), :]).astype(BF16)
        for c in range(4):
            stage[c, :, tile_of(t, 256)] = product[c * ROWS : (c + 1) * ROWS]

    sum_b.send_across()
    grad_f, grad_t = r["grad_f"], r["grad_t"]

    @pl.loop(0, TILES)
    def _(t):
        grad_t[tile_of(t, 256), :] = tn(d_all[:, tile_of(t, 256)], hid[...]).astype(BF16)

    def gradient_sum(tag, grad, columns, final):
        return GradientSum(
            links, at, grad, columns, r["pair_" + tag], r["strips_" + tag], r["cross_" + tag], final
        )

    whole = slice(0, D)
    sum_t = gradient_sum("t", grad_t, whole, fin_t)
    sum_t.send_core()

    @pl.loop(0, TILES)
    def _(t):
        grad_f[tile_of(t, 256), :] = tn(x2[:, tile_of(t, 256)], gp[...]).astype(BF16)

    sum_f = gradient_sum("f", grad_f, whole, fin_f)
    sum_f.send_core()
    sums = r["sums"]
    sums[8:9, :] = column_sum(gp[...].astype(F32))
    unit, scale = norm_stats(r["middle"][...])
    grad = d_all[own, :].astype(F32)
    grad_normed = stage_g[h].astype(F32)
    for i in range(3):
        moves[i].wait_recv()
        grad_normed = grad_normed + parts_g[i].astype(F32)
    grad_middle = grad + norm_gradient(grad_normed, unit, scale, vec[1:2, :])
    r["gm"][...] = grad_middle
    branch = grad_middle.astype(BF16)
    g_all = r["g_all"]
    g_all[own, :] = branch
    gather = GatherZ(links, at, g_all.at[own], g_all)
    sums[1:2, :] = column_sum(grad_normed * unit)
    sums[3:4, :] = column_sum(grad_normed)
    sums[4:5, :] = column_sum(grad)
    sums[5:6, :] = column_sum(branch.astype(F32))
    sum_b.send_ahead()
    sum_b.send_behind()
    sum_t.send_x()
    sum_f.send_x()

    def send_rows(result, target):
        result = result.astype(BF16)
        back = r["back"]
        for part in range(4):
            back[part] = result[:, part * PART : (part + 1) * PART]
        keep = pltpu.make_async_copy(back.at[w], target.at[mine], local.at[6])
        keep.start()
        copies = [links.send(back.at[peer], target.at[mine], device) for device, peer in at.width_peers]
        keep.wait()
        return copies

    dkv, go, dq = r["dkv"], r["go"], r["dq"]
    dkv[...] = jnp.zeros(dkv.shape, F32)
    zeros = jnp.zeros((ROWS, PART), BF16)

    def back_chunk(j):
        keys = (j + 1) * QUARTER
        shift = sub_block(j, w) * ROWS
        rows = slice(j * ROWS, (j + 1) * ROWS)

        @pl.loop(0, HEADS)
        def _(head):
            tile = tile_of(head, 128)
            query, grad = q[rows, tile], go[:, tile]
            scores = visible_scores(nt(kv[0:keys, tile], query), j, shift)
            probs = jnp.exp(scores - lse[pl.ds(j * 8 + head, 1), :])
            grad_probs = nt(kv[0:keys, tile], grad)
            inner = column_sum(grad_probs * probs)
            grad_scores = (probs * (grad_probs - inner)).astype(BF16)
            both = jnp.concatenate([grad_scores, probs.astype(BF16)], axis=1)
            dkv[0:keys, tile] += nn(both, jnp.concatenate([query, grad], axis=0))
            r["att_t"][tile_of(head, HS), :] = nn(kvt[tile, 0:keys], grad_scores)[:HS, :] * HS**-0.5

    @pl.loop(0, 4)
    def _(i):
        pl.when(i == 1)(gather.neighbours)
        pl.when(i == 3)(gather.rest)
        c = at.chunk(jnp.where(i == 2, 3, jnp.where(i == 3, 2, i)))
        rows = rows_of(c * ROWS)
        go[...] = interleave(zeros, nn(g_all[rows, :], r["wpt"][...]).astype(BF16))
        for case in range(4):
            pl.when(c == case)(functools.partial(back_chunk, case))
        dq[rows, :] = r["att_t"][...].T.astype(BF16)

    def piece(who, j):
        return dkv[rows_of((j * 4 + sub_block(j, who)) * ROWS), :]

    take, take_y, gkv = r["take"], r["take_y"], r["gkv"]
    halves = (slice(0, PAIR), slice(PAIR, D))
    for copy in moves:
        copy.wait_send()
    quarters = [slice(j * ROWS, (j + 1) * ROWS) for j in range(4)]
    for j in range(4):
        stage_g[j, :, halves[1]] = piece(at.wyc, j).astype(BF16)
    first = links.send(stage_g.at[:, :, halves[1]], take.at[1], at.core)
    for j in range(4):
        stage_g[j, :, halves[0]] = piece(at.wc, j).astype(BF16)
    second = links.send(stage_g.at[:, :, halves[0]], take.at[0], at.core)
    first.wait_recv()
    for j in range(4):
        gkv[quarters[j], :] = (piece(at.wy, j) + take[1, j].astype(F32)).astype(BF16)
    third = links.send(gkv, take_y, at.near)

    @pl.loop(0, TILES)
    def _(t):
        tile = tile_of(t, 256)
        pieces = [tn(x1[:, tile], dq[...]).astype(BF16), tn(g_all[:, tile], att[...]).astype(BF16)]
        grad_t[tile, PAIR:] = jnp.concatenate(pieces, axis=1)

    sum_q = gradient_sum("q", grad_t, slice(PAIR, D), fin_q)
    sum_q.send_core()
    result = r["middle"][...] + vec[5:6, :] + sum_b.result()
    returns = send_rows(result, bo)
    sums[9:10, 0:PART] = column_sum(dq[...].astype(F32))
    second.wait_recv()
    third.wait()
    for j in range(4):
        total = piece(w, j) + take[0, j].astype(F32) + take_y[quarters[j], :].astype(F32)
        gkv[quarters[j], :] = total.astype(BF16)

    sum_b.sent()
    sum_l = SumZ(links, at, stage, r["parts"], r["over"])

    def first_partial(k):
        c = at.chunk(k)
        rows = rows_of(c * ROWS)
        stage[c] = (nt(dq[rows, :], r["wq"][...]) + nt(gkv[rows, :], r["wkv"][...])).astype(BF16)

    first_partial(2)
    sum_l.send_across()
    first_partial(1)
    first_partial(3)
    sum_l.send_ahead()
    sum_l.send_behind()

    @pl.loop(0, TILES)
    def _(t):
        tile = tile_of(t, 256)
        grad_t[tile, 0:PAIR] = tn(x1[:, tile], gkv[...]).astype(BF16)

    sum_k = gradient_sum("k", grad_t, slice(0, PAIR), fin_k)
    sum_k.send_core()
    first_partial(0)
    sum_q.send_x()
    sum_t.send_y()
    sum_f.send_y()
    sum_k.send_x()
    grad_values = column_sum(gkv[...].astype(F32))
    for head in range(HEADS):
        sums[9:10, PART + head * HS : PART + (head + 1) * HS] = grad_values[:, head * 128 + HS : (head + 1) * 128]
    sums[9:10, PAIR:] = jnp.zeros((1, PAIR), F32)
    sums[10:16, :] = jnp.zeros((6, D), F32)
    sums[6:8, :] = jnp.zeros((2, D), F32)
    grad_normed = sum_l.result()
    unit, scale = norm_stats(r["x"][...].astype(F32))
    sums[0:1, :] = column_sum(grad_normed * unit)
    sums[2:3, :] = column_sum(grad_normed)
    over_z = [links.send(sums.at[0:8], r["sums_z"].at[k - 1], at.along_z(k)) for k in (1, 2, 3)]
    over_w = [links.send(sums.at[8:16], r["take_v"].at[i], at.width_peers[i][0]) for i in range(3)]
    result = r["gm"][...] + norm_gradient(grad_normed, unit, scale, vec[0:1, :])
    for copy in returns:
        copy.wait()
    returns = send_rows(result, dt)

    keep = []

    def send_back(total):
        strip = total.send_back()
        copy = pltpu.make_async_copy(total.total[0], strip, local.at[7 + len(keep)])
        copy.start()
        keep.append(copy)

    send_back(sum_t)
    send_back(sum_f)
    for copy in over_z + over_w:
        copy.wait()
    normed = sums[0:8, :] + r["sums_z"][0] + r["sums_z"][1] + r["sums_z"][2]
    for part in range(4):
        r["sums_w"][part] = normed[:, part * PART : (part + 1) * PART]
    over_w = [links.send(r["sums_w"].at[peer], r["take_w"].at[i], at.width_peers[i][0]) for i, (_, peer) in enumerate(at.width_peers)]
    biases = sums[8:10, :] + r["take_v"][0, 0:2] + r["take_v"][1, 0:2] + r["take_v"][2, 0:2]
    sum_q.send_y()
    for copy in over_w:
        copy.wait()
    sums_d = r["sums_d"]
    normed = r["sums_w"][w] + r["take_w"][0] + r["take_w"][1] + r["take_w"][2]
    sums_d[...] = jnp.zeros((8, D), F32)
    for i in range(6):
        sums_d[i // 3 : i // 3 + 1, (i % 3) * 384 : (i % 3) * 384 + PART] = normed[i : i + 1, :]
    sums_d[2:4, :] = biases
    over_x = [links.send(sums_d, r["sums_x"].at[k - 1], at.along_x(k)) for k in (1, 2, 3)]
    sum_k.send_y()
    for copy in over_x:
        copy.wait()
    sums_d[...] = sums_d[...] + r["sums_x"][0] + r["sums_x"][1] + r["sums_x"][2]
    over_o = links.send(sums_d, r["sums_o"], at.opposite)
    send_back(sum_q)
    send_back(sum_k)
    over_o.wait()
    fin_v[...] = sums_d[...] + r["sums_o"][...]
    for copy in keep:
        copy.wait()
    for total in (sum_t, sum_f, sum_q, sum_k):
        total.finish()
    for copy in returns:
        copy.wait()
    for copy in links.copies:
        copy.wait_send()


def block(*inputs):
    return pl.pallas_call(
        block_kernel,
        name="block",
        out_shape=(
            jax.ShapeDtypeStruct((4, ROWS, PART), BF16),
            jax.ShapeDtypeStruct((4, ROWS, PART), BF16),
            jax.ShapeDtypeStruct((PART, D), BF16),
            jax.ShapeDtypeStruct((PART, D), BF16),
            jax.ShapeDtypeStruct((PART, PAIR), BF16),
            jax.ShapeDtypeStruct((PART, PAIR), BF16),
            jax.ShapeDtypeStruct((8, D), F32),
        ),
        in_specs=[ANY, ANY, VMEM, VMEM, VMEM, VMEM, ANY, VMEM, ANY, ANY, VMEM, ANY],
        out_specs=(ANY, ANY, ANY, ANY, ANY, ANY, VMEM),
        scratch_shapes=[pltpu.VMEM(shape, kind) for shape, kind in SCRATCH.values()]
        + [pltpu.SemaphoreType.DMA((COPIES,)), pltpu.SemaphoreType.DMA((COPIES,)), pltpu.SemaphoreType.DMA((12,))],
        compiler_params=pltpu.CompilerParams(collective_id=1, has_side_effects=True, vmem_limit_bytes=64 * 2**20),
    )(*inputs)


def finish_kernel(bo, dt, f, t, qp, kv, v, out, d_tok, gain, shift, d_wa, d_bqv, d_wp, d_bp, d_wf, d_bf, d_wo, d_bo):
    for part in range(4):
        out[part * ROWS : (part + 1) * ROWS, :] = bo[part]
        d_tok[part * ROWS : (part + 1) * ROWS, :] = dt[part]
    d_wf[...] = f[...].astype(F32)
    d_wo[...] = t[...].astype(F32).T
    d_wa[0] = qp[:, :PART].astype(F32)
    d_wp[...] = qp[:, PART:].astype(F32).T
    both = kv[...].astype(F32)
    d_wa[1] = jnp.concatenate([both[:, head * 128 : head * 128 + HS] for head in range(HEADS)], axis=1)
    d_wa[2] = jnp.concatenate([both[:, head * 128 + HS : (head + 1) * 128] for head in range(HEADS)], axis=1)
    rows = [v[i // 3 : i // 3 + 1, (i % 3) * 384 : (i % 3) * 384 + PART] for i in range(6)]
    gain[0:1, :] = rows[0]
    gain[1:2, :] = rows[1]
    shift[0:1, :] = rows[2]
    shift[1:2, :] = rows[3]
    d_bo[...] = rows[4].reshape(PART)
    d_bp[...] = rows[5].reshape(PART)
    d_bf[...] = v[2:3, :].reshape(D)
    d_bqv[0:1, :] = v[3:4, 0:PART]
    d_bqv[1:2, :] = v[3:4, PART:PAIR]


def finish(*inputs):
    shapes = [
        ((QUARTER, PART), BF16),
        ((QUARTER, PART), BF16),
        ((2, PART), F32),
        ((2, PART), F32),
        ((3, PART, PART), F32),
        ((2, PART), F32),
        ((PART, PART), F32),
        ((PART,), F32),
        ((PART, D), F32),
        ((D,), F32),
        ((D, PART), F32),
        ((PART,), F32),
    ]
    return pl.pallas_call(
        finish_kernel,
        name="finish",
        out_shape=[jax.ShapeDtypeStruct(shape, kind) for shape, kind in shapes],
        in_specs=[VMEM] * 7,
        out_specs=[VMEM] * 12,
        compiler_params=pltpu.CompilerParams(vmem_limit_bytes=48 * 2**20),
    )(*inputs)


def shards(tokens, ln_gain, ln_bias, w_attn, b_qv, w_proj, b_proj, w_fc, b_fc, w_out, b_out, d_out):
    parts = block(tokens, d_out, ln_gain, ln_bias, b_proj, b_out, w_attn, b_qv, w_proj, w_fc, b_fc, w_out)
    return tuple(finish(*parts))


def solution(mesh):
    in_specs = (
        P(("dp", "heads"), "width"),
        P(None, "width"),
        P(None, "width"),
        P(None, "width", "heads"),
        P(None, "heads"),
        P("heads", "width"),
        P("width"),
        P("width", "heads"),
        P("heads"),
        P("heads", "width"),
        P("width"),
        P(("dp", "heads"), "width"),
    )
    out_specs = (
        P(("dp", "heads"), "width"),
        P(("dp", "heads"), "width"),
        P(None, "width"),
        P(None, "width"),
        P(None, "width", "heads"),
        P(None, "heads"),
        P("heads", "width"),
        P("width"),
        P("width", "heads"),
        P("heads"),
        P("heads", "width"),
        P("width"),
    )
    return jax.shard_map(shards, mesh=mesh, in_specs=in_specs, out_specs=out_specs, check_vma=False)
```

```python
import functools

import jax
import jax.numpy as jnp
from jax import lax
from jax.experimental import pallas as pl
from jax.experimental.pallas import tpu as pltpu
from jax.sharding import PartitionSpec as P

F32, BF16 = jnp.float32, jnp.bfloat16
D, HS, ROWS, PART, QUARTER, HEADS = 1280, 64, 128, 320, 512, 5
PAIR = 2 * PART
STRIP = PART // 4
HALF = ROWS // 2
EPSILON = 1e-05
GELU_COEF = 0.7978845608028654
MASKED = -1e30
VMEM = pl.BlockSpec(memory_space=pltpu.VMEM)
ANY = pl.BlockSpec(memory_space=pl.ANY)
TILES = D // 256


def nn(a, b):
    return jnp.dot(a, b, preferred_element_type=F32)


def nt(a, b):
    return lax.dot_general(a, b, (((1,), (1,)), ((), ())), preferred_element_type=F32)


def tn(a, b):
    return lax.dot_general(a, b, (((0,), (0,)), ((), ())), preferred_element_type=F32)


def rows_of(start, size=ROWS):
    return pl.ds(pl.multiple_of(start, size), size)


def block_of(who):
    return pl.ds(pl.multiple_of(who * PART, 64), PART)


def tile_of(i, size):
    return pl.ds(pl.multiple_of(i * size, size), size)


def sub_block(quarter, w):
    return w + lax.rem(quarter, 2) * (3 - 2 * w)


class Place:
    def __init__(self):
        self.dp, self.w, self.h = (lax.axis_index(n) for n in ("dp", "width", "heads"))
        self.x = lax.rem(self.dp, 4)
        self.wc = self.w + 1 - 2 * lax.rem(self.w, 2)
        self.wy = lax.rem(self.w + 2, 4)
        self.wyc = lax.rem(self.wc + 2, 4)
        across = lax.rem(self.dp + 4, 8)
        self.core = (self.dp, self.wc, self.h)
        self.near = (self.dp, self.wy, self.h)
        self.near_core = (self.dp, self.wyc, self.h)
        self.far = (across, self.wy, self.h)
        self.opposite = (across, self.w, self.h)
        self.width_peers = ((self.near, self.wy), (self.near_core, self.wyc), (self.core, self.wc))

        beyond = lax.rem(self.dp + 4, 8) - self.x
        self.dp_peers = [self.along_x(k) for k in (1, 2, 3)] + [self.opposite]
        self.dp_peers += [(beyond + lax.rem(self.x + k, 4), self.w, self.h) for k in (1, 2, 3)]

    def along_z(self, k):
        return (self.dp, self.w, lax.rem(self.h + k, 4))

    def along_x(self, k):
        return (self.dp - self.x + lax.rem(self.x + k, 4), self.w, self.h)

    def chunk(self, k):
        return lax.rem(self.h + k, 4)


def greet(devices):
    barrier = pltpu.get_barrier_semaphore()
    for device in devices:
        pl.semaphore_signal(barrier, inc=1, device_id=device, device_id_type=pl.DeviceIdType.MESH)
    pl.semaphore_wait(barrier, len(devices))


class Move:
    def __init__(self, copy):
        self.copy, self.left = copy, False
        self.start, self.wait_recv = copy.start, copy.wait_recv

    def wait_send(self):
        if not self.left:
            self.copy.wait_send()
        self.left = True

    def wait(self):
        self.wait_recv()
        self.wait_send()


class Links:
    def __init__(self, sent, landed):
        self.sent, self.landed, self.copies = sent, landed, []

    def plan(self, source, target, device):
        i = len(self.copies)
        copy = pltpu.make_async_remote_copy(
            src_ref=source,
            dst_ref=target,
            send_sem=self.sent.at[i],
            recv_sem=self.landed.at[i],
            device_id=device,
            device_id_type=pl.DeviceIdType.MESH,
        )
        self.copies.append(Move(copy))
        return self.copies[-1]

    def send(self, source, target, device):
        copy = self.plan(source, target, device)
        copy.start()
        return copy


class GatherZ:
    def __init__(self, links, at, rows):
        right, left = at.along_z(1), at.along_z(3)
        own, ahead, behind = (rows.at[pl.ds(i * ROWS, ROWS)] for i in range(3))
        self.right = links.send(own, behind, right)
        self.left = links.send(own, ahead, left)
        self.low = links.plan(
            rows.at[pl.ds(2 * ROWS, HALF)], rows.at[pl.ds(3 * ROWS, HALF)], right
        )
        self.high = links.plan(
            rows.at[pl.ds(ROWS + HALF, HALF)], rows.at[pl.ds(3 * ROWS + HALF, HALF)], left
        )

    def neighbours(self):
        self.left.wait_recv()
        self.high.start()
        self.right.wait_recv()
        self.low.start()

    def rest(self):
        self.low.wait_recv()
        self.high.wait_recv()


class SumZ:
    def __init__(self, links, at, stage, parts, over):
        self.stage, self.parts, self.over = stage, parts, over
        right, left = at.along_z(1), at.along_z(3)
        top, bottom = pl.ds(0, HALF), pl.ds(HALF, HALF)
        self.far_right = links.plan(stage.at[3, top], over.at[0], right)
        self.far_left = links.plan(stage.at[3, bottom], over.at[1], left)
        self.right_bottom = links.plan(stage.at[1, bottom], parts.at[0, bottom], right)
        self.right_top = links.plan(stage.at[1, top], parts.at[0, top], right)
        self.left_top = links.plan(stage.at[2, top], parts.at[1, top], left)
        self.left_bottom = links.plan(stage.at[2, bottom], parts.at[1, bottom], left)

    def sent(self):
        for copy in (self.far_right, self.far_left, self.right_bottom, self.right_top, self.left_top, self.left_bottom):
            copy.wait_send()

    def send_across(self):
        self.far_right.start()
        self.far_left.start()

    def send_near(self):
        self.right_bottom.start()
        self.left_top.start()

    def join_ahead(self):
        self.far_right.wait_recv()
        joined = self.stage[1, 0:HALF, :].astype(F32) + self.over[0].astype(F32)
        self.stage[1, 0:HALF, :] = joined.astype(BF16)
        self.right_top.start()

    def join_behind(self):
        self.far_left.wait_recv()
        joined = self.stage[2, HALF:, :].astype(F32) + self.over[1].astype(F32)
        self.stage[2, HALF:, :] = joined.astype(BF16)
        self.left_bottom.start()

    def result(self):
        for copy in (self.right_bottom, self.right_top, self.left_top, self.left_bottom):
            copy.wait_recv()
        return self.stage[0].astype(F32) + self.parts[0].astype(F32) + self.parts[1].astype(F32)


class GradientSum:
    def __init__(self, links, at, grad, columns, pair, strips, cross, final):
        self.links, self.at, self.grad, self.columns = links, at, grad, columns
        self.pair, self.strips, self.cross, self.final = pair, strips, cross, final
        self.strip = rows_of(at.x * STRIP, STRIP)
        self.total = [pair.at[0, self.strip], pair.at[1, self.strip]]

    def mine(self, who):
        return self.grad.at[block_of(who), self.columns]

    def send_core(self):
        at, links = self.at, self.links
        self.core = [
            links.send(self.mine(at.wc), self.pair.at[0], at.core),
            links.send(self.mine(at.wyc), self.pair.at[1], at.core),
        ]

    def sent_core(self):
        for copy in self.core:
            copy.wait_send()

    def send_x(self):
        at, links = self.at, self.links
        for i, who in ((0, at.w), (1, at.wy)):
            self.core[i].wait_recv()
            self.pair[i] = (self.pair[i].astype(F32) + self.mine(who)[...].astype(F32)).astype(BF16)
        self.along = [
            links.send(
                self.pair.at[:, rows_of(lax.rem(at.x + k, 4) * STRIP, STRIP)], self.strips.at[k - 1], at.along_x(k)
            )
            for k in (2, 1, 3)
        ]

    def send_y(self):
        at, links = self.at, self.links
        for copy in self.along:
            copy.wait()
        for i in range(2):
            joined = self.total[i][...].astype(F32)
            for k in range(3):
                joined = joined + self.strips[k, i].astype(F32)
            self.total[i][...] = joined.astype(BF16)
        self.over = [
            links.send(self.total[1], self.cross.at[0], at.near),
            links.send(self.total[1], self.cross.at[1], at.far),
            links.send(self.total[0], self.cross.at[2], at.opposite),
        ]

    def send_back(self):
        at, links = self.at, self.links
        for copy in self.over:
            copy.wait()
        joined = self.total[0][...].astype(F32)
        for k in range(3):
            joined = joined + self.cross[k].astype(F32)
        self.total[0][...] = joined.astype(BF16)
        strip = self.final.at[self.strip]
        self.back = [links.send(self.total[0], strip, at.along_x(k)) for k in (2, 1, 3)]
        return strip

    def finish(self):
        for copy in self.back:
            copy.wait()


class GradientSumY:
    def __init__(self, links, at, grad, pair, cross, strips, half, final):
        self.links, self.at, self.grad = links, at, grad
        self.pair, self.cross, self.strips, self.half, self.final = pair, cross, strips, half, final
        part = at.dp // 4
        self.kept = pl.ds(pl.multiple_of(part * PAIR, PAIR), PAIR)
        self.given = pl.ds(pl.multiple_of((1 - part) * PAIR, PAIR), PAIR)
        self.strip = rows_of(at.x * STRIP, STRIP)

    def mine(self, who):
        return self.grad.at[block_of(who)]

    def send_core(self):
        at, links = self.at, self.links
        self.core = [
            links.send(self.mine(at.wc), self.pair.at[0], at.core),
            links.send(self.mine(at.wyc), self.pair.at[1], at.core),
        ]

    def send_y(self):
        at, links = self.at, self.links
        for i, who in ((0, at.w), (1, at.wy)):
            self.core[i].wait_recv()
            self.pair[i] = (self.pair[i].astype(F32) + self.mine(who)[...].astype(F32)).astype(BF16)
        self.over = [
            links.send(self.pair.at[1, :, self.kept], self.cross.at[0], at.near),
            links.send(self.pair.at[1, :, self.given], self.cross.at[1], at.far),
            links.send(self.pair.at[0, :, self.given], self.cross.at[2], at.opposite),
        ]

    def send_x(self):
        at, links = self.at, self.links
        joined = self.pair[0, :, self.kept].astype(F32)
        for k in range(3):
            self.over[k].wait_recv()
            joined = joined + self.cross[k].astype(F32)
        self.pair[0, :, self.kept] = joined.astype(BF16)
        self.along = [
            links.send(
                self.pair.at[0, rows_of(lax.rem(at.x + k, 4) * STRIP, STRIP), self.kept],
                self.strips.at[k - 1],
                at.along_x(k),
            )
            for k in (2, 1, 3)
        ]

    def send_back(self):
        at, links = self.at, self.links
        joined = self.pair[0, self.strip, self.kept].astype(F32)
        for copy in self.along:
            copy.wait_recv()
        for k in range(3):
            joined = joined + self.strips[k].astype(F32)
        self.half[self.strip, :] = joined.astype(BF16)
        place = self.half.at[self.strip]
        self.back = [links.send(place, place, at.along_x(k)) for k in (2, 1, 3)]

    def send_opposite(self, sem):
        for copy in self.back:
            copy.wait_recv()
        place = self.final.at[:, self.kept]
        self.last = self.links.send(self.half, place, self.at.opposite)
        keep = pltpu.make_async_copy(self.half, place, sem)
        keep.start()
        return keep

    def finish(self):
        self.last.wait_recv()


def norm_stats(values):
    mean = jnp.mean(values, axis=1, keepdims=True)
    centred = values - mean
    scale = lax.rsqrt(jnp.mean(centred * centred, axis=1, keepdims=True) + EPSILON)
    return centred * scale, scale


def norm_gradient(grad, unit, scale, gain):
    scaled = grad * gain
    mean = jnp.mean(scaled, axis=1, keepdims=True)
    along = jnp.mean(scaled * unit, axis=1, keepdims=True)
    return scale * (scaled - mean - unit * along)


def interleave(first, second):
    pieces = []
    for head in range(HEADS):
        part = slice(head * HS, (head + 1) * HS)
        pieces += [first[:, part], second[:, part]]
    return jnp.concatenate(pieces, axis=1)


def mask_last(scores, quarter, shift):
    shape = (4, ROWS, ROWS)
    owner = lax.broadcasted_iota(jnp.int32, shape, 0)
    if quarter % 2:
        owner = 3 - owner
    key = owner * ROWS + lax.broadcasted_iota(jnp.int32, shape, 1)
    query = lax.broadcasted_iota(jnp.int32, shape, 2) + shift
    seen = (key <= query).reshape(QUARTER, ROWS)
    parts = [scores[:, i * ROWS : (i + 1) * ROWS] for i in range(scores.shape[1] // ROWS)]
    parts = [jnp.where(seen, part, MASKED) for part in parts]
    return parts[0] if len(parts) == 1 else jnp.concatenate(parts, axis=1)


def column_sum(values):
    return jnp.sum(values, axis=0, keepdims=True)


SCRATCH = dict(
    wkv=((D, PAIR), BF16),
    wq=((D, PART), BF16),
    wpt=((D, PART), BF16),
    wf=((D, D), BF16),
    wt=((D, D), BF16),
    wa_raw=((3, PART, PART), BF16),
    wp_raw=((PART, PART), BF16),
    xa=((D, ROWS), BF16),
    da=((D, ROWS), BF16),
    vl=((8, PART), F32),
    vg=((4, 8, PART), F32),
    vec=((8, D), F32),
    bf=((8, D), F32),
    x=((ROWS, D), BF16),
    x1=((QUARTER, D), BF16),
    q=((QUARTER, PAIR), BF16),
    kv=((4, 4, ROWS, PAIR), BF16),
    kvt=((PAIR, 2048), BF16),
    att=((QUARTER, PART), BF16),
    att_t=((4, PART, ROWS), F32),
    lse=((32, 128), F32),
    delta=((32, 128), F32),
    middle=((ROWS, D), F32),
    stage=((4, ROWS, D), BF16),
    parts=((2, ROWS, D), BF16),
    over=((2, HALF, D), BF16),
    d_all=((QUARTER, D), BF16),
    x2=((QUARTER, D), BF16),
    hidden_grad=((QUARTER, D), F32),
    hid=((QUARTER, D), BF16),
    gp=((QUARTER, D), BF16),
    stage_g=((4, ROWS, D), BF16),
    parts_g=((3, ROWS, D), BF16),
    parts_b=((2, ROWS, D), BF16),
    over_b=((2, HALF, D), BF16),
    gm=((ROWS, D), F32),
    grad_f=((D, D), BF16),
    grad_t=((D, D), BF16),
    pair_f=((2, PART, D), BF16),
    pair_t=((2, PART, D), BF16),
    pair_q=((2, PART, PAIR), BF16),
    pair_k=((2, PART, PAIR), BF16),
    strips_f=((3, STRIP, PAIR), BF16),
    half_f=((PART, PAIR), BF16),
    strips_t=((3, 2, STRIP, D), BF16),
    strips_q=((3, 2, STRIP, PAIR), BF16),
    strips_k=((3, 2, STRIP, PAIR), BF16),
    cross_f=((3, PART, PAIR), BF16),
    cross_t=((3, STRIP, D), BF16),
    cross_q=((3, STRIP, PAIR), BF16),
    cross_k=((3, STRIP, PAIR), BF16),
    g_all=((QUARTER, D), BF16),
    go=((QUARTER, PAIR), BF16),
    dkv=((4, 4, ROWS, PAIR), BF16),
    take=((2, 4, ROWS, PAIR), BF16),
    take_y=((4, ROWS, PAIR), BF16),
    dq=((QUARTER, PART), BF16),
    gkv=((QUARTER, PAIR), BF16),
    sums=((16, D), F32),
    sums_z=((3, 8, D), F32),
    sums_w=((4, 8, PART), F32),
    take_w=((3, 8, PART), F32),
    take_v=((3, 8, D), F32),
    sums_d=((8, D), F32),
    sums_x=((7, 8, D), F32),
)
COPIES = 176


def block_kernel(*refs):
    names = ("tok", "dout", "gain", "shift", "b_proj", "b_out", "wa_in", "bqv", "wp_in", "wf_in", "b_fc", "wo_in")
    names += ("bo", "dt", "fin_f", "fin_t", "fin_q", "fin_k", "fin_v")
    names += tuple(SCRATCH) + ("sent", "landed", "local")
    r = dict(zip(names, refs))
    (tok, dout, gain, shift, b_proj, b_out, wa_in, bqv, wp_in, wf_in, b_fc, wo_in) = refs[:12]
    (bo, dt, fin_f, fin_t, fin_q, fin_k, fin_v) = refs[12:19]
    at = Place()
    w, h = at.w, at.h
    links = Links(r["sent"], r["landed"])
    local = r["local"]
    mine = sub_block(h, w)
    vec = r["vec"]

    wf, wt = r["wf"], r["wt"]
    loads = [
        pltpu.make_async_copy(wa_in, r["wa_raw"], local.at[0]),
        pltpu.make_async_copy(wp_in, r["wp_raw"], local.at[1]),
        pltpu.make_async_copy(wo_in, wt.at[block_of(w)], local.at[2]),
        pltpu.make_async_copy(wf_in, wf.at[block_of(w)], local.at[3]),
        pltpu.make_async_copy(tok.at[:, rows_of(mine * ROWS)], r["xa"].at[block_of(w)], local.at[4]),
        pltpu.make_async_copy(dout.at[:, rows_of(mine * ROWS)], r["da"].at[block_of(w)], local.at[5]),
    ]
    for copy in loads:
        copy.start()
    vl = r["vl"]
    vl[0:2, :] = gain[...]
    vl[2:4, :] = shift[...]
    vl[4:5, :] = b_proj[...].reshape(1, PART)
    vl[5:6, :] = b_out[...].reshape(1, PART)
    vl[6:8, :] = jnp.zeros((2, PART), F32)
    r["bf"][0:1, :] = b_fc[...].reshape(1, D)
    greet(
        [at.core, at.near, at.near_core, at.far, at.opposite]
        + [at.along_z(k) for k in (1, 2, 3)]
        + [at.along_x(k) for k in (1, 2, 3)]
        + [device for device in at.dp_peers[4:]]
    )

    def spread(source, slots):
        return [
            links.send(source.at[:, rows_of(sub_block(h, peer) * ROWS)], slots.at[block_of(w)], device)
            for device, peer in at.width_peers
        ]

    arrive = spread(tok, r["xa"])
    arrive += [links.send(vl, r["vg"].at[w], device) for device, _ in at.width_peers]
    arrive_d = spread(dout, r["da"])
    r["vg"][w] = vl[...]

    class Weight:
        def __init__(self, full, device):
            own_block, next_block = full.at[block_of(w)], full.at[block_of(at.wy)]
            self.over = links.send(own_block, own_block, device)
            self.core = links.send(own_block, own_block, at.core)
            self.other = links.plan(next_block, next_block, at.core)

        def forward(self):
            self.over.wait_recv()
            self.other.start()

        def ready(self):
            self.core.wait_recv()
            self.other.wait_recv()

    loads[0].wait()
    r["wkv"][block_of(w), :] = interleave(r["wa_raw"][1], r["wa_raw"][2])
    weight_kv = Weight(r["wkv"], at.far)
    r["wq"][block_of(w), :] = r["wa_raw"][0]
    weight_q = Weight(r["wq"], at.far)
    loads[1].wait()
    r["wpt"][block_of(w), :] = r["wp_raw"][...].T
    loads[4].wait()
    for copy in arrive:
        copy.wait_recv()

    vec[...] = jnp.concatenate([r["vg"][i] for i in range(4)], axis=1)
    r["x"][...] = r["xa"][...].T
    unit, _ = norm_stats(r["x"][...].astype(F32))
    x1, kv, q = r["x1"], r["kv"], r["q"]
    x1[0:ROWS, :] = (unit * vec[0:1, :] + vec[2:3, :]).astype(BF16)
    gather = GatherZ(links, at, x1)
    value_bias = interleave(jnp.zeros((1, PART), F32), bqv[1:2, :])
    weight_kv.forward()
    weight_kv.ready()
    weight_p = Weight(r["wpt"], at.far)
    loads[2].wait()
    weight_t = Weight(wt, at.far)
    quarter = [at.chunk(k) for k in (0, 1, 3, 2)]
    shares, passed = [], []

    def key_rows(first, count):
        rows = (nn(x1[first * ROWS : (first + count) * ROWS, :], r["wkv"][...]) + value_bias).astype(BF16)
        for i in range(count):
            block = kv.at[quarter[first + i], w]
            block[...] = rows[i * ROWS : (i + 1) * ROWS, :]
            shares.append(links.send(block, block, at.near))
            shares.append(links.send(block, block, at.core))

    def pass_on(i):
        shares[2 * i].wait_recv()
        block = kv.at[quarter[i], at.wy]
        passed.append(links.send(block, block, at.core))

    key_rows(0, 1)
    gather.neighbours()
    key_rows(1, 2)
    weight_q.forward()
    pass_on(0)
    gather.rest()
    d_all = r["d_all"]
    loads[5].wait()
    for copy in arrive_d:
        copy.wait_recv()
    d_all[0:ROWS, :] = r["da"][...].T
    gather_d = GatherZ(links, at, d_all)
    key_rows(3, 1)
    weight_q.ready()
    queries = (nn(x1[...], r["wq"][...]) + bqv[0:1, :]).astype(BF16).astype(F32) * HS**-0.5
    q[...] = interleave(queries.astype(BF16), jnp.zeros((QUARTER, PART), BF16))
    weight_p.forward()
    for i in (1, 2, 3):
        pass_on(i)
    loads[3].wait()
    weight_f = Weight(wf, at.near)
    for i in range(4):
        shares[2 * i + 1].wait_recv()
        passed[i].wait_recv()

    kvt, att, att_t, lse = r["kvt"], r["att"], r["att_t"], r["lse"]

    def keys_of(j, lanes):
        return kv[j, :, :, lanes].reshape(QUARTER, lanes.stop - lanes.start)

    for j in range(4):
        for head in range(HEADS):
            tile = slice(head * 128, (head + 1) * 128)
            kvt[tile, j * QUARTER : (j + 1) * QUARTER] = keys_of(j, tile).T
    stage = r["stage"]
    sum_p = SumZ(links, at, stage, r["parts"], r["over"])

    def attend_chunk(j, slot):
        shift = sub_block(j, w) * ROWS
        apart = jnp.zeros((ROWS, 128), BF16)
        for first, count in ((0, 2), (2, 2), (4, 1)):
            lanes = slice(first * 128, (first + count) * 128)
            query = q[rows_of(slot * ROWS), lanes]
            if count == 2:
                top = jnp.concatenate([query[:, :128], apart], axis=1)
                query = jnp.concatenate([top, jnp.concatenate([apart, query[:, 128:]], axis=1)], axis=0)
            scores = [nt(keys_of(b, lanes), query) for b in range(j + 1)]
            scores[j] = mask_last(scores[j], j, shift)
            peak = functools.reduce(jnp.maximum, [jnp.max(s, axis=0, keepdims=True) for s in scores])
            total, result = 0.0, 0.0
            for b in range(j + 1):
                weights = jnp.exp(scores[b] - peak)
                total = total + column_sum(weights)
                result = result + nn(kvt[lanes, b * QUARTER : (b + 1) * QUARTER], weights.astype(BF16))
            inverse, log_total = 1.0 / total, peak + jnp.log(total)
            for i in range(count):
                head, part = first + i, slice(i * 128, (i + 1) * 128)
                values = result[i * 128 + HS : (i + 1) * 128, part]
                att_t[slot, head * HS : (head + 1) * HS, :] = values * inverse[:, part]
                lse[pl.ds(slot * 8 + head, 1), :] = log_total[:, part]

    gather_d.neighbours()
    weight_p.ready()

    @pl.loop(0, 4)
    def _(i):
        slot = jnp.where(i == 0, 3, jnp.where(i == 3, 0, i))
        j = at.chunk(jnp.where(slot == 3, 2, jnp.where(slot == 2, 3, slot)))
        for case in range(4):
            pl.when(j == case)(functools.partial(attend_chunk, case, slot))
        attended = att_t[slot].T.astype(BF16)
        att[rows_of(slot * ROWS), :] = attended
        stage[slot] = nt(attended, r["wpt"][...]).astype(BF16)
        pl.when(i == 0)(sum_p.send_across)
        pl.when(i == 1)(sum_p.right_bottom.start)
        pl.when(i == 1)(weight_t.forward)
        pl.when(i == 2)(sum_p.left_top.start)
        pl.when(i == 2)(sum_p.join_ahead)

    sum_p.join_behind()
    gather_d.rest()
    weight_t.ready()
    weight_f.forward()
    middle = r["x"][...].astype(F32) + vec[4:5, :] + sum_p.result()
    r["middle"][...] = middle
    unit, _ = norm_stats(middle)
    x2, hid, gp = r["x2"], r["hid"], r["gp"]
    x2[0:ROWS, :] = (unit * vec[1:2, :] + vec[3:4, :]).astype(BF16)

    gather = GatherZ(links, at, x2)
    hidden_grad = r["hidden_grad"]
    for t in range(TILES):
        tile = slice(t * 256, (t + 1) * 256)
        hidden_grad[:, tile] = nn(d_all[...], wt[:, tile])
    weight_f.ready()
    stage_g, parts_g = r["stage_g"], r["parts_g"]
    moves = []

    def feed(first, count):
        rows = slice(first * ROWS, (first + count) * ROWS)

        for t in range(TILES):
            tile = slice(t * 256, (t + 1) * 256)
            u = nn(x2[rows, :], wf[:, tile]) + r["bf"][0:1, tile]
            square = u * u
            th = jnp.tanh(GELU_COEF * (u + 0.044715 * square * u))
            hid[rows, tile] = (0.5 * u * (1.0 + th)).astype(BF16)
            slope = 0.5 * (1.0 + th) + 0.5 * u * (1.0 - th * th) * (GELU_COEF * (1.0 + 0.134145 * square))
            gp[rows, tile] = (hidden_grad[rows, tile] * slope).astype(BF16)
        for t in range(TILES):
            tile = slice(t * 256, (t + 1) * 256)
            product = nt(gp[rows, :], wf[tile, :]).astype(BF16)
            for i in range(count):
                stage_g[first + i, :, tile] = product[i * ROWS : (i + 1) * ROWS]
        for i in range(first, first + count):
            if i:
                moves.append(links.send(stage_g.at[i], parts_g.at[i - 1], at.along_z((0, 1, 3, 2)[i])))

    feed(0, 1)
    gather.neighbours()
    feed(1, 2)
    gather.rest()
    feed(3, 1)
    grad_f, grad_t = r["grad_f"], r["grad_t"]

    def gradient_sum(tag, grad, columns, final):
        return GradientSum(
            links, at, grad, columns, r["pair_" + tag], r["strips_" + tag], r["cross_" + tag], final
        )

    @pl.loop(0, TILES)
    def _(t):
        grad_t[tile_of(t, 256), :] = tn(d_all[:, tile_of(t, 256)], hid[...]).astype(BF16)

    whole = slice(0, D)
    sum_t = gradient_sum("t", grad_t, whole, fin_t)
    sum_t.send_core()

    @pl.loop(0, TILES)
    def _(t):
        grad_f[tile_of(t, 256), :] = tn(x2[:, tile_of(t, 256)], gp[...]).astype(BF16)

    sum_f = GradientSumY(links, at, grad_f, r["pair_f"], r["cross_f"], r["strips_f"], r["half_f"], fin_f)
    sum_f.send_core()
    sum_t.send_x()
    unit, scale = norm_stats(r["middle"][...])
    grad = d_all[0:ROWS, :].astype(F32)
    grad_normed = stage_g[0].astype(F32)
    for i in range(3):
        moves[i].wait_recv()
        grad_normed = grad_normed + parts_g[i].astype(F32)
    grad_middle = grad + norm_gradient(grad_normed, unit, scale, vec[1:2, :])
    r["gm"][...] = grad_middle
    branch = grad_middle.astype(BF16)
    g_all = r["g_all"]
    g_all[0:ROWS, :] = branch
    gather = GatherZ(links, at, g_all)
    sums = r["sums"]
    sums[1:2, :] = column_sum(grad_normed * unit)
    sums[3:4, :] = column_sum(grad_normed)
    sums[4:5, :] = column_sum(grad)
    sums[5:6, :] = column_sum(branch.astype(F32))
    sums[8:9, :] = column_sum(gp[...].astype(F32))
    sum_f.send_y()
    sum_p.sent()
    sum_b = SumZ(links, at, stage, r["parts_b"], r["over_b"])

    @pl.loop(0, TILES)
    def _(t):
        product = nt(hid[...], wt[tile_of(t, 256), :]).astype(BF16)
        for i in range(4):
            stage[i, :, tile_of(t, 256)] = product[i * ROWS : (i + 1) * ROWS]

    gather.neighbours()
    gather.rest()

    dkv, go, dq, dq_t, delta = r["dkv"], r["go"], r["dq"], att_t, r["delta"]
    take, take_y, gkv = r["take"], r["take_y"], r["gkv"]
    sum_b.send_across()
    grad = nn(g_all[...], r["wpt"][...]).astype(BF16)
    go[...] = interleave(jnp.zeros((QUARTER, PART), BF16), grad)
    for slot in range(4):
        both = grad[slot * ROWS : (slot + 1) * ROWS, :].astype(F32).T * att_t[slot]
        delta[slot * 8 : slot * 8 + HEADS, :] = jnp.sum(both.reshape(HEADS, HS, ROWS), axis=1)
    for copy in moves:
        copy.wait_send()
    sum_t.send_y()
    slots = []
    for j in range(4):
        k = lax.rem(j + 4 - h, 4)
        slots.append(jnp.where(k == 2, 3, jnp.where(k == 3, 2, k)))

    def back_head(head):
        tile = slice(head * 128, (head + 1) * 128)
        sides = [
            jnp.concatenate([q[rows_of(slot * ROWS), tile], go[rows_of(slot * ROWS), tile]], axis=0) for slot in slots
        ]
        logs = [lse[pl.ds(slot * 8 + head, 1), :] for slot in slots]
        inner = [delta[pl.ds(slot * 8 + head, 1), :] for slot in slots]
        grads = [[] for _ in range(4)]
        for b in range(4):
            columns = []
            for j in range(b, 4):
                products = nt(keys_of(b, tile), sides[j])
                scores = products[:, :128]
                if b == j:
                    scores = mask_last(scores, j, sub_block(j, w) * ROWS)
                probs = jnp.exp(scores - logs[j])
                grad_scores = (probs * (products[:, 128:] - inner[j])).astype(BF16)
                columns += [grad_scores, probs.astype(BF16)]
                grads[j].append(grad_scores)
            both = nn(jnp.concatenate(columns, axis=1), jnp.concatenate(sides[b:], axis=0))
            dkv[b, :, :, tile] = both.astype(BF16).reshape(4, ROWS, 128)
        for j in range(4):
            result = nn(kvt[tile, 0 : (j + 1) * QUARTER], jnp.concatenate(grads[j], axis=0))
            dq_t[slots[j], head * HS : (head + 1) * HS, :] = result[:HS, :] * HS**-0.5

    first, second, third = [], [], []

    def share_head(head):
        tile = slice(head * 128, (head + 1) * 128)
        first.append(links.send(dkv.at[:, at.wyc, :, tile], take.at[1, :, :, tile], at.core))
        second.append(links.send(dkv.at[:, at.wc, :, tile], take.at[0, :, :, tile], at.core))

    def cross_head(head):
        tile = slice(head * 128, (head + 1) * 128)
        first[head].wait_recv()
        for j in range(4):
            both = dkv[j, at.wy, :, tile].astype(F32) + take[1, j, :, tile].astype(F32)
            stage_g[j, :, tile] = both.astype(BF16)
        third.append(links.send(stage_g.at[:, :, tile], take_y.at[:, :, tile], at.near))

    keep = []

    def send_back(total):
        strip = total.send_back()
        copy = pltpu.make_async_copy(total.total[0], strip, local.at[7 + len(keep)])
        copy.start()
        keep.append(copy)

    for head in range(HEADS):
        back_head(head)
        share_head(head)
        if head == 0:
            sum_b.send_near()
        if head:
            cross_head(head - 1)
        if head == 2:
            sum_f.send_x()
        if head == 3:
            send_back(sum_t)
    for slot in range(4):
        dq[slot * ROWS : (slot + 1) * ROWS, :] = dq_t[slot].T.astype(BF16)
    cross_head(HEADS - 1)
    sum_b.join_ahead()
    sum_b.join_behind()

    sum_t.sent_core()

    @pl.loop(0, TILES)
    def _(t):
        tile = tile_of(t, 256)
        pieces = [tn(x1[:, tile], dq[...]).astype(BF16), tn(g_all[:, tile], att[...]).astype(BF16)]
        grad_t[tile, PAIR:] = jnp.concatenate(pieces, axis=1)

    sum_q = gradient_sum("q", grad_t, slice(PAIR, D), fin_q)
    sum_q.send_core()
    sum_f.send_back()

    def send_rows(result, back, target):
        back[...] = result.astype(BF16).T
        place = target.at[:, rows_of(mine * ROWS)]
        keep = pltpu.make_async_copy(back.at[block_of(w)], place, local.at[6])
        keep.start()
        copies = [links.send(back.at[block_of(peer)], place, device) for device, peer in at.width_peers]
        keep.wait()
        return copies

    sums[9:10, 0:PART] = column_sum(dq[...].astype(F32))
    sum_q.send_x()
    for head in range(HEADS):
        tile = slice(head * 128, (head + 1) * 128)
        second[head].wait_recv()
        third[head].wait()
        for j in range(4):
            total = dkv[j, w, :, tile].astype(F32) + take[0, j, :, tile].astype(F32) + take_y[j, :, tile].astype(F32)
            gkv[rows_of(slots[j] * ROWS), tile] = total.astype(BF16)

    result = r["middle"][...] + vec[5:6, :] + sum_b.result()
    sum_b.sent()
    sum_l = SumZ(links, at, stage, r["parts"], r["over"])

    def first_partial(first, count):
        rows = slice(first * ROWS, (first + count) * ROWS)
        product = (nt(dq[rows, :], r["wq"][...]) + nt(gkv[rows, :], r["wkv"][...])).astype(BF16)
        for i in range(count):
            stage[first + i] = product[i * ROWS : (i + 1) * ROWS]

    first_partial(3, 1)
    sum_l.send_across()
    first_partial(1, 2)
    sum_l.send_near()

    @pl.loop(0, TILES)
    def _(t):
        tile = tile_of(t, 256)
        grad_t[tile, 0:PAIR] = tn(x1[:, tile], gkv[...]).astype(BF16)

    sum_k = gradient_sum("k", grad_t, slice(0, PAIR), fin_k)
    sum_k.send_core()
    sum_l.join_ahead()
    sum_l.join_behind()
    first_partial(0, 1)
    sum_k.send_x()
    keep.append(sum_f.send_opposite(local.at[7 + len(keep)]))
    returns = send_rows(result, r["xa"], bo)
    grad_values = column_sum(gkv[...].astype(F32))
    for head in range(HEADS):
        sums[9:10, PART + head * HS : PART + (head + 1) * HS] = grad_values[:, head * 128 + HS : (head + 1) * 128]
    sums[9:10, PAIR:] = jnp.zeros((1, PAIR), F32)
    sums[10:16, :] = jnp.zeros((6, D), F32)
    sums[6:8, :] = jnp.zeros((2, D), F32)
    sum_q.send_y()
    grad_normed = sum_l.result()
    unit, scale = norm_stats(r["x"][...].astype(F32))
    sums[0:1, :] = column_sum(grad_normed * unit)
    sums[2:3, :] = column_sum(grad_normed)
    over_z = [links.send(sums.at[0:8], r["sums_z"].at[k - 1], at.along_z(k)) for k in (1, 2, 3)]
    over_w = [links.send(sums.at[8:16], r["take_v"].at[i], at.width_peers[i][0]) for i in range(3)]
    result = r["gm"][...] + norm_gradient(grad_normed, unit, scale, vec[0:1, :])
    returns += send_rows(result, r["da"], dt)

    for copy in over_z + over_w:
        copy.wait_recv()
    normed = sums[0:8, :] + r["sums_z"][0] + r["sums_z"][1] + r["sums_z"][2]
    for part in range(4):
        r["sums_w"][part] = normed[:, part * PART : (part + 1) * PART]
    over_w = [
        links.send(r["sums_w"].at[peer], r["take_w"].at[i], device)
        for i, (device, peer) in enumerate(at.width_peers)
    ]
    biases = sums[8:10, :] + r["take_v"][0, 0:2] + r["take_v"][1, 0:2] + r["take_v"][2, 0:2]
    sum_k.send_y()
    for copy in over_w:
        copy.wait_recv()
    sums_d = r["sums_d"]
    normed = r["sums_w"][w] + r["take_w"][0] + r["take_w"][1] + r["take_w"][2]
    sums_d[...] = jnp.zeros((8, D), F32)
    for i in range(6):
        sums_d[i // 3 : i // 3 + 1, (i % 3) * 384 : (i % 3) * 384 + PART] = normed[i : i + 1, :]
    sums_d[2:4, :] = biases
    over_x = [links.send(sums_d, r["sums_x"].at[i], device) for i, device in enumerate(at.dp_peers)]
    send_back(sum_q)
    send_back(sum_k)
    total = sums_d[...]
    for i, copy in enumerate(over_x):
        copy.wait_recv()
        total = total + r["sums_x"][i]
    fin_v[...] = total
    for copy in keep:
        copy.wait()
    for total in (sum_t, sum_f, sum_q, sum_k):
        total.finish()
    for copy in returns:
        copy.wait()
    for copy in links.copies:
        copy.wait_send()


def block(*inputs):
    return pl.pallas_call(
        block_kernel,
        name="block",
        out_shape=(
            jax.ShapeDtypeStruct((PART, QUARTER), BF16),
            jax.ShapeDtypeStruct((PART, QUARTER), BF16),
            jax.ShapeDtypeStruct((PART, D), BF16),
            jax.ShapeDtypeStruct((PART, D), BF16),
            jax.ShapeDtypeStruct((PART, PAIR), BF16),
            jax.ShapeDtypeStruct((PART, PAIR), BF16),
            jax.ShapeDtypeStruct((8, D), F32),
        ),
        in_specs=[ANY, ANY, VMEM, VMEM, VMEM, VMEM, ANY, VMEM, ANY, ANY, VMEM, ANY],
        out_specs=(ANY, ANY, ANY, ANY, ANY, ANY, VMEM),
        scratch_shapes=[pltpu.VMEM(shape, kind) for shape, kind in SCRATCH.values()]
        + [pltpu.SemaphoreType.DMA((COPIES,)), pltpu.SemaphoreType.DMA((COPIES,)), pltpu.SemaphoreType.DMA((12,))],
        compiler_params=pltpu.CompilerParams(collective_id=1, has_side_effects=True, vmem_limit_bytes=64 * 2**20),
    )(*inputs)


def finish_kernel(bo, dt, f, t, qp, kv, v, out, d_tok, gain, shift, d_wa, d_bqv, d_wp, d_bp, d_wf, d_bf, d_wo, d_bo):
    out[...] = bo[...]
    d_tok[...] = dt[...]
    d_wf[...] = f[...].astype(F32)
    d_wo[...] = t[...].astype(F32)
    d_wa[0] = qp[:, :PART].astype(F32)
    d_wp[...] = qp[:, PART:].astype(F32).T
    both = kv[...].astype(F32)
    d_wa[1] = jnp.concatenate([both[:, head * 128 : head * 128 + HS] for head in range(HEADS)], axis=1)
    d_wa[2] = jnp.concatenate([both[:, head * 128 + HS : (head + 1) * 128] for head in range(HEADS)], axis=1)
    rows = [v[i // 3 : i // 3 + 1, (i % 3) * 384 : (i % 3) * 384 + PART] for i in range(6)]
    gain[0:1, :] = rows[0]
    gain[1:2, :] = rows[1]
    shift[0:1, :] = rows[2]
    shift[1:2, :] = rows[3]
    d_bo[...] = rows[4].reshape(PART)
    d_bp[...] = rows[5].reshape(PART)
    d_bf[...] = v[2:3, :].reshape(D)
    d_bqv[0:1, :] = v[3:4, 0:PART]
    d_bqv[1:2, :] = v[3:4, PART:PAIR]


def finish(*inputs):
    shapes = [
        ((PART, QUARTER), BF16),
        ((PART, QUARTER), BF16),
        ((2, PART), F32),
        ((2, PART), F32),
        ((3, PART, PART), F32),
        ((2, PART), F32),
        ((PART, PART), F32),
        ((PART,), F32),
        ((PART, D), F32),
        ((D,), F32),
        ((PART, D), F32),
        ((PART,), F32),
    ]
    return pl.pallas_call(
        finish_kernel,
        name="finish",
        out_shape=[jax.ShapeDtypeStruct(shape, kind) for shape, kind in shapes],
        in_specs=[VMEM] * 7,
        out_specs=[VMEM] * 12,
        compiler_params=pltpu.CompilerParams(vmem_limit_bytes=63 * 2**20),
    )(*inputs)


def shards(tokens, ln_gain, ln_bias, w_attn, b_qv, w_proj, b_proj, w_fc, b_fc, w_out, b_out, d_out):
    parts = block(tokens.T, d_out.T, ln_gain, ln_bias, b_proj, b_out, w_attn, b_qv, w_proj, w_fc, b_fc, w_out.T)
    results = list(finish(*parts))
    for i in (0, 1, 10):
        results[i] = results[i].T
    return tuple(results)


def solution(mesh):
    in_specs = (
        P(("dp", "heads"), "width"),
        P(None, "width"),
        P(None, "width"),
        P(None, "width", "heads"),
        P(None, "heads"),
        P("heads", "width"),
        P("width"),
        P("width", "heads"),
        P("heads"),
        P("heads", "width"),
        P("width"),
        P(("dp", "heads"), "width"),
    )
    out_specs = (
        P(("dp", "heads"), "width"),
        P(("dp", "heads"), "width"),
        P(None, "width"),
        P(None, "width"),
        P(None, "width", "heads"),
        P(None, "heads"),
        P("heads", "width"),
        P("width"),
        P("width", "heads"),
        P("heads"),
        P("heads", "width"),
        P("width"),
    )
    return jax.shard_map(shards, mesh=mesh, in_specs=in_specs, out_specs=out_specs, check_vma=False)
```

```python
import functools

import jax
import jax.numpy as jnp
from jax import lax
from jax.experimental import pallas as pl
from jax.experimental.pallas import tpu as pltpu
from jax.sharding import PartitionSpec as P

F32, BF16 = jnp.float32, jnp.bfloat16
D, HS, ROWS, PART, QUARTER, HEADS = 1280, 64, 128, 320, 512, 5
PAIR = 2 * PART
STRIP = PART // 4
HALF = ROWS // 2
EPSILON = 1e-05
GELU_COEF = 0.7978845608028654
MASKED = -1e30
VMEM = pl.BlockSpec(memory_space=pltpu.VMEM)
ANY = pl.BlockSpec(memory_space=pl.ANY)
TILES = D // 256


def nn(a, b):
    return jnp.dot(a, b, preferred_element_type=F32)


def nt(a, b):
    return lax.dot_general(a, b, (((1,), (1,)), ((), ())), preferred_element_type=F32)


def tn(a, b):
    return lax.dot_general(a, b, (((0,), (0,)), ((), ())), preferred_element_type=F32)


def rows_of(start, size=ROWS):
    return pl.ds(pl.multiple_of(start, size), size)


def block_of(who):
    return pl.ds(pl.multiple_of(who * PART, 64), PART)


def tile_of(i, size):
    return pl.ds(pl.multiple_of(i * size, size), size)


def sub_block(quarter, w):
    return w + lax.rem(quarter, 2) * (3 - 2 * w)


class Place:
    def __init__(self):
        self.dp, self.w, self.h = (lax.axis_index(n) for n in ("dp", "width", "heads"))
        self.x = lax.rem(self.dp, 4)
        self.wc = self.w + 1 - 2 * lax.rem(self.w, 2)
        self.wy = lax.rem(self.w + 2, 4)
        self.wyc = lax.rem(self.wc + 2, 4)
        across = lax.rem(self.dp + 4, 8)
        self.core = (self.dp, self.wc, self.h)
        self.near = (self.dp, self.wy, self.h)
        self.near_core = (self.dp, self.wyc, self.h)
        self.far = (across, self.wy, self.h)
        self.opposite = (across, self.w, self.h)
        self.width_peers = ((self.near, self.wy), (self.near_core, self.wyc), (self.core, self.wc))

        beyond = lax.rem(self.dp + 4, 8) - self.x
        self.dp_peers = [self.along_x(k) for k in (1, 2, 3)] + [self.opposite]
        self.dp_peers += [(beyond + lax.rem(self.x + k, 4), self.w, self.h) for k in (1, 2, 3)]

    def along_z(self, k):
        return (self.dp, self.w, lax.rem(self.h + k, 4))

    def along_x(self, k):
        return (self.dp - self.x + lax.rem(self.x + k, 4), self.w, self.h)

    def chunk(self, k):
        return lax.rem(self.h + k, 4)


def greet(devices):
    barrier = pltpu.get_barrier_semaphore()
    for device in devices:
        pl.semaphore_signal(barrier, inc=1, device_id=device, device_id_type=pl.DeviceIdType.MESH)
    pl.semaphore_wait(barrier, len(devices))


class Move:
    def __init__(self, copy):
        self.copy, self.left = copy, False
        self.start, self.wait_recv = copy.start, copy.wait_recv

    def wait_send(self):
        if not self.left:
            self.copy.wait_send()
        self.left = True

    def wait(self):
        self.wait_recv()
        self.wait_send()


class Links:
    def __init__(self, sent, landed):
        self.sent, self.landed, self.copies, self.count = sent, landed, [], 0

    def reserve(self, count):
        self.count += count
        return self.count - count

    def make(self, i, source, target, device):
        return pltpu.make_async_remote_copy(
            src_ref=source,
            dst_ref=target,
            send_sem=self.sent.at[i],
            recv_sem=self.landed.at[i],
            device_id=device,
            device_id_type=pl.DeviceIdType.MESH,
        )

    def plan(self, source, target, device):
        self.copies.append(Move(self.make(self.reserve(1), source, target, device)))
        return self.copies[-1]

    def send(self, source, target, device):
        copy = self.plan(source, target, device)
        copy.start()
        return copy


class GatherZ:
    def __init__(self, links, at, rows):
        right, left = at.along_z(1), at.along_z(3)
        own, ahead, behind = (rows.at[pl.ds(i * ROWS, ROWS)] for i in range(3))
        self.right = links.send(own, behind, right)
        self.left = links.send(own, ahead, left)
        self.low = links.plan(
            rows.at[pl.ds(2 * ROWS, HALF)], rows.at[pl.ds(3 * ROWS, HALF)], right
        )
        self.high = links.plan(
            rows.at[pl.ds(ROWS + HALF, HALF)], rows.at[pl.ds(3 * ROWS + HALF, HALF)], left
        )

    def neighbours(self):
        self.left.wait_recv()
        self.high.start()
        self.right.wait_recv()
        self.low.start()

    def rest(self):
        self.low.wait_recv()
        self.high.wait_recv()


class SumZ:
    def __init__(self, links, at, stage, parts, over):
        self.stage, self.parts, self.over = stage, parts, over
        right, left = at.along_z(1), at.along_z(3)
        top, bottom = pl.ds(0, HALF), pl.ds(HALF, HALF)
        self.far_right = links.plan(stage.at[3, top], over.at[0], right)
        self.far_left = links.plan(stage.at[3, bottom], over.at[1], left)
        self.right_bottom = links.plan(stage.at[1, bottom], parts.at[0, bottom], right)
        self.right_top = links.plan(stage.at[1, top], parts.at[0, top], right)
        self.left_top = links.plan(stage.at[2, top], parts.at[1, top], left)
        self.left_bottom = links.plan(stage.at[2, bottom], parts.at[1, bottom], left)

    def sent(self):
        for copy in (self.far_right, self.far_left, self.right_bottom, self.right_top, self.left_top, self.left_bottom):
            copy.wait_send()

    def send_across(self):
        self.far_right.start()
        self.far_left.start()

    def send_near(self):
        self.right_bottom.start()
        self.left_top.start()

    def join_ahead(self):
        self.far_right.wait_recv()
        joined = self.stage[1, 0:HALF, :].astype(F32) + self.over[0].astype(F32)
        self.stage[1, 0:HALF, :] = joined.astype(BF16)
        self.right_top.start()

    def join_behind(self):
        self.far_left.wait_recv()
        joined = self.stage[2, HALF:, :].astype(F32) + self.over[1].astype(F32)
        self.stage[2, HALF:, :] = joined.astype(BF16)
        self.left_bottom.start()

    def result(self):
        for copy in (self.right_bottom, self.right_top, self.left_top, self.left_bottom):
            copy.wait_recv()
        return self.stage[0].astype(F32) + self.parts[0].astype(F32) + self.parts[1].astype(F32)


class GradientSum:
    def __init__(self, links, at, grad, columns, pair, strips, cross, final):
        self.links, self.at, self.grad, self.columns = links, at, grad, columns
        self.pair, self.strips, self.cross, self.final = pair, strips, cross, final
        self.strip = rows_of(at.x * STRIP, STRIP)
        self.total = [pair.at[0, self.strip], pair.at[1, self.strip]]

    def mine(self, who):
        return self.grad.at[block_of(who), self.columns]

    def send_core(self):
        at, links = self.at, self.links
        self.core = [
            links.send(self.mine(at.wc), self.pair.at[0], at.core),
            links.send(self.mine(at.wyc), self.pair.at[1], at.core),
        ]

    def sent_core(self):
        for copy in self.core:
            copy.wait_send()

    def add_core(self):
        for i, who in ((0, self.at.w), (1, self.at.wy)):
            self.core[i].wait_recv()
            self.pair[i] = (self.pair[i].astype(F32) + self.mine(who)[...].astype(F32)).astype(BF16)

    def send_x(self):
        at, links = self.at, self.links
        self.add_core()
        self.along = [
            links.send(
                self.pair.at[:, rows_of(lax.rem(at.x + k, 4) * STRIP, STRIP)], self.strips.at[k - 1], at.along_x(k)
            )
            for k in (2, 1, 3)
        ]

    def send_x_by_neighbours(self):
        at, links = self.at, self.links
        self.add_core()
        right, left = at.along_x(1), at.along_x(3)
        ahead, across, behind = (rows_of(lax.rem(at.x + k, 4) * STRIP, STRIP) for k in (1, 2, 3))
        parts, over = self.strips, self.strips.at[2]
        self.over_x = [
            links.send(self.pair.at[0, across], over.at[0], right),
            links.send(self.pair.at[1, across], over.at[1], left),
        ]
        self.along = [
            links.send(self.pair.at[1, ahead], parts.at[0, 1], right),
            links.send(self.pair.at[0, behind], parts.at[1, 0], left),
            links.plan(self.pair.at[0, ahead], parts.at[0, 0], right),
            links.plan(self.pair.at[1, behind], parts.at[1, 1], left),
        ]
        self.relayed = (self.pair.at[0, ahead], self.pair.at[1, behind])

    def relay_x(self):
        for i in range(2):
            self.over_x[i].wait_recv()
            joined = self.relayed[i][...].astype(F32) + self.strips[2, i].astype(F32)
            self.relayed[i][...] = joined.astype(BF16)
            self.along[2 + i].start()

    def add_strips(self):
        for copy in self.along:
            copy.wait_recv()
        for i in range(2):
            joined = self.total[i][...].astype(F32)
            for k in range(3 if len(self.along) == 3 else 2):
                joined = joined + self.strips[k, i].astype(F32)
            self.total[i][...] = joined.astype(BF16)

    def send_y(self):
        self.add_strips()
        self.over = [
            self.links.send(self.total[1], self.cross.at[0], self.at.near),
            self.links.send(self.total[1], self.cross.at[1], self.at.far),
            self.links.send(self.total[0], self.cross.at[2], self.at.opposite),
        ]

    def send_far(self):
        self.add_strips()
        self.over = [self.links.send(self.total[1], self.cross.at[0], self.at.far)]

    def send_opposite(self):
        self.over[0].wait()
        joined = self.total[0][...].astype(F32) + self.cross[0].astype(F32)
        self.total[0][...] = joined.astype(BF16)
        self.over = [self.links.send(self.total[0], self.cross.at[1], self.at.opposite)]

    def send_back(self, passing):
        at, links = self.at, self.links
        joined = self.total[0][...].astype(F32)
        for copy in self.over:
            copy.wait()
        places = (0, 1, 2) if len(self.over) == 3 else (1,)
        for place in places:
            joined = joined + self.cross[place].astype(F32)
        self.total[0][...] = joined.astype(BF16)
        strip = self.final.at[self.strip]
        self.back = [links.send(self.total[0], strip, at.along_x(k)) for k in ((1, 3) if passing else (2, 1, 3))]
        self.passing = passing
        return strip

    def pass_back(self):
        at, links = self.at, self.links
        behind, ahead = lax.rem(at.x + 3, 4) * STRIP, lax.rem(at.x + 1, 4) * STRIP
        first = self.final.at[pl.ds(pl.multiple_of(behind, 16), 48)]
        second = self.final.at[pl.ds(pl.multiple_of(ahead + 48, 16), 32)]
        self.back[0].wait_recv()
        self.back[1].wait_recv()
        self.back = [
            links.send(first, first, at.along_x(1)),
            links.send(second, second, at.along_x(3)),
        ]

    def finish(self):
        for copy in self.back:
            copy.wait_recv()


class GradientSumY:
    def __init__(self, links, at, grad, pair, cross, strips, half, final):
        self.links, self.at, self.grad = links, at, grad
        self.pair, self.cross, self.strips, self.half, self.final = pair, cross, strips, half, final
        part = at.dp // 4
        self.kept = pl.ds(pl.multiple_of(part * PAIR, PAIR), PAIR)
        self.given = pl.ds(pl.multiple_of((1 - part) * PAIR, PAIR), PAIR)
        self.strip = rows_of(at.x * STRIP, STRIP)

    def mine(self, who):
        return self.grad.at[block_of(who)]

    def send_core(self):
        at, links = self.at, self.links
        self.core = [
            links.send(self.mine(at.wc), self.pair.at[0], at.core),
            links.send(self.mine(at.wyc), self.pair.at[1], at.core),
        ]

    def send_y(self):
        at, links = self.at, self.links
        for i, who in ((0, at.w), (1, at.wy)):
            self.core[i].wait_recv()
            self.pair[i] = (self.pair[i].astype(F32) + self.mine(who)[...].astype(F32)).astype(BF16)
        self.over = [
            links.send(self.pair.at[1, :, self.kept], self.cross.at[0], at.near),
            links.send(self.pair.at[1, :, self.given], self.cross.at[1], at.far),
            links.send(self.pair.at[0, :, self.given], self.cross.at[2], at.opposite),
        ]

    def send_x(self):
        at, links = self.at, self.links
        joined = self.pair[0, :, self.kept].astype(F32)
        for k in range(3):
            self.over[k].wait_recv()
            joined = joined + self.cross[k].astype(F32)
        self.pair[0, :, self.kept] = joined.astype(BF16)
        self.along = [
            links.send(
                self.pair.at[0, rows_of(lax.rem(at.x + k, 4) * STRIP, STRIP), self.kept],
                self.strips.at[k - 1],
                at.along_x(k),
            )
            for k in (2, 1, 3)
        ]

    def send_back(self):
        at, links = self.at, self.links
        joined = self.pair[0, self.strip, self.kept].astype(F32)
        for copy in self.along:
            copy.wait_recv()
        for k in range(3):
            joined = joined + self.strips[k].astype(F32)
        self.half[self.strip, :] = joined.astype(BF16)
        place = self.half.at[self.strip]
        self.back = [links.send(place, place, at.along_x(k)) for k in (2, 1, 3)]

    def send_opposite(self, sem):
        for copy in self.back:
            copy.wait_recv()
        place = self.final.at[:, self.kept]
        self.last = self.links.send(self.half, place, self.at.opposite)
        keep = pltpu.make_async_copy(self.half, place, sem)
        keep.start()
        return keep

    def finish(self):
        self.last.wait_recv()


def norm_stats(values):
    mean = jnp.mean(values, axis=1, keepdims=True)
    centred = values - mean
    scale = lax.rsqrt(jnp.mean(centred * centred, axis=1, keepdims=True) + EPSILON)
    return centred * scale, scale


def norm_gradient(grad, unit, scale, gain):
    scaled = grad * gain
    mean = jnp.mean(scaled, axis=1, keepdims=True)
    along = jnp.mean(scaled * unit, axis=1, keepdims=True)
    return scale * (scaled - mean - unit * along)


def interleave(first, second):
    pieces = []
    for head in range(HEADS):
        part = slice(head * HS, (head + 1) * HS)
        pieces += [first[:, part], second[:, part]]
    return jnp.concatenate(pieces, axis=1)


def mask_last(scores, quarter, shift):
    shape = (4, ROWS, ROWS)
    owner = lax.broadcasted_iota(jnp.int32, shape, 0)
    if quarter % 2:
        owner = 3 - owner
    key = owner * ROWS + lax.broadcasted_iota(jnp.int32, shape, 1)
    query = lax.broadcasted_iota(jnp.int32, shape, 2) + shift
    seen = (key <= query).reshape(QUARTER, ROWS)
    parts = [scores[:, i * ROWS : (i + 1) * ROWS] for i in range(scores.shape[1] // ROWS)]
    parts = [jnp.where(seen, part, MASKED) for part in parts]
    return parts[0] if len(parts) == 1 else jnp.concatenate(parts, axis=1)


def column_sum(values):
    return jnp.sum(values, axis=0, keepdims=True)


SCRATCH = dict(
    wkv=((D, PAIR), BF16),
    wq=((D, PART), BF16),
    wpt=((D, PART), BF16),
    wf=((D, D), BF16),
    wt=((D, D), BF16),
    wa_raw=((3, PART, PART), BF16),
    wp_raw=((PART, PART), BF16),
    xa=((D, ROWS), BF16),
    da=((D, ROWS), BF16),
    vl=((8, PART), F32),
    vg=((4, 8, PART), F32),
    vec=((8, D), F32),
    bf=((8, D), F32),
    x=((ROWS, D), BF16),
    x1=((QUARTER, D), BF16),
    q=((QUARTER, PAIR), BF16),
    kv=((4, 4, ROWS, PAIR), BF16),
    kvt=((PAIR, 2048), BF16),
    att=((QUARTER, PART), BF16),
    att_t=((4, PART, ROWS), F32),
    lse=((32, 128), F32),
    delta=((32, 128), F32),
    middle=((ROWS, D), F32),
    stage=((4, ROWS, D), BF16),
    parts=((2, ROWS, D), BF16),
    over=((2, HALF, D), BF16),
    d_all=((QUARTER, D), BF16),
    x2=((QUARTER, D), BF16),
    hidden_grad=((QUARTER, D), F32),
    hid=((QUARTER, D), BF16),
    gp=((QUARTER, D), BF16),
    stage_g=((4, ROWS, D), BF16),
    parts_g=((3, ROWS, D), BF16),
    parts_b=((2, ROWS, D), BF16),
    over_b=((2, HALF, D), BF16),
    gm=((ROWS, D), F32),
    grad_f=((D, D), BF16),
    grad_t=((D, D), BF16),
    pair_f=((2, PART, D), BF16),
    pair_t=((2, PART, D), BF16),
    pair_q=((2, PART, PAIR), BF16),
    pair_k=((2, PART, PAIR), BF16),
    strips_f=((3, STRIP, PAIR), BF16),
    half_f=((PART, PAIR), BF16),
    strips_t=((3, 2, STRIP, D), BF16),
    strips_q=((3, 2, STRIP, PAIR), BF16),
    strips_k=((3, 2, STRIP, PAIR), BF16),
    cross_f=((3, PART, PAIR), BF16),
    cross_t=((3, STRIP, D), BF16),
    cross_q=((3, STRIP, PAIR), BF16),
    cross_k=((3, STRIP, PAIR), BF16),
    g_all=((QUARTER, D), BF16),
    go=((QUARTER, PAIR), BF16),
    dkv=((HEADS, 4, 4, ROWS, 128), BF16),
    take=((2, HEADS, 4, ROWS, 128), BF16),
    take_y=((HEADS, 4, ROWS, 128), BF16),
    dq=((QUARTER, PART), BF16),
    gkv=((QUARTER, PAIR), BF16),
    sums=((16, D), F32),
    sums_n=((8, PART), F32),
    sums_z=((3, 8, PART), F32),
    sums_w=((4, 8, PART), F32),
    take_w=((3, 8, PART), F32),
    take_v=((3, 8, D), F32),
    sums_d=((8, D), F32),
    sums_x=((7, 8, D), F32),
)
COPIES = 176


def block_kernel(*refs):
    names = ("tok", "dout", "gain", "shift", "b_proj", "b_out", "wa_in", "bqv", "wp_in", "wf_in", "b_fc", "wo_in")
    names += ("bo", "dt", "fin_f", "fin_t", "fin_q", "fin_k", "fin_v")
    names += tuple(SCRATCH) + ("sent", "landed", "local")
    r = dict(zip(names, refs))
    (tok, dout, gain, shift, b_proj, b_out, wa_in, bqv, wp_in, wf_in, b_fc, wo_in) = refs[:12]
    (bo, dt, fin_f, fin_t, fin_q, fin_k, fin_v) = refs[12:19]
    at = Place()
    w, h = at.w, at.h
    links = Links(r["sent"], r["landed"])
    local = r["local"]
    mine = sub_block(h, w)
    vec = r["vec"]

    wf, wt = r["wf"], r["wt"]
    loads = [
        pltpu.make_async_copy(wa_in, r["wa_raw"], local.at[0]),
        pltpu.make_async_copy(wp_in, r["wp_raw"], local.at[1]),
        pltpu.make_async_copy(wo_in, wt.at[block_of(w)], local.at[2]),
        pltpu.make_async_copy(wf_in, wf.at[block_of(w)], local.at[3]),
        pltpu.make_async_copy(tok.at[:, rows_of(mine * ROWS)], r["xa"].at[block_of(w)], local.at[4]),
        pltpu.make_async_copy(dout.at[:, rows_of(mine * ROWS)], r["da"].at[block_of(w)], local.at[5]),
    ]
    for copy in loads:
        copy.start()
    vl = r["vl"]
    vl[0:2, :] = gain[...]
    vl[2:4, :] = shift[...]
    vl[4:5, :] = b_proj[...].reshape(1, PART)
    vl[5:6, :] = b_out[...].reshape(1, PART)
    vl[6:8, :] = jnp.zeros((2, PART), F32)
    r["bf"][0:1, :] = b_fc[...].reshape(1, D)
    greet(
        [at.core, at.near, at.near_core, at.far, at.opposite]
        + [at.along_z(k) for k in (1, 2, 3)]
        + [at.along_x(k) for k in (1, 2, 3)]
        + [device for device in at.dp_peers[4:]]
    )

    def spread(source, slots):
        return [
            links.send(source.at[:, rows_of(sub_block(h, peer) * ROWS)], slots.at[block_of(w)], device)
            for device, peer in at.width_peers
        ]

    arrive = spread(tok, r["xa"])
    arrive += [links.send(vl, r["vg"].at[w], device) for device, _ in at.width_peers]
    r["vg"][w] = vl[...]

    class Weight:
        def __init__(self, full, device):
            own_block, next_block = full.at[block_of(w)], full.at[block_of(at.wy)]
            self.over = links.send(own_block, own_block, device)
            self.core = links.send(own_block, own_block, at.core)
            self.other = links.plan(next_block, next_block, at.core)

        def forward(self):
            self.over.wait_recv()
            self.other.start()

        def ready(self):
            self.core.wait_recv()
            self.other.wait_recv()

    loads[0].wait()
    r["wkv"][block_of(w), :] = interleave(r["wa_raw"][1], r["wa_raw"][2])
    weight_kv = Weight(r["wkv"], at.far)
    r["wq"][block_of(w), :] = r["wa_raw"][0]
    weight_q = Weight(r["wq"], at.far)
    loads[1].wait()
    r["wpt"][block_of(w), :] = r["wp_raw"][...].T
    loads[4].wait()
    for copy in arrive:
        copy.wait_recv()

    arrive_d = spread(dout, r["da"])
    vec[...] = jnp.concatenate([r["vg"][i] for i in range(4)], axis=1)
    r["x"][...] = r["xa"][...].T
    unit, _ = norm_stats(r["x"][...].astype(F32))
    x1, kv, q = r["x1"], r["kv"], r["q"]
    x1[0:ROWS, :] = (unit * vec[0:1, :] + vec[2:3, :]).astype(BF16)
    gather = GatherZ(links, at, x1)
    value_bias = interleave(jnp.zeros((1, PART), F32), bqv[1:2, :])
    weight_kv.forward()
    weight_kv.ready()
    weight_p = Weight(r["wpt"], at.far)
    loads[2].wait()
    weight_t = Weight(wt, at.far)
    quarter = [at.chunk(k) for k in (0, 1, 3, 2)]
    shares, passed = [], []

    def key_rows(first, count):
        rows = (nn(x1[first * ROWS : (first + count) * ROWS, :], r["wkv"][...]) + value_bias).astype(BF16)
        for i in range(count):
            block = kv.at[quarter[first + i], w]
            block[...] = rows[i * ROWS : (i + 1) * ROWS, :]
            shares.append(links.send(block, block, at.near))
            shares.append(links.send(block, block, at.core))

    def pass_on(i):
        shares[2 * i].wait_recv()
        block = kv.at[quarter[i], at.wy]
        passed.append(links.send(block, block, at.core))

    key_rows(0, 1)
    gather.neighbours()
    key_rows(1, 2)
    weight_q.forward()
    pass_on(0)
    gather.rest()
    d_all = r["d_all"]
    loads[5].wait()
    for copy in arrive_d:
        copy.wait_recv()
    d_all[0:ROWS, :] = r["da"][...].T
    gather_d = GatherZ(links, at, d_all)
    key_rows(3, 1)
    weight_q.ready()
    queries = (nn(x1[...], r["wq"][...]) + bqv[0:1, :]).astype(BF16).astype(F32) * HS**-0.5
    q[...] = interleave(queries.astype(BF16), jnp.zeros((QUARTER, PART), BF16))
    weight_p.forward()
    for i in (1, 2, 3):
        pass_on(i)
    loads[3].wait()
    weight_f = Weight(wf, at.near)
    for i in range(4):
        shares[2 * i + 1].wait_recv()
        passed[i].wait_recv()

    kvt, att, att_t, lse = r["kvt"], r["att"], r["att_t"], r["lse"]

    def keys_of(j, lanes):
        return kv[j, :, :, lanes].reshape(QUARTER, lanes.stop - lanes.start)

    for j in range(4):
        for head in range(HEADS):
            tile = slice(head * 128, (head + 1) * 128)
            kvt[tile, j * QUARTER : (j + 1) * QUARTER] = keys_of(j, tile).T
    stage = r["stage"]
    sum_p = SumZ(links, at, stage, r["parts"], r["over"])

    def attend_chunk(j, slot):
        shift = sub_block(j, w) * ROWS
        apart = jnp.zeros((ROWS, 128), BF16)
        for first, count in ((0, 2), (2, 2), (4, 1)):
            lanes = slice(first * 128, (first + count) * 128)
            query = q[rows_of(slot * ROWS), lanes]
            if count == 2:
                top = jnp.concatenate([query[:, :128], apart], axis=1)
                query = jnp.concatenate([top, jnp.concatenate([apart, query[:, 128:]], axis=1)], axis=0)
            scores = [nt(keys_of(b, lanes), query) for b in range(j + 1)]
            scores[j] = mask_last(scores[j], j, shift)
            peak = functools.reduce(jnp.maximum, [jnp.max(s, axis=0, keepdims=True) for s in scores])
            total, result = 0.0, 0.0
            for b in range(j + 1):
                weights = jnp.exp(scores[b] - peak)
                total = total + column_sum(weights)
                result = result + nn(kvt[lanes, b * QUARTER : (b + 1) * QUARTER], weights.astype(BF16))
            inverse, log_total = 1.0 / total, peak + jnp.log(total)
            for i in range(count):
                head, part = first + i, slice(i * 128, (i + 1) * 128)
                values = result[i * 128 + HS : (i + 1) * 128, part]
                att_t[slot, head * HS : (head + 1) * HS, :] = values * inverse[:, part]
                lse[pl.ds(slot * 8 + head, 1), :] = log_total[:, part]

    gather_d.neighbours()
    weight_p.ready()

    @pl.loop(0, 4)
    def _(i):
        slot = jnp.where(i == 0, 3, jnp.where(i == 3, 0, i))
        j = at.chunk(jnp.where(slot == 3, 2, jnp.where(slot == 2, 3, slot)))
        for case in range(4):
            pl.when(j == case)(functools.partial(attend_chunk, case, slot))
        attended = att_t[slot].T.astype(BF16)
        att[rows_of(slot * ROWS), :] = attended
        stage[slot] = nt(attended, r["wpt"][...]).astype(BF16)
        pl.when(i == 0)(sum_p.send_across)
        pl.when(i == 1)(sum_p.right_bottom.start)
        pl.when(i == 1)(weight_t.forward)
        pl.when(i == 2)(sum_p.left_top.start)
        pl.when(i == 2)(sum_p.join_ahead)
        pl.when(i == 2)(sum_p.join_behind)

    gather_d.rest()
    weight_t.ready()
    weight_f.forward()
    middle = r["x"][...].astype(F32) + vec[4:5, :] + sum_p.result()
    r["middle"][...] = middle
    unit, _ = norm_stats(middle)
    x2, hid, gp = r["x2"], r["hid"], r["gp"]
    x2[0:ROWS, :] = (unit * vec[1:2, :] + vec[3:4, :]).astype(BF16)

    gather = GatherZ(links, at, x2)
    hidden_grad = r["hidden_grad"]
    for t in range(TILES):
        tile = slice(t * 256, (t + 1) * 256)
        hidden_grad[:, tile] = nn(d_all[...], wt[:, tile])
    weight_f.ready()
    stage_g, parts_g = r["stage_g"], r["parts_g"]
    moves = []

    def feed(first, count):
        rows = slice(first * ROWS, (first + count) * ROWS)

        for t in range(TILES):
            tile = slice(t * 256, (t + 1) * 256)
            u = nn(x2[rows, :], wf[:, tile]) + r["bf"][0:1, tile]
            square = u * u
            th = jnp.tanh(GELU_COEF * (u + 0.044715 * square * u))
            hid[rows, tile] = (0.5 * u * (1.0 + th)).astype(BF16)
            slope = 0.5 * (1.0 + th) + 0.5 * u * (1.0 - th * th) * (GELU_COEF * (1.0 + 0.134145 * square))
            gp[rows, tile] = (hidden_grad[rows, tile] * slope).astype(BF16)
        for t in range(TILES):
            tile = slice(t * 256, (t + 1) * 256)
            product = nt(gp[rows, :], wf[tile, :]).astype(BF16)
            for i in range(count):
                stage_g[first + i, :, tile] = product[i * ROWS : (i + 1) * ROWS]
        for i in range(first, first + count):
            if i:
                moves.append(links.send(stage_g.at[i], parts_g.at[i - 1], at.along_z((0, 1, 3, 2)[i])))

    feed(0, 1)
    gather.neighbours()
    feed(1, 2)
    gather.rest()
    feed(3, 1)
    grad_f, grad_t = r["grad_f"], r["grad_t"]

    def gradient_sum(tag, grad, columns, final):
        return GradientSum(
            links, at, grad, columns, r["pair_" + tag], r["strips_" + tag], r["cross_" + tag], final
        )

    @pl.loop(0, TILES)
    def _(t):
        grad_t[tile_of(t, 256), :] = tn(d_all[:, tile_of(t, 256)], hid[...]).astype(BF16)

    whole = slice(0, D)
    sum_t = gradient_sum("t", grad_t, whole, fin_t)
    sum_t.send_core()

    @pl.loop(0, TILES)
    def _(t):
        grad_f[tile_of(t, 256), :] = tn(x2[:, tile_of(t, 256)], gp[...]).astype(BF16)

    sum_f = GradientSumY(links, at, grad_f, r["pair_f"], r["cross_f"], r["strips_f"], r["half_f"], fin_f)
    sum_f.send_core()
    sum_t.send_x_by_neighbours()
    unit, scale = norm_stats(r["middle"][...])
    grad = d_all[0:ROWS, :].astype(F32)
    grad_normed = stage_g[0].astype(F32)
    for i in range(3):
        moves[i].wait_recv()
        grad_normed = grad_normed + parts_g[i].astype(F32)
    grad_middle = grad + norm_gradient(grad_normed, unit, scale, vec[1:2, :])
    r["gm"][...] = grad_middle
    branch = grad_middle.astype(BF16)
    g_all = r["g_all"]
    g_all[0:ROWS, :] = branch
    gather = GatherZ(links, at, g_all)
    sums = r["sums"]
    sums[1:2, :] = column_sum(grad_normed * unit)
    sums[3:4, :] = column_sum(grad_normed)
    sums[4:5, :] = column_sum(grad)
    sums[5:6, :] = column_sum(branch.astype(F32))
    sums[8:9, :] = column_sum(gp[...].astype(F32))
    sum_f.send_y()
    sum_p.sent()
    sum_b = SumZ(links, at, stage, r["parts_b"], r["over_b"])

    @pl.loop(0, TILES)
    def _(t):
        product = nt(hid[...], wt[tile_of(t, 256), :]).astype(BF16)
        for i in range(4):
            stage[i, :, tile_of(t, 256)] = product[i * ROWS : (i + 1) * ROWS]


    dkv, go, dq, dq_t, delta = r["dkv"], r["go"], r["dq"], att_t, r["delta"]
    take, take_y, gkv = r["take"], r["take_y"], r["gkv"]
    dkv[...] = jnp.zeros(dkv.shape, BF16)

    def rows_back(first, count):
        rows = slice(first * ROWS, (first + count) * ROWS)
        grad = nn(g_all[rows, :], r["wpt"][...]).astype(BF16)
        go[rows, :] = interleave(jnp.zeros((count * ROWS, PART), BF16), grad)
        for i in range(count):
            slot = first + i
            both = grad[i * ROWS : (i + 1) * ROWS, :].astype(F32).T * att_t[slot]
            delta[slot * 8 : slot * 8 + HEADS, :] = jnp.sum(both.reshape(HEADS, HS, ROWS), axis=1)

    shared = links.reserve(3 * HEADS)

    def head_move(kind, head):
        source = dkv.at[head, :, (at.wyc, at.wc, at.wy)[kind]]
        target = take_y.at[head] if kind == 2 else take.at[1 - kind, head]
        return links.make(shared + kind * HEADS + head, source, target, at.near if kind == 2 else at.core)

    def cross_head(head):
        head_move(0, head).wait_recv()
        for j in range(4):
            both = dkv[head, j, at.wy].astype(F32) + take[1, head, j].astype(F32)
            dkv[head, j, at.wy] = both.astype(BF16)
        head_move(2, head).start()

    def back_chunk(j, slot):
        rows = rows_of(slot * ROWS)

        @pl.loop(0, HEADS)
        def _(head):
            tile = tile_of(head, 128)
            side = jnp.concatenate([q[rows, tile], go[rows, tile]], axis=0)
            log_total = lse[pl.ds(slot * 8 + head, 1), :]
            inner = delta[pl.ds(slot * 8 + head, 1), :]
            grads = []
            for b in range(j + 1):
                products = nt(kv[b, :, :, tile].reshape(QUARTER, 128), side)
                scores = products[:, :128]
                if b == j:
                    scores = mask_last(scores, j, sub_block(j, w) * ROWS)
                probs = jnp.exp(scores - log_total)
                grads.append((probs * (products[:, 128:] - inner)).astype(BF16))
                both = nn(jnp.concatenate([grads[b], probs.astype(BF16)], axis=1), side)
                both = dkv[head, b].reshape(QUARTER, 128).astype(F32) + both
                dkv[head, b] = both.astype(BF16).reshape(4, ROWS, 128)
            result = nn(kvt[tile, 0 : (j + 1) * QUARTER], jnp.concatenate(grads, axis=0))
            dq_t[slot, tile_of(head, HS), :] = result[:HS, :] * HS**-0.5
            pl.when(slot == 3)(lambda: head_move(0, head).start())

    def near_back():
        gather.neighbours()
        rows_back(1, 2)

    for copy in moves:
        copy.wait_send()
    rows_back(0, 1)

    sum_t.relay_x()

    def far_back():
        gather.rest()
        rows_back(3, 1)
        sum_b.send_across()
        sum_b.send_near()

    @pl.loop(0, 4)
    def _(slot):
        pl.when(slot == 1)(near_back)
        pl.when(slot == 3)(far_back)
        j = at.chunk(jnp.where(slot == 2, 3, jnp.where(slot == 3, 2, slot)))
        for case in range(4):
            pl.when(j == case)(functools.partial(back_chunk, case, slot))

    for slot in range(4):
        dq[slot * ROWS : (slot + 1) * ROWS, :] = dq_t[slot].T.astype(BF16)
    for head in range(HEADS):
        cross_head(head)
    for head in range(HEADS):
        head_move(1, head).start()
    sum_f.send_x()
    slots = []
    for j in range(4):
        k = lax.rem(j + 4 - h, 4)
        slots.append(jnp.where(k == 2, 3, jnp.where(k == 3, 2, k)))
    keep = []

    def send_back(total, passing=False):
        strip = total.send_back(passing)
        copy = pltpu.make_async_copy(total.total[0], strip, local.at[7 + len(keep)])
        copy.start()
        keep.append(copy)

    def send_rows(back, target):
        place = target.at[:, rows_of(mine * ROWS)]
        keep = pltpu.make_async_copy(back.at[block_of(w)], place, local.at[6])
        keep.start()
        copies = [links.send(back.at[block_of(peer)], place, device) for device, peer in at.width_peers]
        keep.wait()
        return copies

    sum_t.sent_core()

    @pl.loop(0, TILES)
    def _(t):
        tile = tile_of(t, 256)
        pieces = [tn(x1[:, tile], dq[...]).astype(BF16), tn(g_all[:, tile], att[...]).astype(BF16)]
        grad_t[tile, PAIR:] = jnp.concatenate(pieces, axis=1)

    sum_q = gradient_sum("q", grad_t, slice(PAIR, D), fin_q)
    sum_q.send_core()
    sum_t.send_far()
    sums[9:10, 0:PART] = column_sum(dq[...].astype(F32))
    sum_b.join_ahead()
    sum_b.join_behind()
    sum_q.send_x()
    sum_f.send_back()
    result = r["middle"][...] + vec[5:6, :] + sum_b.result()
    r["xa"][...] = result.astype(BF16).T
    returns = send_rows(r["xa"], bo)

    for head in range(HEADS):
        tile = slice(head * 128, (head + 1) * 128)
        head_move(1, head).wait_recv()
        head_move(2, head).wait_recv()
        for j in range(4):
            total = dkv[head, j, w].astype(F32) + take[0, head, j].astype(F32) + take_y[head, j].astype(F32)
            gkv[rows_of(slots[j] * ROWS), tile] = total.astype(BF16)


    @pl.loop(0, TILES)
    def _(t):
        tile = tile_of(t, 256)
        grad_t[tile, 0:PAIR] = tn(x1[:, tile], gkv[...]).astype(BF16)

    sum_k = gradient_sum("k", grad_t, slice(0, PAIR), fin_k)
    sum_k.send_core()
    sum_t.send_opposite()
    sum_b.sent()
    sum_l = SumZ(links, at, stage, r["parts"], r["over"])

    def first_partial(first, count):
        rows = slice(first * ROWS, (first + count) * ROWS)
        product = (nt(dq[rows, :], r["wq"][...]) + nt(gkv[rows, :], r["wkv"][...])).astype(BF16)
        for i in range(count):
            stage[first + i] = product[i * ROWS : (i + 1) * ROWS]

    first_partial(3, 1)
    sum_l.send_across()
    first_partial(1, 2)
    sum_l.send_near()
    grad_values = column_sum(gkv[...].astype(F32))
    for head in range(HEADS):
        sums[9:10, PART + head * HS : PART + (head + 1) * HS] = grad_values[:, head * 128 + HS : (head + 1) * 128]
    sums[9:10, PAIR:] = jnp.zeros((1, PAIR), F32)
    sums[10:16, :] = jnp.zeros((6, D), F32)
    sums[6:8, :] = jnp.zeros((2, D), F32)
    over_v = [links.send(sums.at[8:16], r["take_v"].at[i], at.width_peers[i][0]) for i in range(3)]
    sum_k.send_x()
    keep.append(sum_f.send_opposite(local.at[7 + len(keep)]))
    sum_l.join_ahead()
    sum_l.join_behind()
    first_partial(0, 1)
    sum_q.send_y()
    send_back(sum_t, True)
    grad_normed = sum_l.result()
    unit, scale = norm_stats(r["x"][...].astype(F32))
    sums[0:1, :] = column_sum(grad_normed * unit)
    sums[2:3, :] = column_sum(grad_normed)
    for part in range(4):
        r["sums_w"][part] = sums[0:8, part * PART : (part + 1) * PART]
    over_w = [
        links.send(r["sums_w"].at[peer], r["take_w"].at[i], device)
        for i, (device, peer) in enumerate(at.width_peers)
    ]
    result = r["gm"][...] + norm_gradient(grad_normed, unit, scale, vec[0:1, :])
    r["da"][...] = result.astype(BF16).T
    returns += send_rows(r["da"], dt)
    sum_t.pass_back()
    send_back(sum_q)

    for copy in over_w + over_v:
        copy.wait_recv()
    sums_d = r["sums_d"]
    normed = r["sums_w"][w] + r["take_w"][0] + r["take_w"][1] + r["take_w"][2]
    biases = sums[8:10, :] + r["take_v"][0, 0:2] + r["take_v"][1, 0:2] + r["take_v"][2, 0:2]
    r["sums_n"][...] = normed
    over_z = [links.send(r["sums_n"], r["sums_z"].at[k - 1], at.along_z(k)) for k in (1, 2, 3)]
    sum_k.send_y()
    for copy in over_z:
        copy.wait_recv()
    normed = r["sums_n"][...] + r["sums_z"][0] + r["sums_z"][1] + r["sums_z"][2]
    sums_d[...] = jnp.zeros((8, D), F32)
    for i in range(6):
        sums_d[i // 3 : i // 3 + 1, (i % 3) * 384 : (i % 3) * 384 + PART] = normed[i : i + 1, :]
    sums_d[2:4, :] = biases
    over_x = [links.send(sums_d, r["sums_x"].at[i], device) for i, device in enumerate(at.dp_peers)]
    send_back(sum_k)
    total = sums_d[...]
    for i, copy in enumerate(over_x):
        copy.wait_recv()
        total = total + r["sums_x"][i]
    fin_v[...] = total
    for copy in keep:
        copy.wait()
    for total in (sum_t, sum_f, sum_q, sum_k):
        total.finish()
    for copy in returns:
        copy.wait()
    for kind in range(3):
        for head in range(HEADS):
            head_move(kind, head).wait_send()
    for copy in links.copies:
        copy.wait_send()


def block(*inputs):
    return pl.pallas_call(
        block_kernel,
        name="block",
        out_shape=(
            jax.ShapeDtypeStruct((PART, QUARTER), BF16),
            jax.ShapeDtypeStruct((PART, QUARTER), BF16),
            jax.ShapeDtypeStruct((PART, D), BF16),
            jax.ShapeDtypeStruct((PART, D), BF16),
            jax.ShapeDtypeStruct((PART, PAIR), BF16),
            jax.ShapeDtypeStruct((PART, PAIR), BF16),
            jax.ShapeDtypeStruct((8, D), F32),
        ),
        in_specs=[ANY, ANY, VMEM, VMEM, VMEM, VMEM, ANY, VMEM, ANY, ANY, VMEM, ANY],
        out_specs=(ANY, ANY, ANY, ANY, ANY, ANY, VMEM),
        scratch_shapes=[pltpu.VMEM(shape, kind) for shape, kind in SCRATCH.values()]
        + [pltpu.SemaphoreType.DMA((COPIES,)), pltpu.SemaphoreType.DMA((COPIES,)), pltpu.SemaphoreType.DMA((12,))],
        compiler_params=pltpu.CompilerParams(collective_id=1, has_side_effects=True, vmem_limit_bytes=64 * 2**20),
    )(*inputs)


def finish_kernel(*refs):
    inputs, outputs, (f, t, qp, kv, d_wa, d_wp, d_wf, d_wo, rows_b, rows_d, sems) = refs[:7], refs[7:19], refs[19:]
    bo, dt, f_in, t_in, qp_in, kv_in, v = inputs
    out, d_tok, gain, shift, wa_out, d_bqv, wp_out, d_bp, wf_out, d_bf, wo_out, d_bo = outputs
    loads = [
        pltpu.make_async_copy(source, target, sems.at[i])
        for i, (source, target) in enumerate(((t_in, t), (f_in, f), (qp_in, qp), (kv_in, kv), (bo, rows_b), (dt, rows_d)))
    ]
    stores = [
        pltpu.make_async_copy(source, target, sems.at[6 + i])
        for i, (source, target) in enumerate(
            ((rows_b, out), (rows_d, d_tok), (d_wo, wo_out), (d_wf, wf_out), (d_wa, wa_out), (d_wp, wp_out))
        )
    ]
    for copy in loads:
        copy.start()
    loads[0].wait()
    d_wo[...] = t[...].astype(F32)
    stores[2].start()
    loads[1].wait()
    d_wf[...] = f[...].astype(F32)
    stores[3].start()
    loads[2].wait()
    d_wa[0] = qp[:, :PART].astype(F32)
    d_wp[...] = qp[:, PART:].astype(F32).T
    stores[5].start()
    loads[3].wait()
    both = kv[...].astype(F32)
    d_wa[1] = jnp.concatenate([both[:, head * 128 : head * 128 + HS] for head in range(HEADS)], axis=1)
    d_wa[2] = jnp.concatenate([both[:, head * 128 + HS : (head + 1) * 128] for head in range(HEADS)], axis=1)
    stores[4].start()
    for i in range(2):
        loads[4 + i].wait()
        stores[i].start()
    rows = [v[i // 3 : i // 3 + 1, (i % 3) * 384 : (i % 3) * 384 + PART] for i in range(6)]
    gain[0:1, :] = rows[0]
    gain[1:2, :] = rows[1]
    shift[0:1, :] = rows[2]
    shift[1:2, :] = rows[3]
    d_bo[...] = rows[4].reshape(PART)
    d_bp[...] = rows[5].reshape(PART)
    d_bf[...] = v[2:3, :].reshape(D)
    d_bqv[0:1, :] = v[3:4, 0:PART]
    d_bqv[1:2, :] = v[3:4, PART:PAIR]
    for copy in stores:
        copy.wait()


def finish(*inputs):
    shapes = [
        ((PART, QUARTER), BF16),
        ((PART, QUARTER), BF16),
        ((2, PART), F32),
        ((2, PART), F32),
        ((3, PART, PART), F32),
        ((2, PART), F32),
        ((PART, PART), F32),
        ((PART,), F32),
        ((PART, D), F32),
        ((D,), F32),
        ((PART, D), F32),
        ((PART,), F32),
    ]
    return pl.pallas_call(
        finish_kernel,
        name="finish",
        out_shape=[jax.ShapeDtypeStruct(shape, kind) for shape, kind in shapes],
        in_specs=[ANY] * 6 + [VMEM],
        out_specs=[ANY, ANY, VMEM, VMEM, ANY, VMEM, ANY, VMEM, ANY, VMEM, ANY, VMEM],
        scratch_shapes=[
            pltpu.VMEM((PART, D), BF16),
            pltpu.VMEM((PART, D), BF16),
            pltpu.VMEM((PART, PAIR), BF16),
            pltpu.VMEM((PART, PAIR), BF16),
            pltpu.VMEM((3, PART, PART), F32),
            pltpu.VMEM((PART, PART), F32),
            pltpu.VMEM((PART, D), F32),
            pltpu.VMEM((PART, D), F32),
            pltpu.VMEM((PART, QUARTER), BF16),
            pltpu.VMEM((PART, QUARTER), BF16),
            pltpu.SemaphoreType.DMA((12,)),
        ],
        compiler_params=pltpu.CompilerParams(vmem_limit_bytes=63 * 2**20),
    )(*inputs)


def shards(tokens, ln_gain, ln_bias, w_attn, b_qv, w_proj, b_proj, w_fc, b_fc, w_out, b_out, d_out):
    parts = block(tokens.T, d_out.T, ln_gain, ln_bias, b_proj, b_out, w_attn, b_qv, w_proj, w_fc, b_fc, w_out.T)
    results = list(finish(*parts))
    for i in (0, 1, 10):
        results[i] = results[i].T
    return tuple(results)


def solution(mesh):
    in_specs = (
        P(("dp", "heads"), "width"),
        P(None, "width"),
        P(None, "width"),
        P(None, "width", "heads"),
        P(None, "heads"),
        P("heads", "width"),
        P("width"),
        P("width", "heads"),
        P("heads"),
        P("heads", "width"),
        P("width"),
        P(("dp", "heads"), "width"),
    )
    out_specs = (
        P(("dp", "heads"), "width"),
        P(("dp", "heads"), "width"),
        P(None, "width"),
        P(None, "width"),
        P(None, "width", "heads"),
        P(None, "heads"),
        P("heads", "width"),
        P("width"),
        P("width", "heads"),
        P("heads"),
        P("heads", "width"),
        P("width"),
    )
    return jax.shard_map(shards, mesh=mesh, in_specs=in_specs, out_specs=out_specs, check_vma=False)
```

```python
import functools

import jax
import jax.numpy as jnp
from jax import lax
from jax.experimental import pallas as pl
from jax.experimental.pallas import tpu as pltpu
from jax.sharding import PartitionSpec as P

F32, BF16 = jnp.float32, jnp.bfloat16
D, HS, ROWS, PART, QUARTER, HEADS = 1280, 64, 128, 320, 512, 5
PAIR = 2 * PART
STRIP = PART // 4
HALF = ROWS // 2
EPSILON = 1e-05
GELU_COEF = 0.7978845608028654
MASKED = -1e30
VMEM = pl.BlockSpec(memory_space=pltpu.VMEM)
ANY = pl.BlockSpec(memory_space=pl.ANY)
TILES = D // 256


def nn(a, b):
    return jnp.dot(a, b, preferred_element_type=F32)


def nt(a, b):
    return lax.dot_general(a, b, (((1,), (1,)), ((), ())), preferred_element_type=F32)


def tn(a, b):
    return lax.dot_general(a, b, (((0,), (0,)), ((), ())), preferred_element_type=F32)


def rows_of(start, size=ROWS):
    return pl.ds(pl.multiple_of(start, size), size)


def block_of(who):
    return pl.ds(pl.multiple_of(who * PART, 64), PART)


def tile_of(i, size):
    return pl.ds(pl.multiple_of(i * size, size), size)


def sub_block(quarter, w):
    return w + lax.rem(quarter, 2) * (3 - 2 * w)


class Place:
    def __init__(self):
        self.dp, self.w, self.h = (lax.axis_index(n) for n in ("dp", "width", "heads"))
        self.x = lax.rem(self.dp, 4)
        self.wc = self.w + 1 - 2 * lax.rem(self.w, 2)
        self.wy = lax.rem(self.w + 2, 4)
        self.wyc = lax.rem(self.wc + 2, 4)
        across = lax.rem(self.dp + 4, 8)
        self.core = (self.dp, self.wc, self.h)
        self.near = (self.dp, self.wy, self.h)
        self.near_core = (self.dp, self.wyc, self.h)
        self.far = (across, self.wy, self.h)
        self.opposite = (across, self.w, self.h)
        self.width_peers = ((self.near, self.wy), (self.near_core, self.wyc), (self.core, self.wc))

        beyond = lax.rem(self.dp + 4, 8) - self.x
        self.dp_peers = [self.along_x(k) for k in (1, 2, 3)] + [self.opposite]
        self.dp_peers += [(beyond + lax.rem(self.x + k, 4), self.w, self.h) for k in (1, 2, 3)]

    def along_z(self, k):
        return (self.dp, self.w, lax.rem(self.h + k, 4))

    def along_x(self, k):
        return (self.dp - self.x + lax.rem(self.x + k, 4), self.w, self.h)

    def chunk(self, k):
        return lax.rem(self.h + k, 4)


def greet(devices):
    barrier = pltpu.get_barrier_semaphore()
    for device in devices:
        pl.semaphore_signal(barrier, inc=1, device_id=device, device_id_type=pl.DeviceIdType.MESH)
    pl.semaphore_wait(barrier, len(devices))


class Move:
    def __init__(self, copy):
        self.copy, self.left = copy, False
        self.start, self.wait_recv = copy.start, copy.wait_recv

    def wait_send(self):
        if not self.left:
            self.copy.wait_send()
        self.left = True

    def wait(self):
        self.wait_recv()
        self.wait_send()


class Links:
    def __init__(self, sent, landed):
        self.sent, self.landed, self.copies, self.count = sent, landed, [], 0

    def reserve(self, count):
        self.count += count
        return self.count - count

    def make(self, i, source, target, device):
        return pltpu.make_async_remote_copy(
            src_ref=source,
            dst_ref=target,
            send_sem=self.sent.at[i],
            recv_sem=self.landed.at[i],
            device_id=device,
            device_id_type=pl.DeviceIdType.MESH,
        )

    def plan(self, source, target, device):
        self.copies.append(Move(self.make(self.reserve(1), source, target, device)))
        return self.copies[-1]

    def send(self, source, target, device):
        copy = self.plan(source, target, device)
        copy.start()
        return copy


class GatherZ:
    def __init__(self, links, at, rows):
        right, left = at.along_z(1), at.along_z(3)
        own, ahead, behind = (rows.at[pl.ds(i * ROWS, ROWS)] for i in range(3))
        self.right = links.send(own, behind, right)
        self.left = links.send(own, ahead, left)
        self.low = links.plan(
            rows.at[pl.ds(2 * ROWS, HALF)], rows.at[pl.ds(3 * ROWS, HALF)], right
        )
        self.high = links.plan(
            rows.at[pl.ds(ROWS + HALF, HALF)], rows.at[pl.ds(3 * ROWS + HALF, HALF)], left
        )

    def neighbours(self):
        self.left.wait_recv()
        self.high.start()
        self.right.wait_recv()
        self.low.start()

    def rest(self):
        self.low.wait_recv()
        self.high.wait_recv()


class SumZ:
    def __init__(self, links, at, stage, parts, over):
        self.stage, self.parts, self.over = stage, parts, over
        right, left = at.along_z(1), at.along_z(3)
        top, bottom = pl.ds(0, HALF), pl.ds(HALF, HALF)
        self.far_right = links.plan(stage.at[3, top], over.at[0], right)
        self.far_left = links.plan(stage.at[3, bottom], over.at[1], left)
        self.right_bottom = links.plan(stage.at[1, bottom], parts.at[0, bottom], right)
        self.right_top = links.plan(stage.at[1, top], parts.at[0, top], right)
        self.left_top = links.plan(stage.at[2, top], parts.at[1, top], left)
        self.left_bottom = links.plan(stage.at[2, bottom], parts.at[1, bottom], left)

    def sent(self):
        for copy in (self.far_right, self.far_left, self.right_bottom, self.right_top, self.left_top, self.left_bottom):
            copy.wait_send()

    def send_across(self):
        self.far_right.start()
        self.far_left.start()

    def send_near(self):
        self.right_bottom.start()
        self.left_top.start()

    def join_ahead(self):
        self.far_right.wait_recv()
        joined = self.stage[1, 0:HALF, :].astype(F32) + self.over[0].astype(F32)
        self.stage[1, 0:HALF, :] = joined.astype(BF16)
        self.right_top.start()

    def join_behind(self):
        self.far_left.wait_recv()
        joined = self.stage[2, HALF:, :].astype(F32) + self.over[1].astype(F32)
        self.stage[2, HALF:, :] = joined.astype(BF16)
        self.left_bottom.start()

    def result(self):
        for copy in (self.right_bottom, self.right_top, self.left_top, self.left_bottom):
            copy.wait_recv()
        return self.stage[0].astype(F32) + self.parts[0].astype(F32) + self.parts[1].astype(F32)


class GradientSum:
    def __init__(self, links, at, grad, columns, pair, strips, cross, final):
        self.links, self.at, self.grad, self.columns = links, at, grad, columns
        self.pair, self.strips, self.cross, self.final = pair, strips, cross, final
        self.strip = rows_of(at.x * STRIP, STRIP)
        self.total = [pair.at[0, self.strip], pair.at[1, self.strip]]

    def mine(self, who):
        return self.grad.at[block_of(who), self.columns]

    def send_core(self):
        at, links = self.at, self.links
        self.core = [
            links.send(self.mine(at.wc), self.pair.at[0], at.core),
            links.send(self.mine(at.wyc), self.pair.at[1], at.core),
        ]

    def sent_core(self):
        for copy in self.core:
            copy.wait_send()

    def add_core(self):
        for i, who in ((0, self.at.w), (1, self.at.wy)):
            self.core[i].wait_recv()
            self.pair[i] = (self.pair[i].astype(F32) + self.mine(who)[...].astype(F32)).astype(BF16)

    def send_x(self):
        at, links = self.at, self.links
        self.add_core()
        self.along = [
            links.send(
                self.pair.at[:, rows_of(lax.rem(at.x + k, 4) * STRIP, STRIP)], self.strips.at[k - 1], at.along_x(k)
            )
            for k in (2, 1, 3)
        ]

    def send_x_by_neighbours(self):
        at, links = self.at, self.links
        self.add_core()
        right, left = at.along_x(1), at.along_x(3)
        ahead, across, behind = (rows_of(lax.rem(at.x + k, 4) * STRIP, STRIP) for k in (1, 2, 3))
        parts, over = self.strips, self.strips.at[2]
        self.over_x = [
            links.send(self.pair.at[0, across], over.at[0], right),
            links.send(self.pair.at[1, across], over.at[1], left),
        ]
        self.along = [
            links.send(self.pair.at[1, ahead], parts.at[0, 1], right),
            links.send(self.pair.at[0, behind], parts.at[1, 0], left),
            links.plan(self.pair.at[0, ahead], parts.at[0, 0], right),
            links.plan(self.pair.at[1, behind], parts.at[1, 1], left),
        ]
        self.relayed = (self.pair.at[0, ahead], self.pair.at[1, behind])

    def relay_x(self):
        for i in range(2):
            self.over_x[i].wait_recv()
            joined = self.relayed[i][...].astype(F32) + self.strips[2, i].astype(F32)
            self.relayed[i][...] = joined.astype(BF16)
            self.along[2 + i].start()

    def add_strips(self):
        for copy in self.along:
            copy.wait_recv()
        for i in range(2):
            joined = self.total[i][...].astype(F32)
            for k in range(3 if len(self.along) == 3 else 2):
                joined = joined + self.strips[k, i].astype(F32)
            self.total[i][...] = joined.astype(BF16)

    def send_y(self):
        self.add_strips()
        self.over = [
            self.links.send(self.total[1], self.cross.at[0], self.at.near),
            self.links.send(self.total[1], self.cross.at[1], self.at.far),
            self.links.send(self.total[0], self.cross.at[2], self.at.opposite),
        ]

    def send_far(self):
        self.add_strips()
        self.over = [self.links.send(self.total[1], self.cross.at[0], self.at.far)]

    def send_opposite(self):
        self.over[0].wait()
        joined = self.total[0][...].astype(F32) + self.cross[0].astype(F32)
        self.total[0][...] = joined.astype(BF16)
        self.over = [self.links.send(self.total[0], self.cross.at[1], self.at.opposite)]

    def send_back(self, passing):
        at, links = self.at, self.links
        joined = self.total[0][...].astype(F32)
        for copy in self.over:
            copy.wait()
        places = (0, 1, 2) if len(self.over) == 3 else (1,)
        for place in places:
            joined = joined + self.cross[place].astype(F32)
        self.total[0][...] = joined.astype(BF16)
        strip = self.final.at[self.strip]
        self.back = [links.send(self.total[0], strip, at.along_x(k)) for k in ((1, 3) if passing else (2, 1, 3))]
        self.passing = passing
        return strip

    def pass_back(self):
        at, links = self.at, self.links
        behind, ahead = lax.rem(at.x + 3, 4) * STRIP, lax.rem(at.x + 1, 4) * STRIP
        first = self.final.at[pl.ds(pl.multiple_of(behind, 16), 48)]
        second = self.final.at[pl.ds(pl.multiple_of(ahead + 48, 16), 32)]
        self.back[0].wait_recv()
        self.back[1].wait_recv()
        self.back = [
            links.send(first, first, at.along_x(1)),
            links.send(second, second, at.along_x(3)),
        ]

    def finish(self):
        for copy in self.back:
            copy.wait_recv()


class GradientSumY:
    def __init__(self, links, at, grad, pair, cross, strips, half, final):
        self.links, self.at, self.grad = links, at, grad
        self.pair, self.cross, self.strips, self.half, self.final = pair, cross, strips, half, final
        part = at.dp // 4
        self.kept = pl.ds(pl.multiple_of(part * PAIR, PAIR), PAIR)
        self.given = pl.ds(pl.multiple_of((1 - part) * PAIR, PAIR), PAIR)
        self.strip = rows_of(at.x * STRIP, STRIP)

    def mine(self, who):
        return self.grad.at[block_of(who)]

    def send_core(self):
        at, links = self.at, self.links
        self.core = [
            links.send(self.mine(at.wc), self.pair.at[0], at.core),
            links.send(self.mine(at.wyc), self.pair.at[1], at.core),
        ]

    def send_y(self):
        at, links = self.at, self.links
        for i, who in ((0, at.w), (1, at.wy)):
            self.core[i].wait_recv()
            self.pair[i] = (self.pair[i].astype(F32) + self.mine(who)[...].astype(F32)).astype(BF16)
        self.over = [
            links.send(self.pair.at[1, :, self.kept], self.cross.at[0], at.near),
            links.send(self.pair.at[1, :, self.given], self.cross.at[1], at.far),
            links.send(self.pair.at[0, :, self.given], self.cross.at[2], at.opposite),
        ]

    def send_x(self):
        at, links = self.at, self.links
        joined = self.pair[0, :, self.kept].astype(F32)
        for k in range(3):
            self.over[k].wait_recv()
            joined = joined + self.cross[k].astype(F32)
        self.pair[0, :, self.kept] = joined.astype(BF16)
        self.along = [
            links.send(
                self.pair.at[0, rows_of(lax.rem(at.x + k, 4) * STRIP, STRIP), self.kept],
                self.strips.at[k - 1],
                at.along_x(k),
            )
            for k in (2, 1, 3)
        ]

    def send_back(self):
        at, links = self.at, self.links
        joined = self.pair[0, self.strip, self.kept].astype(F32)
        for copy in self.along:
            copy.wait_recv()
        for k in range(3):
            joined = joined + self.strips[k].astype(F32)
        self.half[self.strip, :] = joined.astype(BF16)
        place = self.half.at[self.strip]
        self.back = [links.send(place, place, at.along_x(k)) for k in (2, 1, 3)]

    def send_opposite(self, sem):
        for copy in self.back:
            copy.wait_recv()
        place = self.final.at[:, self.kept]
        self.last = self.links.send(self.half, place, self.at.opposite)
        keep = pltpu.make_async_copy(self.half, place, sem)
        keep.start()
        return keep

    def finish(self):
        self.last.wait_recv()


def norm_stats(values):
    mean = jnp.mean(values, axis=1, keepdims=True)
    centred = values - mean
    scale = lax.rsqrt(jnp.mean(centred * centred, axis=1, keepdims=True) + EPSILON)
    return centred * scale, scale


def norm_gradient(grad, unit, scale, gain):
    scaled = grad * gain
    mean = jnp.mean(scaled, axis=1, keepdims=True)
    along = jnp.mean(scaled * unit, axis=1, keepdims=True)
    return scale * (scaled - mean - unit * along)


def interleave(first, second):
    pieces = []
    for head in range(HEADS):
        part = slice(head * HS, (head + 1) * HS)
        pieces += [first[:, part], second[:, part]]
    return jnp.concatenate(pieces, axis=1)


def mask_last(scores, quarter, shift, start=0):
    shape = (scores.shape[0] // ROWS, ROWS, ROWS)
    owner = start + lax.broadcasted_iota(jnp.int32, shape, 0)
    if quarter % 2:
        owner = 3 - owner
    key = owner * ROWS + lax.broadcasted_iota(jnp.int32, shape, 1)
    query = lax.broadcasted_iota(jnp.int32, shape, 2) + shift
    seen = (key <= query).reshape(scores.shape[0], ROWS)
    parts = [scores[:, i * ROWS : (i + 1) * ROWS] for i in range(scores.shape[1] // ROWS)]
    parts = [jnp.where(seen, part, MASKED) for part in parts]
    return parts[0] if len(parts) == 1 else jnp.concatenate(parts, axis=1)


def column_sum(values):
    return jnp.sum(values, axis=0, keepdims=True)


SCRATCH = dict(
    wkv=((D, PAIR), BF16),
    wq=((D, PART), BF16),
    wpt=((D, PART), BF16),
    wf=((D, D), BF16),
    wt=((D, D), BF16),
    wa_raw=((3, PART, PART), BF16),
    wp_raw=((PART, PART), BF16),
    xa=((D, ROWS), BF16),
    da=((D, ROWS), BF16),
    vl=((8, PART), F32),
    vg=((4, 8, PART), F32),
    vec=((8, D), F32),
    bf=((8, D), F32),
    x=((ROWS, D), BF16),
    x1=((QUARTER, D), BF16),
    q=((QUARTER, PAIR), BF16),
    kv=((4, 4, ROWS, PAIR), BF16),
    kvt=((PAIR, 2048), BF16),
    att=((QUARTER, PART), BF16),
    att_t=((4, PART, ROWS), F32),
    lse=((32, 128), F32),
    delta=((32, 128), F32),
    middle=((ROWS, D), F32),
    stage=((4, ROWS, D), BF16),
    parts=((2, ROWS, D), BF16),
    over=((2, HALF, D), BF16),
    d_all=((QUARTER, D), BF16),
    x2=((QUARTER, D), BF16),
    hidden_grad=((QUARTER, D), F32),
    hid=((QUARTER, D), BF16),
    gp=((QUARTER, D), BF16),
    stage_g=((4, ROWS, D), BF16),
    parts_g=((3, ROWS, D), BF16),
    parts_b=((2, ROWS, D), BF16),
    over_b=((2, HALF, D), BF16),
    gm=((ROWS, D), F32),
    grad_f=((D, D), BF16),
    grad_t=((D, D), BF16),
    pair_f=((2, PART, D), BF16),
    pair_t=((2, PART, D), BF16),
    pair_q=((2, PART, PAIR), BF16),
    pair_k=((2, PART, PAIR), BF16),
    strips_f=((3, STRIP, PAIR), BF16),
    half_f=((PART, PAIR), BF16),
    strips_t=((3, 2, STRIP, D), BF16),
    strips_q=((3, 2, STRIP, PAIR), BF16),
    strips_k=((3, 2, STRIP, PAIR), BF16),
    cross_f=((3, PART, PAIR), BF16),
    cross_t=((3, STRIP, D), BF16),
    cross_q=((3, STRIP, PAIR), BF16),
    cross_k=((3, STRIP, PAIR), BF16),
    g_all=((QUARTER, D), BF16),
    go=((QUARTER, PAIR), BF16),
    dkv=((HEADS, 4, 4, ROWS, 128), BF16),
    take=((2, HEADS, 4, ROWS, 128), BF16),
    take_y=((HEADS, 4, ROWS, 128), BF16),
    dq=((QUARTER, PART), BF16),
    gkv=((QUARTER, PAIR), BF16),
    sums=((16, D), F32),
    sums_n=((8, PART), F32),
    sums_z=((3, 8, PART), F32),
    sums_w=((4, 8, PART), F32),
    take_w=((3, 8, PART), F32),
    take_v=((3, 8, D), F32),
    sums_d=((8, D), F32),
    sums_x=((7, 8, D), F32),
)
COPIES = 176


def block_kernel(*refs):
    names = ("tok", "dout", "gain", "shift", "b_proj", "b_out", "wa_in", "bqv", "wp_in", "wf_in", "b_fc", "wo_in")
    names += ("bo", "dt", "fin_f", "fin_t", "fin_q", "fin_k", "fin_v")
    names += tuple(SCRATCH) + ("sent", "landed", "local")
    r = dict(zip(names, refs))
    (tok, dout, gain, shift, b_proj, b_out, wa_in, bqv, wp_in, wf_in, b_fc, wo_in) = refs[:12]
    (bo, dt, fin_f, fin_t, fin_q, fin_k, fin_v) = refs[12:19]
    at = Place()
    w, h = at.w, at.h
    links = Links(r["sent"], r["landed"])
    local = r["local"]
    mine = sub_block(h, w)
    vec = r["vec"]

    wf, wt = r["wf"], r["wt"]
    loads = [
        pltpu.make_async_copy(wa_in, r["wa_raw"], local.at[0]),
        pltpu.make_async_copy(wp_in, r["wp_raw"], local.at[1]),
        pltpu.make_async_copy(wo_in, wt.at[block_of(w)], local.at[2]),
        pltpu.make_async_copy(wf_in, wf.at[block_of(w)], local.at[3]),
        pltpu.make_async_copy(tok.at[:, rows_of(mine * ROWS)], r["xa"].at[block_of(w)], local.at[4]),
        pltpu.make_async_copy(dout.at[:, rows_of(mine * ROWS)], r["da"].at[block_of(w)], local.at[5]),
    ]
    for copy in loads:
        copy.start()
    vl = r["vl"]
    vl[0:2, :] = gain[...]
    vl[2:4, :] = shift[...]
    vl[4:5, :] = b_proj[...].reshape(1, PART)
    vl[5:6, :] = b_out[...].reshape(1, PART)
    vl[6:8, :] = jnp.zeros((2, PART), F32)
    r["bf"][0:1, :] = b_fc[...].reshape(1, D)
    greet(
        [at.core, at.near, at.near_core, at.far, at.opposite]
        + [at.along_z(k) for k in (1, 2, 3)]
        + [at.along_x(k) for k in (1, 2, 3)]
        + [device for device in at.dp_peers[4:]]
    )

    def spread(source, slots):
        return [
            links.send(source.at[:, rows_of(sub_block(h, peer) * ROWS)], slots.at[block_of(w)], device)
            for device, peer in at.width_peers
        ]

    arrive = spread(tok, r["xa"])
    arrive += [links.send(vl, r["vg"].at[w], device) for device, _ in at.width_peers]
    r["vg"][w] = vl[...]

    class Weight:
        def __init__(self, full, device):
            own_block, next_block = full.at[block_of(w)], full.at[block_of(at.wy)]
            self.over = links.send(own_block, own_block, device)
            self.core = links.send(own_block, own_block, at.core)
            self.other = links.plan(next_block, next_block, at.core)

        def forward(self):
            self.over.wait_recv()
            self.other.start()

        def ready(self):
            self.core.wait_recv()
            self.other.wait_recv()

    loads[0].wait()
    r["wkv"][block_of(w), :] = interleave(r["wa_raw"][1], r["wa_raw"][2])
    weight_kv = Weight(r["wkv"], at.far)
    r["wq"][block_of(w), :] = r["wa_raw"][0]
    weight_q = Weight(r["wq"], at.far)
    loads[1].wait()
    r["wpt"][block_of(w), :] = r["wp_raw"][...].T
    loads[4].wait()
    for copy in arrive:
        copy.wait_recv()

    arrive_d = spread(dout, r["da"])
    vec[...] = jnp.concatenate([r["vg"][i] for i in range(4)], axis=1)
    r["x"][...] = r["xa"][...].T
    unit, _ = norm_stats(r["x"][...].astype(F32))
    x1, kv, q = r["x1"], r["kv"], r["q"]
    x1[0:ROWS, :] = (unit * vec[0:1, :] + vec[2:3, :]).astype(BF16)
    gather = GatherZ(links, at, x1)
    value_bias = interleave(jnp.zeros((1, PART), F32), bqv[1:2, :])
    weight_kv.forward()
    weight_kv.ready()
    weight_p = Weight(r["wpt"], at.far)
    loads[2].wait()
    weight_t = Weight(wt, at.far)
    quarter = [at.chunk(k) for k in (0, 1, 3, 2)]
    shares, passed = [], []

    def key_rows(first, count):
        rows = (nn(x1[first * ROWS : (first + count) * ROWS, :], r["wkv"][...]) + value_bias).astype(BF16)
        for i in range(count):
            block = kv.at[quarter[first + i], w]
            block[...] = rows[i * ROWS : (i + 1) * ROWS, :]
            shares.append(links.send(block, block, at.near))
            shares.append(links.send(block, block, at.core))

    for i in range(4):
        block = kv.at[quarter[i], at.wy]
        passed.append(links.plan(block, block, at.core))

    def pass_on(i):
        shares[2 * i].wait_recv()
        passed[i].start()

    key_rows(0, 1)
    gather.neighbours()
    key_rows(1, 2)
    weight_q.forward()
    pass_on(0)
    gather.rest()
    d_all = r["d_all"]
    loads[5].wait()
    for copy in arrive_d:
        copy.wait_recv()
    d_all[0:ROWS, :] = r["da"][...].T
    gather_d = GatherZ(links, at, d_all)
    key_rows(3, 1)
    weight_q.ready()
    queries = (nn(x1[...], r["wq"][...]) + bqv[0:1, :]).astype(BF16).astype(F32) * HS**-0.5
    q[...] = interleave(queries.astype(BF16), jnp.zeros((QUARTER, PART), BF16))
    weight_p.forward()
    for i in range(4):
        shares[2 * i + 1].wait_recv()

    kvt, att, att_t, lse, delta = r["kvt"], r["att"], r["att_t"], r["lse"], r["delta"]
    here = w - lax.rem(w, 2)
    there = 2 - here

    def half_keys(j, lanes, start):
        return kv[j, pl.ds(start, 2), :, lanes].reshape(2 * ROWS, lanes.stop - lanes.start)

    def half_columns(j, start):
        return pl.ds(pl.multiple_of(j * QUARTER + start * ROWS, 2 * ROWS), 2 * ROWS)

    def transpose_keys(start):
        for j in range(4):
            for head in range(HEADS):
                tile = slice(head * 128, (head + 1) * 128)
                kvt[tile, half_columns(j, start)] = half_keys(j, tile, start).T

    def attend_chunk(j, slot, start, merge):
        shift = sub_block(j, w) * ROWS
        apart = jnp.zeros((ROWS, 128), BF16)
        for first, count in ((0, 2), (2, 2), (4, 1)):
            lanes = slice(first * 128, (first + count) * 128)
            query = q[rows_of(slot * ROWS), lanes]
            if count == 2:
                top = jnp.concatenate([query[:, :128], apart], axis=1)
                query = jnp.concatenate([top, jnp.concatenate([apart, query[:, 128:]], axis=1)], axis=0)
            scores = [nt(half_keys(b, lanes, start), query) for b in range(j + 1)]
            scores[j] = mask_last(scores[j], j, shift, start)
            peak = functools.reduce(jnp.maximum, [jnp.max(s, axis=0, keepdims=True) for s in scores])
            total, result = 0.0, 0.0
            if merge:
                rows = [pl.ds(slot * 8 + first + i, 1) for i in range(count)]
                before = jnp.concatenate([lse[row, :] for row in rows], axis=1)
                peak = jnp.maximum(peak, before)
                scale = jnp.exp(before - peak)
                total = jnp.concatenate([delta[row, :] for row in rows], axis=1) * scale
            for b in range(j + 1):
                weights = jnp.exp(scores[b] - peak)
                total = total + column_sum(weights)
                result = result + nn(kvt[lanes, half_columns(b, start)], weights.astype(BF16))
            for i in range(count):
                head, part = first + i, slice(i * 128, (i + 1) * 128)
                place, row = slice(head * HS, (head + 1) * HS), pl.ds(slot * 8 + head, 1)
                values = result[i * 128 + HS : (i + 1) * 128, part]
                if merge:
                    values = (values + att_t[slot, place, :] * scale[:, part]) * (1.0 / total[:, part])
                    lse[row, :] = peak[:, part] + jnp.log(total[:, part])
                else:
                    lse[row, :] = peak[:, part]
                    delta[row, :] = total[:, part]
                att_t[slot, place, :] = values

    transpose_keys(here)

    @pl.loop(0, 4)
    def _(slot):
        pl.when(slot == 1)(functools.partial(pass_on, 1))
        pl.when(slot == 3)(functools.partial(pass_on, 2))
        j = at.chunk(jnp.where(slot == 3, 2, jnp.where(slot == 2, 3, slot)))
        for case in range(4):
            pl.when(j == case)(functools.partial(attend_chunk, case, slot, here, False))

    pass_on(3)
    loads[3].wait()
    weight_f = Weight(wf, at.near)
    for i in range(4):
        passed[i].wait_recv()

    transpose_keys(there)
    stage = r["stage"]
    sum_p = SumZ(links, at, stage, r["parts"], r["over"])

    gather_d.neighbours()
    weight_p.ready()

    @pl.loop(0, 4)
    def _(i):
        slot = jnp.where(i == 0, 3, jnp.where(i == 3, 0, i))
        j = at.chunk(jnp.where(slot == 3, 2, jnp.where(slot == 2, 3, slot)))
        for case in range(4):
            pl.when(j == case)(functools.partial(attend_chunk, case, slot, there, True))
        attended = att_t[slot].T.astype(BF16)
        att[rows_of(slot * ROWS), :] = attended
        stage[slot] = nt(attended, r["wpt"][...]).astype(BF16)
        pl.when(i == 0)(sum_p.send_across)
        pl.when(i == 1)(sum_p.right_bottom.start)
        pl.when(i == 1)(weight_t.forward)
        pl.when(i == 2)(sum_p.left_top.start)
        pl.when(i == 2)(sum_p.join_ahead)
        pl.when(i == 2)(sum_p.join_behind)

    gather_d.rest()
    weight_t.ready()
    weight_f.forward()
    middle = r["x"][...].astype(F32) + vec[4:5, :] + sum_p.result()
    r["middle"][...] = middle
    unit, _ = norm_stats(middle)
    x2, hid, gp = r["x2"], r["hid"], r["gp"]
    x2[0:ROWS, :] = (unit * vec[1:2, :] + vec[3:4, :]).astype(BF16)

    gather = GatherZ(links, at, x2)
    hidden_grad = r["hidden_grad"]
    for t in range(TILES):
        tile = slice(t * 256, (t + 1) * 256)
        hidden_grad[:, tile] = nn(d_all[...], wt[:, tile])
    weight_f.ready()
    stage_g, parts_g = r["stage_g"], r["parts_g"]
    moves = []

    def feed(first, count):
        rows = slice(first * ROWS, (first + count) * ROWS)

        for t in range(TILES):
            tile = slice(t * 256, (t + 1) * 256)
            u = nn(x2[rows, :], wf[:, tile]) + r["bf"][0:1, tile]
            square = u * u
            th = jnp.tanh(GELU_COEF * (u + 0.044715 * square * u))
            hid[rows, tile] = (0.5 * u * (1.0 + th)).astype(BF16)
            slope = 0.5 * (1.0 + th) + 0.5 * u * (1.0 - th * th) * (GELU_COEF * (1.0 + 0.134145 * square))
            gp[rows, tile] = (hidden_grad[rows, tile] * slope).astype(BF16)
        for t in range(TILES):
            tile = slice(t * 256, (t + 1) * 256)
            product = nt(gp[rows, :], wf[tile, :]).astype(BF16)
            for i in range(count):
                stage_g[first + i, :, tile] = product[i * ROWS : (i + 1) * ROWS]
        for i in range(first, first + count):
            if i:
                moves.append(links.send(stage_g.at[i], parts_g.at[i - 1], at.along_z((0, 1, 3, 2)[i])))

    feed(0, 1)
    gather.neighbours()
    feed(1, 2)
    gather.rest()
    feed(3, 1)
    grad_f, grad_t = r["grad_f"], r["grad_t"]

    def gradient_sum(tag, grad, columns, final):
        return GradientSum(
            links, at, grad, columns, r["pair_" + tag], r["strips_" + tag], r["cross_" + tag], final
        )

    @pl.loop(0, TILES)
    def _(t):
        grad_t[tile_of(t, 256), :] = tn(d_all[:, tile_of(t, 256)], hid[...]).astype(BF16)

    whole = slice(0, D)
    sum_t = gradient_sum("t", grad_t, whole, fin_t)
    sum_t.send_core()

    @pl.loop(0, TILES)
    def _(t):
        grad_f[tile_of(t, 256), :] = tn(x2[:, tile_of(t, 256)], gp[...]).astype(BF16)

    sum_f = GradientSumY(links, at, grad_f, r["pair_f"], r["cross_f"], r["strips_f"], r["half_f"], fin_f)
    sum_f.send_core()
    sum_t.send_x_by_neighbours()
    unit, scale = norm_stats(r["middle"][...])
    grad = d_all[0:ROWS, :].astype(F32)
    grad_normed = stage_g[0].astype(F32)
    for i in range(3):
        moves[i].wait_recv()
        grad_normed = grad_normed + parts_g[i].astype(F32)
    grad_middle = grad + norm_gradient(grad_normed, unit, scale, vec[1:2, :])
    r["gm"][...] = grad_middle
    branch = grad_middle.astype(BF16)
    g_all = r["g_all"]
    g_all[0:ROWS, :] = branch
    gather = GatherZ(links, at, g_all)
    sums = r["sums"]
    sums[1:2, :] = column_sum(grad_normed * unit)
    sums[3:4, :] = column_sum(grad_normed)
    sums[4:5, :] = column_sum(grad)
    sums[5:6, :] = column_sum(branch.astype(F32))
    sums[8:9, :] = column_sum(gp[...].astype(F32))
    sum_f.send_y()
    sum_p.sent()
    sum_b = SumZ(links, at, stage, r["parts_b"], r["over_b"])

    @pl.loop(0, TILES)
    def _(t):
        product = nt(hid[...], wt[tile_of(t, 256), :]).astype(BF16)
        for i in range(4):
            stage[i, :, tile_of(t, 256)] = product[i * ROWS : (i + 1) * ROWS]


    dkv, go, dq, dq_t = r["dkv"], r["go"], r["dq"], att_t
    take, take_y, gkv = r["take"], r["take_y"], r["gkv"]
    dkv[...] = jnp.zeros(dkv.shape, BF16)

    def rows_back(first, count):
        rows = slice(first * ROWS, (first + count) * ROWS)
        grad = nn(g_all[rows, :], r["wpt"][...]).astype(BF16)
        go[rows, :] = interleave(jnp.zeros((count * ROWS, PART), BF16), grad)
        for i in range(count):
            slot = first + i
            both = grad[i * ROWS : (i + 1) * ROWS, :].astype(F32).T * att_t[slot]
            delta[slot * 8 : slot * 8 + HEADS, :] = jnp.sum(both.reshape(HEADS, HS, ROWS), axis=1)

    shared = links.reserve(3 * HEADS)

    def head_move(kind, head):
        source = dkv.at[head, :, (at.wyc, at.wc, at.wy)[kind]]
        target = take_y.at[head] if kind == 2 else take.at[1 - kind, head]
        return links.make(shared + kind * HEADS + head, source, target, at.near if kind == 2 else at.core)

    def cross_head(head):
        head_move(0, head).wait_recv()
        for j in range(4):
            both = dkv[head, j, at.wy].astype(F32) + take[1, head, j].astype(F32)
            dkv[head, j, at.wy] = both.astype(BF16)
        head_move(2, head).start()

    def back_chunk(j, slot):
        rows = rows_of(slot * ROWS)

        @pl.loop(0, HEADS)
        def _(head):
            tile = tile_of(head, 128)
            side = jnp.concatenate([q[rows, tile], go[rows, tile]], axis=0)
            log_total = lse[pl.ds(slot * 8 + head, 1), :]
            inner = delta[pl.ds(slot * 8 + head, 1), :]
            grads = []
            for b in range(j + 1):
                products = nt(kv[b, :, :, tile].reshape(QUARTER, 128), side)
                scores = products[:, :128]
                if b == j:
                    scores = mask_last(scores, j, sub_block(j, w) * ROWS)
                probs = jnp.exp(scores - log_total)
                grads.append((probs * (products[:, 128:] - inner)).astype(BF16))
                both = nn(jnp.concatenate([grads[b], probs.astype(BF16)], axis=1), side)
                both = dkv[head, b].reshape(QUARTER, 128).astype(F32) + both
                dkv[head, b] = both.astype(BF16).reshape(4, ROWS, 128)
            result = nn(kvt[tile, 0 : (j + 1) * QUARTER], jnp.concatenate(grads, axis=0))
            dq_t[slot, tile_of(head, HS), :] = result[:HS, :] * HS**-0.5
            pl.when(slot == 3)(lambda: head_move(0, head).start())

    def near_back():
        gather.neighbours()
        rows_back(1, 2)

    for copy in moves:
        copy.wait_send()
    rows_back(0, 1)

    sum_t.relay_x()

    def far_back():
        gather.rest()
        rows_back(3, 1)
        sum_b.send_across()
        sum_b.send_near()

    @pl.loop(0, 4)
    def _(slot):
        pl.when(slot == 1)(near_back)
        pl.when(slot == 3)(far_back)
        j = at.chunk(jnp.where(slot == 2, 3, jnp.where(slot == 3, 2, slot)))
        for case in range(4):
            pl.when(j == case)(functools.partial(back_chunk, case, slot))

    for slot in range(4):
        dq[slot * ROWS : (slot + 1) * ROWS, :] = dq_t[slot].T.astype(BF16)
    for head in range(HEADS):
        cross_head(head)
    for head in range(HEADS):
        head_move(1, head).start()
    sum_f.send_x()
    slots = []
    for j in range(4):
        k = lax.rem(j + 4 - h, 4)
        slots.append(jnp.where(k == 2, 3, jnp.where(k == 3, 2, k)))
    keep = []

    def send_back(total, passing=False):
        strip = total.send_back(passing)
        copy = pltpu.make_async_copy(total.total[0], strip, local.at[7 + len(keep)])
        copy.start()
        keep.append(copy)

    def send_rows(back, target):
        place = target.at[:, rows_of(mine * ROWS)]
        keep = pltpu.make_async_copy(back.at[block_of(w)], place, local.at[6])
        keep.start()
        copies = [links.send(back.at[block_of(peer)], place, device) for device, peer in at.width_peers]
        keep.wait()
        return copies

    sum_t.sent_core()

    @pl.loop(0, TILES)
    def _(t):
        tile = tile_of(t, 256)
        pieces = [tn(x1[:, tile], dq[...]).astype(BF16), tn(g_all[:, tile], att[...]).astype(BF16)]
        grad_t[tile, PAIR:] = jnp.concatenate(pieces, axis=1)

    sum_q = gradient_sum("q", grad_t, slice(PAIR, D), fin_q)
    sum_q.send_core()
    sum_t.send_far()
    sums[9:10, 0:PART] = column_sum(dq[...].astype(F32))
    sum_b.join_ahead()
    sum_b.join_behind()
    sum_q.send_x()
    sum_f.send_back()
    result = r["middle"][...] + vec[5:6, :] + sum_b.result()
    r["xa"][...] = result.astype(BF16).T
    returns = send_rows(r["xa"], bo)

    for head in range(HEADS):
        tile = slice(head * 128, (head + 1) * 128)
        head_move(1, head).wait_recv()
        head_move(2, head).wait_recv()
        for j in range(4):
            total = dkv[head, j, w].astype(F32) + take[0, head, j].astype(F32) + take_y[head, j].astype(F32)
            gkv[rows_of(slots[j] * ROWS), tile] = total.astype(BF16)


    @pl.loop(0, TILES)
    def _(t):
        tile = tile_of(t, 256)
        grad_t[tile, 0:PAIR] = tn(x1[:, tile], gkv[...]).astype(BF16)

    sum_k = gradient_sum("k", grad_t, slice(0, PAIR), fin_k)
    sum_k.send_core()
    sum_t.send_opposite()
    sum_b.sent()
    sum_l = SumZ(links, at, stage, r["parts"], r["over"])

    def first_partial(first, count):
        rows = slice(first * ROWS, (first + count) * ROWS)
        product = (nt(dq[rows, :], r["wq"][...]) + nt(gkv[rows, :], r["wkv"][...])).astype(BF16)
        for i in range(count):
            stage[first + i] = product[i * ROWS : (i + 1) * ROWS]

    first_partial(3, 1)
    sum_l.send_across()
    first_partial(1, 2)
    sum_l.send_near()
    grad_values = column_sum(gkv[...].astype(F32))
    for head in range(HEADS):
        sums[9:10, PART + head * HS : PART + (head + 1) * HS] = grad_values[:, head * 128 + HS : (head + 1) * 128]
    sums[9:10, PAIR:] = jnp.zeros((1, PAIR), F32)
    sums[10:16, :] = jnp.zeros((6, D), F32)
    sums[6:8, :] = jnp.zeros((2, D), F32)
    over_v = [links.send(sums.at[8:16], r["take_v"].at[i], at.width_peers[i][0]) for i in range(3)]
    sum_k.send_x()
    keep.append(sum_f.send_opposite(local.at[7 + len(keep)]))
    sum_l.join_ahead()
    sum_l.join_behind()
    first_partial(0, 1)
    sum_q.send_y()
    send_back(sum_t, True)
    grad_normed = sum_l.result()
    unit, scale = norm_stats(r["x"][...].astype(F32))
    sums[0:1, :] = column_sum(grad_normed * unit)
    sums[2:3, :] = column_sum(grad_normed)
    for part in range(4):
        r["sums_w"][part] = sums[0:8, part * PART : (part + 1) * PART]
    over_w = [
        links.send(r["sums_w"].at[peer], r["take_w"].at[i], device)
        for i, (device, peer) in enumerate(at.width_peers)
    ]
    result = r["gm"][...] + norm_gradient(grad_normed, unit, scale, vec[0:1, :])
    r["da"][...] = result.astype(BF16).T
    returns += send_rows(r["da"], dt)
    sum_t.pass_back()
    send_back(sum_q)

    for copy in over_w + over_v:
        copy.wait_recv()
    sums_d = r["sums_d"]
    normed = r["sums_w"][w] + r["take_w"][0] + r["take_w"][1] + r["take_w"][2]
    biases = sums[8:10, :] + r["take_v"][0, 0:2] + r["take_v"][1, 0:2] + r["take_v"][2, 0:2]
    r["sums_n"][...] = normed
    over_z = [links.send(r["sums_n"], r["sums_z"].at[k - 1], at.along_z(k)) for k in (1, 2, 3)]
    sum_k.send_y()
    for copy in over_z:
        copy.wait_recv()
    normed = r["sums_n"][...] + r["sums_z"][0] + r["sums_z"][1] + r["sums_z"][2]
    sums_d[...] = jnp.zeros((8, D), F32)
    for i in range(6):
        sums_d[i // 3 : i // 3 + 1, (i % 3) * 384 : (i % 3) * 384 + PART] = normed[i : i + 1, :]
    sums_d[2:4, :] = biases
    over_x = [links.send(sums_d, r["sums_x"].at[i], device) for i, device in enumerate(at.dp_peers)]
    send_back(sum_k)
    total = sums_d[...]
    for i, copy in enumerate(over_x):
        copy.wait_recv()
        total = total + r["sums_x"][i]
    fin_v[...] = total
    for copy in keep:
        copy.wait()
    for total in (sum_t, sum_f, sum_q, sum_k):
        total.finish()
    for copy in returns:
        copy.wait()
    for kind in range(3):
        for head in range(HEADS):
            head_move(kind, head).wait_send()
    for copy in links.copies:
        copy.wait_send()


def block(*inputs):
    return pl.pallas_call(
        block_kernel,
        name="block",
        out_shape=(
            jax.ShapeDtypeStruct((PART, QUARTER), BF16),
            jax.ShapeDtypeStruct((PART, QUARTER), BF16),
            jax.ShapeDtypeStruct((PART, D), BF16),
            jax.ShapeDtypeStruct((PART, D), BF16),
            jax.ShapeDtypeStruct((PART, PAIR), BF16),
            jax.ShapeDtypeStruct((PART, PAIR), BF16),
            jax.ShapeDtypeStruct((8, D), F32),
        ),
        in_specs=[ANY, ANY, VMEM, VMEM, VMEM, VMEM, ANY, VMEM, ANY, ANY, VMEM, ANY],
        out_specs=(ANY, ANY, ANY, ANY, ANY, ANY, VMEM),
        scratch_shapes=[pltpu.VMEM(shape, kind) for shape, kind in SCRATCH.values()]
        + [pltpu.SemaphoreType.DMA((COPIES,)), pltpu.SemaphoreType.DMA((COPIES,)), pltpu.SemaphoreType.DMA((12,))],
        compiler_params=pltpu.CompilerParams(collective_id=1, has_side_effects=True, vmem_limit_bytes=64 * 2**20),
    )(*inputs)


def finish_kernel(*refs):
    inputs, outputs, (f, t, qp, kv, d_wa, d_wp, d_wf, d_wo, rows_b, rows_d, sems) = refs[:7], refs[7:19], refs[19:]
    bo, dt, f_in, t_in, qp_in, kv_in, v = inputs
    out, d_tok, gain, shift, wa_out, d_bqv, wp_out, d_bp, wf_out, d_bf, wo_out, d_bo = outputs
    loads = [
        pltpu.make_async_copy(source, target, sems.at[i])
        for i, (source, target) in enumerate(((t_in, t), (f_in, f), (qp_in, qp), (kv_in, kv), (bo, rows_b), (dt, rows_d)))
    ]
    stores = [
        pltpu.make_async_copy(source, target, sems.at[6 + i])
        for i, (source, target) in enumerate(
            ((rows_b, out), (rows_d, d_tok), (d_wo, wo_out), (d_wf, wf_out), (d_wa, wa_out), (d_wp, wp_out))
        )
    ]
    for copy in loads:
        copy.start()
    loads[0].wait()
    d_wo[...] = t[...].astype(F32)
    stores[2].start()
    loads[1].wait()
    d_wf[...] = f[...].astype(F32)
    stores[3].start()
    loads[2].wait()
    d_wa[0] = qp[:, :PART].astype(F32)
    d_wp[...] = qp[:, PART:].astype(F32).T
    stores[5].start()
    loads[3].wait()
    both = kv[...].astype(F32)
    d_wa[1] = jnp.concatenate([both[:, head * 128 : head * 128 + HS] for head in range(HEADS)], axis=1)
    d_wa[2] = jnp.concatenate([both[:, head * 128 + HS : (head + 1) * 128] for head in range(HEADS)], axis=1)
    stores[4].start()
    for i in range(2):
        loads[4 + i].wait()
        stores[i].start()
    rows = [v[i // 3 : i // 3 + 1, (i % 3) * 384 : (i % 3) * 384 + PART] for i in range(6)]
    gain[0:1, :] = rows[0]
    gain[1:2, :] = rows[1]
    shift[0:1, :] = rows[2]
    shift[1:2, :] = rows[3]
    d_bo[...] = rows[4].reshape(PART)
    d_bp[...] = rows[5].reshape(PART)
    d_bf[...] = v[2:3, :].reshape(D)
    d_bqv[0:1, :] = v[3:4, 0:PART]
    d_bqv[1:2, :] = v[3:4, PART:PAIR]
    for copy in stores:
        copy.wait()


def finish(*inputs):
    shapes = [
        ((PART, QUARTER), BF16),
        ((PART, QUARTER), BF16),
        ((2, PART), F32),
        ((2, PART), F32),
        ((3, PART, PART), F32),
        ((2, PART), F32),
        ((PART, PART), F32),
        ((PART,), F32),
        ((PART, D), F32),
        ((D,), F32),
        ((PART, D), F32),
        ((PART,), F32),
    ]
    return pl.pallas_call(
        finish_kernel,
        name="finish",
        out_shape=[jax.ShapeDtypeStruct(shape, kind) for shape, kind in shapes],
        in_specs=[ANY] * 6 + [VMEM],
        out_specs=[ANY, ANY, VMEM, VMEM, ANY, VMEM, ANY, VMEM, ANY, VMEM, ANY, VMEM],
        scratch_shapes=[
            pltpu.VMEM((PART, D), BF16),
            pltpu.VMEM((PART, D), BF16),
            pltpu.VMEM((PART, PAIR), BF16),
            pltpu.VMEM((PART, PAIR), BF16),
            pltpu.VMEM((3, PART, PART), F32),
            pltpu.VMEM((PART, PART), F32),
            pltpu.VMEM((PART, D), F32),
            pltpu.VMEM((PART, D), F32),
            pltpu.VMEM((PART, QUARTER), BF16),
            pltpu.VMEM((PART, QUARTER), BF16),
            pltpu.SemaphoreType.DMA((12,)),
        ],
        compiler_params=pltpu.CompilerParams(vmem_limit_bytes=63 * 2**20),
    )(*inputs)


def shards(tokens, ln_gain, ln_bias, w_attn, b_qv, w_proj, b_proj, w_fc, b_fc, w_out, b_out, d_out):
    parts = block(tokens.T, d_out.T, ln_gain, ln_bias, b_proj, b_out, w_attn, b_qv, w_proj, w_fc, b_fc, w_out.T)
    results = list(finish(*parts))
    for i in (0, 1, 10):
        results[i] = results[i].T
    return tuple(results)


def solution(mesh):
    in_specs = (
        P(("dp", "heads"), "width"),
        P(None, "width"),
        P(None, "width"),
        P(None, "width", "heads"),
        P(None, "heads"),
        P("heads", "width"),
        P("width"),
        P("width", "heads"),
        P("heads"),
        P("heads", "width"),
        P("width"),
        P(("dp", "heads"), "width"),
    )
    out_specs = (
        P(("dp", "heads"), "width"),
        P(("dp", "heads"), "width"),
        P(None, "width"),
        P(None, "width"),
        P(None, "width", "heads"),
        P(None, "heads"),
        P("heads", "width"),
        P("width"),
        P("width", "heads"),
        P("heads"),
        P("heads", "width"),
        P("width"),
    )
    return jax.shard_map(shards, mesh=mesh, in_specs=in_specs, out_specs=out_specs, check_vma=False)
```

```python
import functools

import jax
import jax.numpy as jnp
from jax import lax
from jax.experimental import pallas as pl
from jax.experimental.pallas import tpu as pltpu
from jax.sharding import PartitionSpec as P

F32, BF16 = jnp.float32, jnp.bfloat16
D, HS, ROWS, PART, QUARTER, HEADS = 1280, 64, 128, 320, 512, 5
PAIR = 2 * PART
STRIP = PART // 4
HALF = ROWS // 2
EPSILON = 1e-05
GELU_COEF = 0.7978845608028654
MASKED = -1e30
VMEM = pl.BlockSpec(memory_space=pltpu.VMEM)
ANY = pl.BlockSpec(memory_space=pl.ANY)
TILES = D // 256


def nn(a, b):
    return jnp.dot(a, b, preferred_element_type=F32)


def nt(a, b):
    return lax.dot_general(a, b, (((1,), (1,)), ((), ())), preferred_element_type=F32)


def tn(a, b):
    return lax.dot_general(a, b, (((0,), (0,)), ((), ())), preferred_element_type=F32)


def rows_of(start, size=ROWS):
    return pl.ds(pl.multiple_of(start, size), size)


def block_of(who):
    return pl.ds(pl.multiple_of(who * PART, 64), PART)


def tile_of(i, size):
    if isinstance(i, int):
        return slice(i * size, (i + 1) * size)
    return pl.ds(pl.multiple_of(i * size, size), size)


def sub_block(quarter, w):
    return w + lax.rem(quarter, 2) * (3 - 2 * w)


class Place:
    def __init__(self):
        self.dp, self.w, self.h = (lax.axis_index(n) for n in ("dp", "width", "heads"))
        self.x = lax.rem(self.dp, 4)
        self.wc = self.w + 1 - 2 * lax.rem(self.w, 2)
        self.wy = lax.rem(self.w + 2, 4)
        self.wyc = lax.rem(self.wc + 2, 4)
        across = lax.rem(self.dp + 4, 8)
        self.core = (self.dp, self.wc, self.h)
        self.near = (self.dp, self.wy, self.h)
        self.near_core = (self.dp, self.wyc, self.h)
        self.far = (across, self.wy, self.h)
        self.opposite = (across, self.w, self.h)
        self.width_peers = ((self.near, self.wy), (self.near_core, self.wyc), (self.core, self.wc))

        beyond = lax.rem(self.dp + 4, 8) - self.x
        self.dp_peers = [self.along_x(k) for k in (1, 2, 3)] + [self.opposite]
        self.dp_peers += [(beyond + lax.rem(self.x + k, 4), self.w, self.h) for k in (1, 2, 3)]

    def along_z(self, k):
        return (self.dp, self.w, lax.rem(self.h + k, 4))

    def along_x(self, k):
        return (self.dp - self.x + lax.rem(self.x + k, 4), self.w, self.h)

    def chunk(self, k):
        return lax.rem(self.h + k, 4)


def greet(devices):
    barrier = pltpu.get_barrier_semaphore()
    for device in devices:
        pl.semaphore_signal(barrier, inc=1, device_id=device, device_id_type=pl.DeviceIdType.MESH)
    pl.semaphore_wait(barrier, len(devices))


class Move:
    def __init__(self, copy):
        self.copy, self.left = copy, False
        self.start, self.wait_recv = copy.start, copy.wait_recv

    def wait_send(self):
        if not self.left:
            self.copy.wait_send()
        self.left = True

    def wait(self):
        self.wait_recv()
        self.wait_send()


class Links:
    def __init__(self, sent, landed):
        self.sent, self.landed, self.copies, self.count = sent, landed, [], 0

    def reserve(self, count):
        self.count += count
        return self.count - count

    def make(self, i, source, target, device):
        return pltpu.make_async_remote_copy(
            src_ref=source,
            dst_ref=target,
            send_sem=self.sent.at[i],
            recv_sem=self.landed.at[i],
            device_id=device,
            device_id_type=pl.DeviceIdType.MESH,
        )

    def plan(self, source, target, device):
        self.copies.append(Move(self.make(self.reserve(1), source, target, device)))
        return self.copies[-1]

    def send(self, source, target, device):
        copy = self.plan(source, target, device)
        copy.start()
        return copy


class GatherZ:
    def __init__(self, links, at, rows):
        right, left = at.along_z(1), at.along_z(3)
        own, ahead, behind = (rows.at[pl.ds(i * ROWS, ROWS)] for i in range(3))
        self.right = links.send(own, behind, right)
        self.left = links.send(own, ahead, left)
        self.low = links.plan(
            rows.at[pl.ds(2 * ROWS, HALF)], rows.at[pl.ds(3 * ROWS, HALF)], right
        )
        self.high = links.plan(
            rows.at[pl.ds(ROWS + HALF, HALF)], rows.at[pl.ds(3 * ROWS + HALF, HALF)], left
        )

    def neighbours(self):
        self.left.wait_recv()
        self.high.start()
        self.right.wait_recv()
        self.low.start()

    def rest(self):
        self.low.wait_recv()
        self.high.wait_recv()


class SumZ:
    def __init__(self, links, at, stage, parts, over):
        self.stage, self.parts, self.over = stage, parts, over
        right, left = at.along_z(1), at.along_z(3)
        top, bottom = pl.ds(0, HALF), pl.ds(HALF, HALF)
        self.far_right = links.plan(stage.at[3, top], over.at[0], right)
        self.far_left = links.plan(stage.at[3, bottom], over.at[1], left)
        self.right_bottom = links.plan(stage.at[1, bottom], parts.at[0, bottom], right)
        self.right_top = links.plan(stage.at[1, top], parts.at[0, top], right)
        self.left_top = links.plan(stage.at[2, top], parts.at[1, top], left)
        self.left_bottom = links.plan(stage.at[2, bottom], parts.at[1, bottom], left)

    def sent(self):
        for copy in (self.far_right, self.far_left, self.right_bottom, self.right_top, self.left_top, self.left_bottom):
            copy.wait_send()

    def send_across(self):
        self.far_right.start()
        self.far_left.start()

    def send_near(self):
        self.right_bottom.start()
        self.left_top.start()

    def join_ahead(self):
        self.far_right.wait_recv()
        joined = self.stage[1, 0:HALF, :].astype(F32) + self.over[0].astype(F32)
        self.stage[1, 0:HALF, :] = joined.astype(BF16)
        self.right_top.start()

    def join_behind(self):
        self.far_left.wait_recv()
        joined = self.stage[2, HALF:, :].astype(F32) + self.over[1].astype(F32)
        self.stage[2, HALF:, :] = joined.astype(BF16)
        self.left_bottom.start()

    def result(self):
        for copy in (self.right_bottom, self.right_top, self.left_top, self.left_bottom):
            copy.wait_recv()
        return self.stage[0].astype(F32) + self.parts[0].astype(F32) + self.parts[1].astype(F32)


class GradientSum:
    def __init__(self, links, at, grad, columns, pair, strips, cross, final):
        self.links, self.at, self.grad, self.columns = links, at, grad, columns
        self.pair, self.strips, self.cross, self.final = pair, strips, cross, final
        self.strip = rows_of(at.x * STRIP, STRIP)
        self.total = [pair.at[0, self.strip], pair.at[1, self.strip]]

    def mine(self, who):
        return self.grad.at[block_of(who), self.columns]

    def send_core(self):
        at, links = self.at, self.links
        self.core = [
            links.send(self.mine(at.wc), self.pair.at[0], at.core),
            links.send(self.mine(at.wyc), self.pair.at[1], at.core),
        ]

    def sent_core(self):
        for copy in self.core:
            copy.wait_send()

    def add_core(self):
        for i, who in ((0, self.at.w), (1, self.at.wy)):
            self.core[i].wait_recv()
            self.pair[i] = (self.pair[i].astype(F32) + self.mine(who)[...].astype(F32)).astype(BF16)

    def send_x(self):
        at, links = self.at, self.links
        self.add_core()
        self.along = [
            links.send(
                self.pair.at[:, rows_of(lax.rem(at.x + k, 4) * STRIP, STRIP)], self.strips.at[k - 1], at.along_x(k)
            )
            for k in (2, 1, 3)
        ]

    def send_x_by_neighbours(self):
        at, links = self.at, self.links
        self.add_core()
        right, left = at.along_x(1), at.along_x(3)
        ahead, across, behind = (rows_of(lax.rem(at.x + k, 4) * STRIP, STRIP) for k in (1, 2, 3))
        parts, over = self.strips, self.strips.at[2]
        self.over_x = [
            links.send(self.pair.at[0, across], over.at[0], right),
            links.send(self.pair.at[1, across], over.at[1], left),
        ]
        self.along = [
            links.send(self.pair.at[1, ahead], parts.at[0, 1], right),
            links.send(self.pair.at[0, behind], parts.at[1, 0], left),
            links.plan(self.pair.at[0, ahead], parts.at[0, 0], right),
            links.plan(self.pair.at[1, behind], parts.at[1, 1], left),
        ]
        self.relayed = (self.pair.at[0, ahead], self.pair.at[1, behind])

    def relay_x(self):
        for i in range(2):
            self.over_x[i].wait_recv()
            joined = self.relayed[i][...].astype(F32) + self.strips[2, i].astype(F32)
            self.relayed[i][...] = joined.astype(BF16)
            self.along[2 + i].start()

    def add_strips(self):
        for copy in self.along:
            copy.wait_recv()
        for i in range(2):
            joined = self.total[i][...].astype(F32)
            for k in range(3 if len(self.along) == 3 else 2):
                joined = joined + self.strips[k, i].astype(F32)
            self.total[i][...] = joined.astype(BF16)

    def send_y(self):
        self.add_strips()
        self.over = [
            self.links.send(self.total[1], self.cross.at[0], self.at.near),
            self.links.send(self.total[1], self.cross.at[1], self.at.far),
            self.links.send(self.total[0], self.cross.at[2], self.at.opposite),
        ]

    def send_far(self):
        self.add_strips()
        self.over = [self.links.send(self.total[1], self.cross.at[0], self.at.far)]

    def send_opposite(self):
        self.over[0].wait()
        joined = self.total[0][...].astype(F32) + self.cross[0].astype(F32)
        self.total[0][...] = joined.astype(BF16)
        self.over = [self.links.send(self.total[0], self.cross.at[1], self.at.opposite)]

    def send_back(self, passing):
        at, links = self.at, self.links
        joined = self.total[0][...].astype(F32)
        for copy in self.over:
            copy.wait()
        places = (0, 1, 2) if len(self.over) == 3 else (1,)
        for place in places:
            joined = joined + self.cross[place].astype(F32)
        self.total[0][...] = joined.astype(BF16)
        strip = self.final.at[self.strip]
        self.back = [links.send(self.total[0], strip, at.along_x(k)) for k in ((1, 3) if passing else (2, 1, 3))]
        self.passing = passing
        return strip

    def pass_back(self):
        at, links = self.at, self.links
        behind, ahead = lax.rem(at.x + 3, 4) * STRIP, lax.rem(at.x + 1, 4) * STRIP
        first = self.final.at[pl.ds(pl.multiple_of(behind, 16), 48)]
        second = self.final.at[pl.ds(pl.multiple_of(ahead + 48, 16), 32)]
        self.back[0].wait_recv()
        self.back[1].wait_recv()
        self.back = [
            links.send(first, first, at.along_x(1)),
            links.send(second, second, at.along_x(3)),
        ]

    def finish(self):
        for copy in self.back:
            copy.wait_recv()


class GradientSumY:
    def __init__(self, links, at, grad, pair, cross, strips, half, final):
        self.links, self.at, self.grad = links, at, grad
        self.pair, self.cross, self.strips, self.half, self.final = pair, cross, strips, half, final
        part = at.dp // 4
        self.kept = pl.ds(pl.multiple_of(part * PAIR, PAIR), PAIR)
        self.given = pl.ds(pl.multiple_of((1 - part) * PAIR, PAIR), PAIR)
        self.strip = rows_of(at.x * STRIP, STRIP)

    def mine(self, who):
        return self.grad.at[block_of(who)]

    def send_core(self):
        at, links = self.at, self.links
        self.core = [
            links.send(self.mine(at.wc), self.pair.at[0], at.core),
            links.send(self.mine(at.wyc), self.pair.at[1], at.core),
        ]

    def send_y(self):
        at, links = self.at, self.links
        for i, who in ((0, at.w), (1, at.wy)):
            self.core[i].wait_recv()
            self.pair[i] = (self.pair[i].astype(F32) + self.mine(who)[...].astype(F32)).astype(BF16)
        self.over = [
            links.send(self.pair.at[1, :, self.kept], self.cross.at[0], at.near),
            links.send(self.pair.at[1, :, self.given], self.cross.at[1], at.far),
            links.send(self.pair.at[0, :, self.given], self.cross.at[2], at.opposite),
        ]

    def send_x(self):
        at, links = self.at, self.links
        joined = self.pair[0, :, self.kept].astype(F32)
        for k in range(3):
            self.over[k].wait_recv()
            joined = joined + self.cross[k].astype(F32)
        self.pair[0, :, self.kept] = joined.astype(BF16)
        self.along = [
            links.send(
                self.pair.at[0, rows_of(lax.rem(at.x + k, 4) * STRIP, STRIP), self.kept],
                self.strips.at[k - 1],
                at.along_x(k),
            )
            for k in (2, 1, 3)
        ]

    def send_back(self):
        at, links = self.at, self.links
        joined = self.pair[0, self.strip, self.kept].astype(F32)
        for copy in self.along:
            copy.wait_recv()
        for k in range(3):
            joined = joined + self.strips[k].astype(F32)
        self.half[self.strip, :] = joined.astype(BF16)
        place = self.half.at[self.strip]
        self.back = [links.send(place, place, at.along_x(k)) for k in (2, 1, 3)]

    def send_opposite(self, sem):
        for copy in self.back:
            copy.wait_recv()
        place = self.final.at[:, self.kept]
        self.last = self.links.send(self.half, place, self.at.opposite)
        keep = pltpu.make_async_copy(self.half, place, sem)
        keep.start()
        return keep

    def finish(self):
        self.last.wait_recv()


def norm_stats(values):
    mean = jnp.mean(values, axis=1, keepdims=True)
    centred = values - mean
    scale = lax.rsqrt(jnp.mean(centred * centred, axis=1, keepdims=True) + EPSILON)
    return centred * scale, scale


def norm_gradient(grad, unit, scale, gain):
    scaled = grad * gain
    mean = jnp.mean(scaled, axis=1, keepdims=True)
    along = jnp.mean(scaled * unit, axis=1, keepdims=True)
    return scale * (scaled - mean - unit * along)


def interleave(first, second):
    pieces = []
    for head in range(HEADS):
        part = slice(head * HS, (head + 1) * HS)
        pieces += [first[:, part], second[:, part]]
    return jnp.concatenate(pieces, axis=1)


def mask_last(scores, quarter, shift, start=0):
    shape = (scores.shape[0] // ROWS, ROWS, ROWS)
    owner = start + lax.broadcasted_iota(jnp.int32, shape, 0)
    if quarter % 2:
        owner = 3 - owner
    key = owner * ROWS + lax.broadcasted_iota(jnp.int32, shape, 1)
    query = lax.broadcasted_iota(jnp.int32, shape, 2) + shift
    seen = (key <= query).reshape(scores.shape[0], ROWS)
    parts = [scores[:, i * ROWS : (i + 1) * ROWS] for i in range(scores.shape[1] // ROWS)]
    parts = [jnp.where(seen, part, MASKED) for part in parts]
    return parts[0] if len(parts) == 1 else jnp.concatenate(parts, axis=1)


def column_sum(values):
    return jnp.sum(values, axis=0, keepdims=True)


SCRATCH = dict(
    wkv=((D, PAIR), BF16),
    wq=((D, PART), BF16),
    wpt=((D, PART), BF16),
    wf=((D, D), BF16),
    wt=((D, D), BF16),
    wa_raw=((3, PART, PART), BF16),
    wp_raw=((PART, PART), BF16),
    xa=((D, ROWS), BF16),
    da=((D, ROWS), BF16),
    vl=((8, PART), F32),
    vg=((4, 8, PART), F32),
    vec=((8, D), F32),
    bf=((8, D), F32),
    x=((ROWS, D), BF16),
    x1=((QUARTER, D), BF16),
    q=((QUARTER, PAIR), BF16),
    kv=((4, 4, ROWS, PAIR), BF16),
    kvt=((PAIR, 2048), BF16),
    att=((QUARTER, PART), BF16),
    att_t=((4, PART, ROWS), F32),
    lse=((32, 128), F32),
    delta=((32, 128), F32),
    middle=((ROWS, D), F32),
    stage=((4, ROWS, D), BF16),
    parts=((2, ROWS, D), BF16),
    over=((2, HALF, D), BF16),
    d_all=((QUARTER, D), BF16),
    x2=((QUARTER, D), BF16),
    hidden_grad=((QUARTER, D), F32),
    hid=((QUARTER, D), BF16),
    gp=((QUARTER, D), BF16),
    stage_g=((4, ROWS, D), BF16),
    parts_g=((3, ROWS, D), BF16),
    parts_b=((2, ROWS, D), BF16),
    over_b=((2, HALF, D), BF16),
    gm=((ROWS, D), F32),
    grad_f=((D, D), BF16),
    grad_t=((D, D), BF16),
    pair_f=((2, PART, D), BF16),
    pair_t=((2, PART, D), BF16),
    pair_q=((2, PART, PAIR), BF16),
    pair_k=((2, PART, PAIR), BF16),
    strips_f=((3, STRIP, PAIR), BF16),
    half_f=((PART, PAIR), BF16),
    strips_t=((3, 2, STRIP, D), BF16),
    strips_q=((3, 2, STRIP, PAIR), BF16),
    strips_k=((3, 2, STRIP, PAIR), BF16),
    cross_f=((3, PART, PAIR), BF16),
    cross_t=((3, STRIP, D), BF16),
    cross_q=((3, STRIP, PAIR), BF16),
    cross_k=((3, STRIP, PAIR), BF16),
    g_all=((QUARTER, D), BF16),
    go=((QUARTER, PAIR), BF16),
    dkv=((HEADS, 4, 4, ROWS, 128), BF16),
    take=((2, HEADS, 4, ROWS, 128), BF16),
    take_y=((HEADS, 4, ROWS, 128), BF16),
    dq=((QUARTER, PART), BF16),
    gkv=((QUARTER, PAIR), BF16),
    sums=((16, D), F32),
    sums_n=((8, PART), F32),
    sums_z=((3, 8, PART), F32),
    sums_w=((4, 8, PART), F32),
    take_w=((3, 8, PART), F32),
    take_v=((3, 8, D), F32),
    sums_d=((8, D), F32),
    sums_x=((7, 8, D), F32),
)
COPIES = 176


def block_kernel(*refs):
    names = ("tok", "dout", "gain", "shift", "b_proj", "b_out", "wa_in", "bqv", "wp_in", "wf_in", "b_fc", "wo_in")
    names += ("bo", "dt", "fin_f", "fin_t", "fin_q", "fin_k", "fin_v")
    names += tuple(SCRATCH) + ("sent", "landed", "local")
    r = dict(zip(names, refs))
    (tok, dout, gain, shift, b_proj, b_out, wa_in, bqv, wp_in, wf_in, b_fc, wo_in) = refs[:12]
    (bo, dt, fin_f, fin_t, fin_q, fin_k, fin_v) = refs[12:19]
    at = Place()
    w, h = at.w, at.h
    links = Links(r["sent"], r["landed"])
    local = r["local"]
    mine = sub_block(h, w)
    vec = r["vec"]

    wf, wt = r["wf"], r["wt"]
    loads = [
        pltpu.make_async_copy(wa_in, r["wa_raw"], local.at[0]),
        pltpu.make_async_copy(wp_in, r["wp_raw"], local.at[1]),
        pltpu.make_async_copy(wo_in, wt.at[block_of(w)], local.at[2]),
        pltpu.make_async_copy(wf_in, wf.at[block_of(w)], local.at[3]),
        pltpu.make_async_copy(tok.at[:, rows_of(mine * ROWS)], r["xa"].at[block_of(w)], local.at[4]),
        pltpu.make_async_copy(dout.at[:, rows_of(mine * ROWS)], r["da"].at[block_of(w)], local.at[5]),
    ]
    for copy in loads:
        copy.start()
    vl = r["vl"]
    vl[0:2, :] = gain[...]
    vl[2:4, :] = shift[...]
    vl[4:5, :] = b_proj[...].reshape(1, PART)
    vl[5:6, :] = b_out[...].reshape(1, PART)
    vl[6:8, :] = jnp.zeros((2, PART), F32)
    r["bf"][0:1, :] = b_fc[...].reshape(1, D)
    greet(
        [at.core, at.near, at.near_core, at.far, at.opposite]
        + [at.along_z(k) for k in (1, 2, 3)]
        + [at.along_x(k) for k in (1, 2, 3)]
        + [device for device in at.dp_peers[4:]]
    )

    def spread(source, slots):
        return [
            links.send(source.at[:, rows_of(sub_block(h, peer) * ROWS)], slots.at[block_of(w)], device)
            for device, peer in at.width_peers
        ]

    arrive = spread(tok, r["xa"])
    arrive += [links.send(vl, r["vg"].at[w], device) for device, _ in at.width_peers]
    r["vg"][w] = vl[...]

    class Weight:
        def __init__(self, full, device):
            own_block, next_block = full.at[block_of(w)], full.at[block_of(at.wy)]
            self.over = links.send(own_block, own_block, device)
            self.core = links.send(own_block, own_block, at.core)
            self.other = links.plan(next_block, next_block, at.core)

        def forward(self):
            self.over.wait_recv()
            self.other.start()

        def ready(self):
            self.core.wait_recv()
            self.other.wait_recv()

    loads[0].wait()
    r["wkv"][block_of(w), :] = interleave(r["wa_raw"][1], r["wa_raw"][2])
    weight_kv = Weight(r["wkv"], at.far)
    r["wq"][block_of(w), :] = r["wa_raw"][0]
    weight_q = Weight(r["wq"], at.far)
    loads[1].wait()
    r["wpt"][block_of(w), :] = r["wp_raw"][...].T
    loads[4].wait()
    for copy in arrive:
        copy.wait_recv()

    arrive_d = spread(dout, r["da"])
    vec[...] = jnp.concatenate([r["vg"][i] for i in range(4)], axis=1)
    r["x"][...] = r["xa"][...].T
    unit, _ = norm_stats(r["x"][...].astype(F32))
    x1, kv, q = r["x1"], r["kv"], r["q"]
    x1[0:ROWS, :] = (unit * vec[0:1, :] + vec[2:3, :]).astype(BF16)
    gather = GatherZ(links, at, x1)
    value_bias = interleave(jnp.zeros((1, PART), F32), bqv[1:2, :])
    weight_kv.forward()
    weight_kv.ready()
    weight_p = Weight(r["wpt"], at.far)
    loads[2].wait()
    weight_t = Weight(wt, at.far)
    quarter = [at.chunk(k) for k in (0, 1, 3, 2)]
    shares, passed = [], []

    def key_rows(first, count):
        rows = (nn(x1[first * ROWS : (first + count) * ROWS, :], r["wkv"][...]) + value_bias).astype(BF16)
        for i in range(count):
            block = kv.at[quarter[first + i], w]
            block[...] = rows[i * ROWS : (i + 1) * ROWS, :]
            shares.append(links.send(block, block, at.near))
            shares.append(links.send(block, block, at.core))

    for i in range(4):
        block = kv.at[quarter[i], at.wy]
        passed.append(links.plan(block, block, at.core))

    def pass_on(i):
        shares[2 * i].wait_recv()
        passed[i].start()

    key_rows(0, 1)
    gather.neighbours()
    key_rows(1, 2)
    weight_q.forward()
    pass_on(0)
    gather.rest()
    d_all = r["d_all"]
    loads[5].wait()
    for copy in arrive_d:
        copy.wait_recv()
    d_all[0:ROWS, :] = r["da"][...].T
    gather_d = GatherZ(links, at, d_all)
    key_rows(3, 1)
    weight_q.ready()
    queries = (nn(x1[...], r["wq"][...]) + bqv[0:1, :]).astype(BF16).astype(F32) * HS**-0.5
    q[...] = interleave(queries.astype(BF16), jnp.zeros((QUARTER, PART), BF16))
    weight_p.forward()
    for i in range(4):
        shares[2 * i + 1].wait_recv()

    kvt, att, att_t, lse, delta = r["kvt"], r["att"], r["att_t"], r["lse"], r["delta"]
    here = w - lax.rem(w, 2)
    there = 2 - here

    def half_keys(j, lanes, start):
        return kv[j, pl.ds(start, 2), :, lanes].reshape(2 * ROWS, lanes.stop - lanes.start)

    def half_columns(j, start):
        return pl.ds(pl.multiple_of(j * QUARTER + start * ROWS, 2 * ROWS), 2 * ROWS)

    def transpose_keys(start):
        for j in range(4):
            for head in range(HEADS):
                tile = slice(head * 128, (head + 1) * 128)
                kvt[tile, half_columns(j, start)] = half_keys(j, tile, start).T

    def attend_chunk(j, slot, start, merge):
        shift = sub_block(j, w) * ROWS
        apart = jnp.zeros((ROWS, 128), BF16)
        for first, count in ((0, 2), (2, 2), (4, 1)):
            lanes = slice(first * 128, (first + count) * 128)
            query = q[rows_of(slot * ROWS), lanes]
            if count == 2:
                top = jnp.concatenate([query[:, :128], apart], axis=1)
                query = jnp.concatenate([top, jnp.concatenate([apart, query[:, 128:]], axis=1)], axis=0)
            scores = [nt(half_keys(b, lanes, start), query) for b in range(j + 1)]
            scores[j] = mask_last(scores[j], j, shift, start)
            peak = functools.reduce(jnp.maximum, [jnp.max(s, axis=0, keepdims=True) for s in scores])
            total, result = 0.0, 0.0
            if merge:
                rows = [pl.ds(slot * 8 + first + i, 1) for i in range(count)]
                before = jnp.concatenate([lse[row, :] for row in rows], axis=1)
                peak = jnp.maximum(peak, before)
                scale = jnp.exp(before - peak)
                total = jnp.concatenate([delta[row, :] for row in rows], axis=1) * scale
            for b in range(j + 1):
                weights = jnp.exp(scores[b] - peak)
                total = total + column_sum(weights)
                result = result + nn(kvt[lanes, half_columns(b, start)], weights.astype(BF16))
            for i in range(count):
                head, part = first + i, slice(i * 128, (i + 1) * 128)
                place, row = slice(head * HS, (head + 1) * HS), pl.ds(slot * 8 + head, 1)
                values = result[i * 128 + HS : (i + 1) * 128, part]
                if merge:
                    values = (values + att_t[slot, place, :] * scale[:, part]) * (1.0 / total[:, part])
                    lse[row, :] = peak[:, part] + jnp.log(total[:, part])
                else:
                    lse[row, :] = peak[:, part]
                    delta[row, :] = total[:, part]
                att_t[slot, place, :] = values

    transpose_keys(here)

    @pl.loop(0, 4)
    def _(slot):
        pl.when(slot == 1)(functools.partial(pass_on, 1))
        pl.when(slot == 3)(functools.partial(pass_on, 2))
        j = at.chunk(jnp.where(slot == 3, 2, jnp.where(slot == 2, 3, slot)))
        for case in range(4):
            pl.when(j == case)(functools.partial(attend_chunk, case, slot, here, False))

    pass_on(3)
    loads[3].wait()
    weight_f = Weight(wf, at.near)
    for i in range(4):
        passed[i].wait_recv()

    transpose_keys(there)
    stage = r["stage"]
    sum_p = SumZ(links, at, stage, r["parts"], r["over"])

    gather_d.neighbours()
    weight_p.ready()

    @pl.loop(0, 4)
    def _(i):
        slot = jnp.where(i == 0, 3, jnp.where(i == 3, 0, i))
        j = at.chunk(jnp.where(slot == 3, 2, jnp.where(slot == 2, 3, slot)))
        for case in range(4):
            pl.when(j == case)(functools.partial(attend_chunk, case, slot, there, True))
        attended = att_t[slot].T.astype(BF16)
        att[rows_of(slot * ROWS), :] = attended
        stage[slot] = nt(attended, r["wpt"][...]).astype(BF16)
        pl.when(i == 0)(sum_p.send_across)
        pl.when(i == 1)(sum_p.right_bottom.start)
        pl.when(i == 1)(weight_t.forward)
        pl.when(i == 2)(sum_p.left_top.start)
        pl.when(i == 2)(sum_p.join_ahead)
        pl.when(i == 2)(sum_p.join_behind)

    gather_d.rest()
    weight_t.ready()
    weight_f.forward()
    middle = r["x"][...].astype(F32) + vec[4:5, :] + sum_p.result()
    r["middle"][...] = middle
    unit, _ = norm_stats(middle)
    x2, hid, gp = r["x2"], r["hid"], r["gp"]
    x2[0:ROWS, :] = (unit * vec[1:2, :] + vec[3:4, :]).astype(BF16)

    gather = GatherZ(links, at, x2)
    hidden_grad = r["hidden_grad"]
    for t in range(TILES):
        tile = slice(t * 256, (t + 1) * 256)
        hidden_grad[:, tile] = nn(d_all[...], wt[:, tile])
    weight_f.ready()
    stage_g, parts_g = r["stage_g"], r["parts_g"]
    moves = []

    def feed(first, count):
        rows = slice(first * ROWS, (first + count) * ROWS)

        for t in range(TILES):
            tile = slice(t * 256, (t + 1) * 256)
            u = nn(x2[rows, :], wf[:, tile]) + r["bf"][0:1, tile]
            square = u * u
            th = jnp.tanh(GELU_COEF * (u + 0.044715 * square * u))
            hid[rows, tile] = (0.5 * u * (1.0 + th)).astype(BF16)
            slope = 0.5 * (1.0 + th) + 0.5 * u * (1.0 - th * th) * (GELU_COEF * (1.0 + 0.134145 * square))
            gp[rows, tile] = (hidden_grad[rows, tile] * slope).astype(BF16)
        for t in range(TILES):
            tile = slice(t * 256, (t + 1) * 256)
            product = nt(gp[rows, :], wf[tile, :]).astype(BF16)
            for i in range(count):
                stage_g[first + i, :, tile] = product[i * ROWS : (i + 1) * ROWS]
        for i in range(first, first + count):
            if i:
                moves.append(links.send(stage_g.at[i], parts_g.at[i - 1], at.along_z((0, 1, 3, 2)[i])))

    feed(0, 1)
    gather.neighbours()
    feed(1, 2)
    gather.rest()
    feed(3, 1)
    grad_f, grad_t = r["grad_f"], r["grad_t"]

    def gradient_sum(tag, grad, columns, final):
        return GradientSum(
            links, at, grad, columns, r["pair_" + tag], r["strips_" + tag], r["cross_" + tag], final
        )

    for t in range(TILES):
        grad_t[tile_of(t, 256), :] = tn(d_all[:, tile_of(t, 256)], hid[...]).astype(BF16)

    whole = slice(0, D)
    sum_t = gradient_sum("t", grad_t, whole, fin_t)
    sum_t.send_core()

    for t in range(TILES):
        grad_f[tile_of(t, 256), :] = tn(x2[:, tile_of(t, 256)], gp[...]).astype(BF16)

    sum_f = GradientSumY(links, at, grad_f, r["pair_f"], r["cross_f"], r["strips_f"], r["half_f"], fin_f)
    sum_f.send_core()
    sum_t.send_x_by_neighbours()
    unit, scale = norm_stats(r["middle"][...])
    grad = d_all[0:ROWS, :].astype(F32)
    grad_normed = stage_g[0].astype(F32)
    for i in range(3):
        moves[i].wait_recv()
        grad_normed = grad_normed + parts_g[i].astype(F32)
    grad_middle = grad + norm_gradient(grad_normed, unit, scale, vec[1:2, :])
    r["gm"][...] = grad_middle
    branch = grad_middle.astype(BF16)
    g_all = r["g_all"]
    g_all[0:ROWS, :] = branch
    gather = GatherZ(links, at, g_all)
    sums = r["sums"]
    sums[1:2, :] = column_sum(grad_normed * unit)
    sums[3:4, :] = column_sum(grad_normed)
    sums[4:5, :] = column_sum(grad)
    sums[5:6, :] = column_sum(branch.astype(F32))
    sums[8:9, :] = column_sum(gp[...].astype(F32))
    sum_f.send_y()
    sum_p.sent()
    sum_b = SumZ(links, at, stage, r["parts_b"], r["over_b"])

    for t in range(TILES):
        product = nt(hid[...], wt[tile_of(t, 256), :]).astype(BF16)
        for i in range(4):
            stage[i, :, tile_of(t, 256)] = product[i * ROWS : (i + 1) * ROWS]


    dkv, go, dq, dq_t = r["dkv"], r["go"], r["dq"], att_t
    take, take_y, gkv = r["take"], r["take_y"], r["gkv"]
    dkv[...] = jnp.zeros(dkv.shape, BF16)

    def rows_back(first, count):
        rows = slice(first * ROWS, (first + count) * ROWS)
        grad = nn(g_all[rows, :], r["wpt"][...]).astype(BF16)
        go[rows, :] = interleave(jnp.zeros((count * ROWS, PART), BF16), grad)
        for i in range(count):
            slot = first + i
            both = grad[i * ROWS : (i + 1) * ROWS, :].astype(F32).T * att_t[slot]
            delta[slot * 8 : slot * 8 + HEADS, :] = jnp.sum(both.reshape(HEADS, HS, ROWS), axis=1)

    shared = links.reserve(3 * HEADS)

    def head_move(kind, head):
        source = dkv.at[head, :, (at.wyc, at.wc, at.wy)[kind]]
        target = take_y.at[head] if kind == 2 else take.at[1 - kind, head]
        return links.make(shared + kind * HEADS + head, source, target, at.near if kind == 2 else at.core)

    def cross_head(head):
        head_move(0, head).wait_recv()
        for j in range(4):
            both = dkv[head, j, at.wy].astype(F32) + take[1, head, j].astype(F32)
            dkv[head, j, at.wy] = both.astype(BF16)
        head_move(2, head).start()

    def back_chunk(j, slot):
        rows = rows_of(slot * ROWS)

        @pl.loop(0, HEADS)
        def _(head):
            tile = tile_of(head, 128)
            side = jnp.concatenate([q[rows, tile], go[rows, tile]], axis=0)
            log_total = lse[pl.ds(slot * 8 + head, 1), :]
            inner = delta[pl.ds(slot * 8 + head, 1), :]
            grads = []
            for b in range(j + 1):
                products = nt(kv[b, :, :, tile].reshape(QUARTER, 128), side)
                scores = products[:, :128]
                if b == j:
                    scores = mask_last(scores, j, sub_block(j, w) * ROWS)
                probs = jnp.exp(scores - log_total)
                grads.append((probs * (products[:, 128:] - inner)).astype(BF16))
                both = nn(jnp.concatenate([grads[b], probs.astype(BF16)], axis=1), side)
                both = dkv[head, b].reshape(QUARTER, 128).astype(F32) + both
                dkv[head, b] = both.astype(BF16).reshape(4, ROWS, 128)
            result = nn(kvt[tile, 0 : (j + 1) * QUARTER], jnp.concatenate(grads, axis=0))
            dq_t[slot, tile_of(head, HS), :] = result[:HS, :] * HS**-0.5
            pl.when(slot == 3)(lambda: head_move(0, head).start())

    def near_back():
        gather.neighbours()
        rows_back(1, 2)

    for copy in moves:
        copy.wait_send()
    rows_back(0, 1)

    sum_t.relay_x()

    def far_back():
        gather.rest()
        rows_back(3, 1)
        sum_b.send_across()
        sum_b.send_near()

    @pl.loop(0, 4)
    def _(slot):
        pl.when(slot == 1)(near_back)
        pl.when(slot == 3)(far_back)
        j = at.chunk(jnp.where(slot == 2, 3, jnp.where(slot == 3, 2, slot)))
        for case in range(4):
            pl.when(j == case)(functools.partial(back_chunk, case, slot))

    for slot in range(4):
        dq[slot * ROWS : (slot + 1) * ROWS, :] = dq_t[slot].T.astype(BF16)
    for head in range(HEADS):
        cross_head(head)
    for head in range(HEADS):
        head_move(1, head).start()
    sum_f.send_x()
    slots = []
    for j in range(4):
        k = lax.rem(j + 4 - h, 4)
        slots.append(jnp.where(k == 2, 3, jnp.where(k == 3, 2, k)))
    keep = []

    def send_back(total, passing=False):
        strip = total.send_back(passing)
        copy = pltpu.make_async_copy(total.total[0], strip, local.at[7 + len(keep)])
        copy.start()
        keep.append(copy)

    def send_rows(back, target):
        place = target.at[:, rows_of(mine * ROWS)]
        keep = pltpu.make_async_copy(back.at[block_of(w)], place, local.at[6])
        keep.start()
        copies = [links.send(back.at[block_of(peer)], place, device) for device, peer in at.width_peers]
        keep.wait()
        return copies

    sum_t.sent_core()

    for t in range(TILES):
        tile = tile_of(t, 256)
        pieces = [tn(x1[:, tile], dq[...]).astype(BF16), tn(g_all[:, tile], att[...]).astype(BF16)]
        grad_t[tile, PAIR:] = jnp.concatenate(pieces, axis=1)

    sum_q = gradient_sum("q", grad_t, slice(PAIR, D), fin_q)
    sum_q.send_core()
    sum_t.send_far()
    sums[9:10, 0:PART] = column_sum(dq[...].astype(F32))
    sum_b.join_ahead()
    sum_b.join_behind()
    sum_q.send_x()
    sum_f.send_back()
    result = r["middle"][...] + vec[5:6, :] + sum_b.result()
    r["xa"][...] = result.astype(BF16).T
    returns = send_rows(r["xa"], bo)

    for head in range(HEADS):
        tile = slice(head * 128, (head + 1) * 128)
        head_move(1, head).wait_recv()
        head_move(2, head).wait_recv()
        for j in range(4):
            total = dkv[head, j, w].astype(F32) + take[0, head, j].astype(F32) + take_y[head, j].astype(F32)
            gkv[rows_of(slots[j] * ROWS), tile] = total.astype(BF16)


    for t in range(TILES):
        tile = tile_of(t, 256)
        grad_t[tile, 0:PAIR] = tn(x1[:, tile], gkv[...]).astype(BF16)

    sum_k = gradient_sum("k", grad_t, slice(0, PAIR), fin_k)
    sum_k.send_core()
    sum_t.send_opposite()
    sum_b.sent()
    sum_l = SumZ(links, at, stage, r["parts"], r["over"])

    def first_partial(first, count):
        rows = slice(first * ROWS, (first + count) * ROWS)
        product = (nt(dq[rows, :], r["wq"][...]) + nt(gkv[rows, :], r["wkv"][...])).astype(BF16)
        for i in range(count):
            stage[first + i] = product[i * ROWS : (i + 1) * ROWS]

    first_partial(3, 1)
    sum_l.send_across()
    first_partial(1, 2)
    sum_l.send_near()
    grad_values = column_sum(gkv[...].astype(F32))
    for head in range(HEADS):
        sums[9:10, PART + head * HS : PART + (head + 1) * HS] = grad_values[:, head * 128 + HS : (head + 1) * 128]
    sums[9:10, PAIR:] = jnp.zeros((1, PAIR), F32)
    sums[10:16, :] = jnp.zeros((6, D), F32)
    sums[6:8, :] = jnp.zeros((2, D), F32)
    over_v = [links.send(sums.at[8:16], r["take_v"].at[i], at.width_peers[i][0]) for i in range(3)]
    sum_k.send_x()
    keep.append(sum_f.send_opposite(local.at[7 + len(keep)]))
    sum_l.join_ahead()
    sum_l.join_behind()
    first_partial(0, 1)
    sum_q.send_y()
    send_back(sum_t, True)
    grad_normed = sum_l.result()
    unit, scale = norm_stats(r["x"][...].astype(F32))
    sums[0:1, :] = column_sum(grad_normed * unit)
    sums[2:3, :] = column_sum(grad_normed)
    for part in range(4):
        r["sums_w"][part] = sums[0:8, part * PART : (part + 1) * PART]
    over_w = [
        links.send(r["sums_w"].at[peer], r["take_w"].at[i], device)
        for i, (device, peer) in enumerate(at.width_peers)
    ]
    result = r["gm"][...] + norm_gradient(grad_normed, unit, scale, vec[0:1, :])
    r["da"][...] = result.astype(BF16).T
    returns += send_rows(r["da"], dt)
    sum_t.pass_back()
    send_back(sum_q)

    for copy in over_w + over_v:
        copy.wait_recv()
    sums_d = r["sums_d"]
    normed = r["sums_w"][w] + r["take_w"][0] + r["take_w"][1] + r["take_w"][2]
    biases = sums[8:10, :] + r["take_v"][0, 0:2] + r["take_v"][1, 0:2] + r["take_v"][2, 0:2]
    r["sums_n"][...] = normed
    over_z = [links.send(r["sums_n"], r["sums_z"].at[k - 1], at.along_z(k)) for k in (1, 2, 3)]
    sum_k.send_y()
    for copy in over_z:
        copy.wait_recv()
    normed = r["sums_n"][...] + r["sums_z"][0] + r["sums_z"][1] + r["sums_z"][2]
    sums_d[...] = jnp.zeros((8, D), F32)
    for i in range(6):
        sums_d[i // 3 : i // 3 + 1, (i % 3) * 384 : (i % 3) * 384 + PART] = normed[i : i + 1, :]
    sums_d[2:4, :] = biases
    over_x = [links.send(sums_d, r["sums_x"].at[i], device) for i, device in enumerate(at.dp_peers)]
    send_back(sum_k)
    total = sums_d[...]
    for i, copy in enumerate(over_x):
        copy.wait_recv()
        total = total + r["sums_x"][i]
    fin_v[...] = total
    for copy in keep:
        copy.wait()
    for total in (sum_t, sum_f, sum_q, sum_k):
        total.finish()
    for copy in returns:
        copy.wait()
    for kind in range(3):
        for head in range(HEADS):
            head_move(kind, head).wait_send()
    for copy in links.copies:
        copy.wait_send()


def block(*inputs):
    return pl.pallas_call(
        block_kernel,
        name="block",
        out_shape=(
            jax.ShapeDtypeStruct((PART, QUARTER), BF16),
            jax.ShapeDtypeStruct((PART, QUARTER), BF16),
            jax.ShapeDtypeStruct((PART, D), BF16),
            jax.ShapeDtypeStruct((PART, D), BF16),
            jax.ShapeDtypeStruct((PART, PAIR), BF16),
            jax.ShapeDtypeStruct((PART, PAIR), BF16),
            jax.ShapeDtypeStruct((8, D), F32),
        ),
        in_specs=[ANY, ANY, VMEM, VMEM, VMEM, VMEM, ANY, VMEM, ANY, ANY, VMEM, ANY],
        out_specs=(ANY, ANY, ANY, ANY, ANY, ANY, VMEM),
        scratch_shapes=[pltpu.VMEM(shape, kind) for shape, kind in SCRATCH.values()]
        + [pltpu.SemaphoreType.DMA((COPIES,)), pltpu.SemaphoreType.DMA((COPIES,)), pltpu.SemaphoreType.DMA((12,))],
        compiler_params=pltpu.CompilerParams(collective_id=1, has_side_effects=True, vmem_limit_bytes=64 * 2**20),
    )(*inputs)


def finish_kernel(*refs):
    inputs, outputs, (f, t, qp, kv, d_wa, d_wp, d_wf, d_wo, rows_b, rows_d, sems) = refs[:7], refs[7:19], refs[19:]
    bo, dt, f_in, t_in, qp_in, kv_in, v = inputs
    out, d_tok, gain, shift, wa_out, d_bqv, wp_out, d_bp, wf_out, d_bf, wo_out, d_bo = outputs
    loads = [
        pltpu.make_async_copy(source, target, sems.at[i])
        for i, (source, target) in enumerate(((t_in, t), (f_in, f), (qp_in, qp), (kv_in, kv), (bo, rows_b), (dt, rows_d)))
    ]
    stores = [
        pltpu.make_async_copy(source, target, sems.at[6 + i])
        for i, (source, target) in enumerate(
            ((rows_b, out), (rows_d, d_tok), (d_wo, wo_out), (d_wf, wf_out), (d_wa, wa_out), (d_wp, wp_out))
        )
    ]
    for copy in loads:
        copy.start()
    loads[0].wait()
    d_wo[...] = t[...].astype(F32)
    stores[2].start()
    loads[1].wait()
    d_wf[...] = f[...].astype(F32)
    stores[3].start()
    loads[2].wait()
    d_wa[0] = qp[:, :PART].astype(F32)
    d_wp[...] = qp[:, PART:].astype(F32).T
    stores[5].start()
    loads[3].wait()
    both = kv[...].astype(F32)
    d_wa[1] = jnp.concatenate([both[:, head * 128 : head * 128 + HS] for head in range(HEADS)], axis=1)
    d_wa[2] = jnp.concatenate([both[:, head * 128 + HS : (head + 1) * 128] for head in range(HEADS)], axis=1)
    stores[4].start()
    for i in range(2):
        loads[4 + i].wait()
        stores[i].start()
    rows = [v[i // 3 : i // 3 + 1, (i % 3) * 384 : (i % 3) * 384 + PART] for i in range(6)]
    gain[0:1, :] = rows[0]
    gain[1:2, :] = rows[1]
    shift[0:1, :] = rows[2]
    shift[1:2, :] = rows[3]
    d_bo[...] = rows[4].reshape(PART)
    d_bp[...] = rows[5].reshape(PART)
    d_bf[...] = v[2:3, :].reshape(D)
    d_bqv[0:1, :] = v[3:4, 0:PART]
    d_bqv[1:2, :] = v[3:4, PART:PAIR]
    for copy in stores:
        copy.wait()


def finish(*inputs):
    shapes = [
        ((PART, QUARTER), BF16),
        ((PART, QUARTER), BF16),
        ((2, PART), F32),
        ((2, PART), F32),
        ((3, PART, PART), F32),
        ((2, PART), F32),
        ((PART, PART), F32),
        ((PART,), F32),
        ((PART, D), F32),
        ((D,), F32),
        ((PART, D), F32),
        ((PART,), F32),
    ]
    return pl.pallas_call(
        finish_kernel,
        name="finish",
        out_shape=[jax.ShapeDtypeStruct(shape, kind) for shape, kind in shapes],
        in_specs=[ANY] * 6 + [VMEM],
        out_specs=[ANY, ANY, VMEM, VMEM, ANY, VMEM, ANY, VMEM, ANY, VMEM, ANY, VMEM],
        scratch_shapes=[
            pltpu.VMEM((PART, D), BF16),
            pltpu.VMEM((PART, D), BF16),
            pltpu.VMEM((PART, PAIR), BF16),
            pltpu.VMEM((PART, PAIR), BF16),
            pltpu.VMEM((3, PART, PART), F32),
            pltpu.VMEM((PART, PART), F32),
            pltpu.VMEM((PART, D), F32),
            pltpu.VMEM((PART, D), F32),
            pltpu.VMEM((PART, QUARTER), BF16),
            pltpu.VMEM((PART, QUARTER), BF16),
            pltpu.SemaphoreType.DMA((12,)),
        ],
        compiler_params=pltpu.CompilerParams(vmem_limit_bytes=63 * 2**20),
    )(*inputs)


def shards(tokens, ln_gain, ln_bias, w_attn, b_qv, w_proj, b_proj, w_fc, b_fc, w_out, b_out, d_out):
    parts = block(tokens.T, d_out.T, ln_gain, ln_bias, b_proj, b_out, w_attn, b_qv, w_proj, w_fc, b_fc, w_out.T)
    results = list(finish(*parts))
    for i in (0, 1, 10):
        results[i] = results[i].T
    return tuple(results)


def solution(mesh):
    in_specs = (
        P(("dp", "heads"), "width"),
        P(None, "width"),
        P(None, "width"),
        P(None, "width", "heads"),
        P(None, "heads"),
        P("heads", "width"),
        P("width"),
        P("width", "heads"),
        P("heads"),
        P("heads", "width"),
        P("width"),
        P(("dp", "heads"), "width"),
    )
    out_specs = (
        P(("dp", "heads"), "width"),
        P(("dp", "heads"), "width"),
        P(None, "width"),
        P(None, "width"),
        P(None, "width", "heads"),
        P(None, "heads"),
        P("heads", "width"),
        P("width"),
        P("width", "heads"),
        P("heads"),
        P("heads", "width"),
        P("width"),
    )
    return jax.shard_map(shards, mesh=mesh, in_specs=in_specs, out_specs=out_specs, check_vma=False)
```
